128 devices in a mesh: grid: 2 (over z_hi), gx: 8 (over z_lo, x), gy: 8 (over y, core).
Axes of the slice: x: 4, y: 4, z: 4 (z_hi: 2, z_lo: 2; z = z_hi * 2 + z_lo), core: 2. Of those that a mesh axis runs over, the one named last changes fastest.
Arguments:
- fields: float32 [2, 9, 48, 192, 384], P('grid', None, 'gx', 'gy'), may hold values from -6 to 6
- material: int32 [2, 48, 192, 384], P('grid', 'gx', 'gy'), may hold values from 0 to 7
- permittivity: float32 [8], replicated, may hold values from 4 to 81
- conductivity: float32 [8], replicated, may hold values from 0.02 to 0.6
- relax_rate: float32 [8], replicated, may hold values from 0.05 to 0.8
- debye_strength: float32 [8], replicated, may hold values from 0.5 to 4
- subgrids: int32 [8, 8, 6], P('gx', 'gy'), may hold values from 0 to 256, as said below
Outputs:
- fields_out: float32 [2, 9, 48, 192, 384], P('grid', None, 'gx', 'gy')
The draws below stay inside these ranges and needn't reach their ends.
Inputs may be any that keep to these rules, and one draw needn't show every extreme that they name: subgrids[a, b] = (x0, y0, z0, lx, ly, lz): x0 <= 4, y0 <= 16, z0 <= 256; lx is at least 1 and at most 2, ly at least 4 and at most 8, lz at least 64 and at most 128; some block reaches every upper bound.
All inputs are finite; a program needn't handle non-finite values.
Results may differ from the reference program's by a relative error of at most 0.0003.
Values sent between devices are 32-bit elements; how exact they have to be, the bound alone decides.
A program may use at most 128 MiB of HBM per device.

```python
import math
import jax
import jax.numpy as jnp
from jax import lax

CX = 6
CY = 24
CZ = 384
NMAT = 8
COARSE_STEPS = 3
NX = 48
NY = 192
N_GX = 8
N_GY = 8


def draw_subgrids(key, part):
    key = jax.random.fold_in(key, 7)
    keys = jax.random.split(key, 6)
    grid_shape = (N_GX, N_GY)
    widest_x = CX // 3
    widest_y = CY // 3
    widest_z = CZ // 3
    length_x = jax.random.randint(keys[0], grid_shape, max(CX // 6, 1), widest_x + 1)
    length_y = jax.random.randint(keys[1], grid_shape, max(CY // 6, 1), widest_y + 1)
    length_z = jax.random.randint(keys[2], grid_shape, max(CZ // 6, 1), widest_z + 1)
    corner_x = jax.random.randint(keys[3], grid_shape, 0, CX - widest_x + 1)
    corner_y = jax.random.randint(keys[4], grid_shape, 0, CY - widest_y + 1)
    corner_z = jax.random.randint(keys[5], grid_shape, 0, CZ - widest_z + 1)
    leading = (lax.broadcasted_iota(jnp.int32, grid_shape, 0) == 0) & (lax.broadcasted_iota(jnp.int32, grid_shape, 1) == 0)
    length_x = jnp.where(leading, widest_x, length_x)
    length_y = jnp.where(leading, widest_y, length_y)
    length_z = jnp.where(leading, widest_z, length_z)
    corner_x = jnp.where(leading, CX - widest_x, corner_x)
    corner_y = jnp.where(leading, CY - widest_y, corner_y)
    corner_z = jnp.where(leading, CZ - widest_z, corner_z)
    return jnp.stack([corner_x, corner_y, corner_z, length_x, length_y, length_z], axis=-1).astype(jnp.int32)


def plant(drawn, stream_key, smallest, largest):
    shape = drawn.shape
    place = [jax.random.randint(jax.random.fold_in(stream_key, axis), (), 0, shape[axis]) for axis in range(len(shape))]
    drawn = drawn.at[tuple(place)].set(smallest)
    longest = shape.index(max(shape))
    place[longest] = (place[longest] + 1) % shape[longest]
    return drawn.at[tuple(place)].set(largest)


def levels(rng, shape, cuts, low, high):
    def one(position, shards_of):
        draws = jax.random.uniform(jax.random.fold_in(jax.random.fold_in(rng, 6), position), (shards_of,), jnp.float32, low / len(cuts), high / len(cuts))
        return jnp.repeat(jnp.exp(draws), shape[position] // shards_of).reshape((-1,) + (1,) * (len(shape) - position - 1))

    level = one(*cuts[0])
    for cut in cuts[1:]:
        level = level * one(*cut)
    return level


def gaussian(rng, dims, scale, bound, pieces=(), kind=jnp.bfloat16):
    level = levels(rng, dims, pieces, -0.22, 0.18) if pieces else 1.0
    values = jax.random.normal(rng, dims, jnp.float32) * scale * level
    return jnp.minimum(jnp.maximum(values, -bound), bound).astype(kind)


def setup_inputs(seed: int = 0) -> dict:
    streams_of = jax.random.split(jax.random.key(seed), 8)
    fields = gaussian(streams_of[0], (2, 9, NX, NY, CZ), 1.0, 6.0, ((0, 2), (2, 8), (3, 8)), jnp.float32)
    material = plant(jax.random.randint(streams_of[1], (2, NX, NY, CZ), 0, NMAT), jax.random.fold_in(streams_of[1], 1), 0, NMAT - 1).astype(jnp.int32)
    permittivity = jnp.clip(jnp.exp(jax.random.uniform(streams_of[2], (NMAT,), jnp.float32, math.log(4.0), math.log(81.0))), 4.0, 81.0)
    conductivity = jnp.clip(jnp.exp(jax.random.uniform(streams_of[3], (NMAT,), jnp.float32, math.log(0.02), math.log(0.6))), 0.02, 0.6)
    relax_rate = jnp.clip(jnp.exp(jax.random.uniform(streams_of[4], (NMAT,), jnp.float32, math.log(0.05), math.log(0.8))), 0.05, 0.8)
    debye_strength = jnp.clip(jax.random.uniform(streams_of[5], (NMAT,), jnp.float32, 0.5, 4.0), 0.5, 4.0)
    subgrids = draw_subgrids(jax.random.fold_in(streams_of[7], 71), 0)
    return dict(fields=fields, material=material, permittivity=permittivity, conductivity=conductivity, relax_rate=relax_rate, debye_strength=debye_strength, subgrids=subgrids)


courant = 0.5
one_third = 1.0 / 3.0


def lookup(material, entries):
    picked = jnp.zeros(material.shape, entries.dtype)
    for candidate in range(entries.shape[0]):
        picked = jnp.where(material == candidate, entries[candidate], picked)
    return picked


def material_factors(material, permittivity, conductivity, relax_rate, debye_strength, factor):
    permit = lookup(material, permittivity)
    damping = lookup(material, conductivity) * factor / (2.0 * permit)
    relaxing = lookup(material, relax_rate) * factor
    return jnp.stack([(1.0 - damping) / (1.0 + damping), 1.0 / (permit * (1.0 + damping)), relaxing, jnp.exp(-relaxing), lookup(material, debye_strength)])


def diff_ahead(values, direction):
    base_cut = [slice(0, -1)] * 3
    moved_cut = [slice(0, -1)] * 3
    moved_cut[direction] = slice(1, None)
    return values[tuple(moved_cut)] - values[tuple(base_cut)]


def diff_behind(values, direction):
    base_cut = [slice(1, None)] * 3
    moved_cut = [slice(1, None)] * 3
    moved_cut[direction] = slice(0, -1)
    return values[tuple(base_cut)] - values[tuple(moved_cut)]


def curl_ahead(padded):
    return jnp.stack([diff_ahead(padded[2], 1) - diff_ahead(padded[1], 2), diff_ahead(padded[0], 2) - diff_ahead(padded[2], 0), diff_ahead(padded[1], 0) - diff_ahead(padded[0], 1)])


def curl_behind(padded):
    return jnp.stack([diff_behind(padded[2], 1) - diff_behind(padded[1], 2), diff_behind(padded[0], 2) - diff_behind(padded[2], 0), diff_behind(padded[1], 0) - diff_behind(padded[0], 1)])


def electric(efield, polarization, rotation, factors):
    return factors[0] * efield + factors[1] * (courant * rotation - factors[2] * (factors[4] * efield - polarization))


def relaxation(polarization, efield, factors):
    return factors[3] * polarization + (1.0 - factors[3]) * factors[4] * efield


def coarse_update(fields, factors):
    efield, hfield, polarization = fields[0:3], fields[3:6], fields[6:9]
    hfield = hfield - courant * curl_ahead(jnp.pad(efield, ((0, 0), (0, 1), (0, 1), (0, 1))))
    rotation = curl_behind(jnp.pad(hfield, ((0, 0), (1, 0), (1, 0), (1, 0))))
    efield = electric(efield, polarization, rotation, factors)
    polarization = relaxation(polarization, efield, factors)
    return jnp.concatenate([efield, hfield, polarization])


def fine_update(fields, factors, inside, border, driven):
    efield, hfield, polarization = fields[0:3], fields[3:6], fields[6:9]
    hfield = inside * (hfield - courant * curl_ahead(jnp.pad(efield, ((0, 0), (0, 1), (0, 1), (0, 1)))))
    rotation = curl_behind(jnp.pad(hfield, ((0, 0), (1, 0), (1, 0), (1, 0))))
    efield = jnp.where(border, driven, inside * electric(efield, polarization, rotation, factors))
    polarization = inside * relaxation(polarization, efield, factors)
    return jnp.concatenate([efield, hfield, polarization])


def subgrid_masks(extent, cell_shape):
    along_x = lax.broadcasted_iota(jnp.int32, cell_shape, 0)
    along_y = lax.broadcasted_iota(jnp.int32, cell_shape, 1)
    along_z = lax.broadcasted_iota(jnp.int32, cell_shape, 2)
    xlength = 3 * extent[3]
    ylength = 3 * extent[4]
    zlength = 3 * extent[5]
    covered = (along_x < xlength) & (along_y < ylength) & (along_z < zlength)
    xfaces = (along_x == 0) | (along_x == xlength - 1)
    yfaces = (along_y == 0) | (along_y == ylength - 1)
    zfaces = (along_z == 0) | (along_z == zlength - 1)
    border = jnp.stack([covered & (yfaces | zfaces), covered & (xfaces | zfaces), covered & (xfaces | yfaces)])
    return covered.astype(jnp.float32), border


def cut_region(efield, extent):
    region_shape = (3, efield.shape[1] // 3, efield.shape[2] // 3, efield.shape[3] // 3)
    return lax.dynamic_slice(efield, (jnp.int32(0), extent[0], extent[1], extent[2]), region_shape)


def upsample(region):
    sizes = region.shape
    spread = jnp.broadcast_to(region[:, :, None, :, None, :, None], (sizes[0], sizes[1], 3, sizes[2], 3, sizes[3], 3))
    return spread.reshape(sizes[0], 3 * sizes[1], 3 * sizes[2], 3 * sizes[3])


def restrict(efield):
    sizes = efield.shape
    grouped = efield.reshape(sizes[0], sizes[1] // 3, 3, sizes[2] // 3, 3, sizes[3] // 3, 3)
    return grouped.mean(axis=(2, 4, 6))


def overwrite(fields, restricted, extent):
    region = cut_region(fields[0:3], extent)
    along_x = lax.broadcasted_iota(jnp.int32, region.shape, 1)
    along_y = lax.broadcasted_iota(jnp.int32, region.shape, 2)
    along_z = lax.broadcasted_iota(jnp.int32, region.shape, 3)
    covered = (along_x < extent[3]) & (along_y < extent[4]) & (along_z < extent[5])
    updated = jnp.where(covered, restricted, region)
    return lax.dynamic_update_slice(fields, updated, (jnp.int32(0), extent[0], extent[1], extent[2]))


def to_blocks(values):
    components = values.shape[0]
    split = values.reshape(components, N_GX, CX, N_GY, CY, CZ)
    return split.transpose(1, 3, 0, 2, 4, 5).reshape(N_GX * N_GY, components, CX, CY, CZ)


def from_blocks(blocks):
    components = blocks.shape[1]
    split = blocks.reshape(N_GX, N_GY, components, CX, CY, CZ)
    return split.transpose(2, 0, 3, 1, 4, 5).reshape(components, N_GX * CX, N_GY * CY, CZ)


def reference(fields, material, permittivity, conductivity, relax_rate, debye_strength, subgrids):
    coarse_fields = fields[0]
    coarse_factors = material_factors(material[0], permittivity, conductivity, relax_rate, debye_strength, 1.0)
    fine_factors = to_blocks(material_factors(material[1], permittivity, conductivity, relax_rate, debye_strength, one_third))
    extents = subgrids.reshape(N_GX * N_GY, 6)
    inside, border = jax.vmap(lambda extent: subgrid_masks(extent, (CX, CY, CZ)))(extents)
    fine_fields = to_blocks(fields[1]) * inside[:, None]
    for number in range(COARSE_STEPS):
        earlier = jax.vmap(cut_region)(to_blocks(coarse_fields[0:3]), extents)
        coarse_fields = coarse_update(coarse_fields, coarse_factors)
        latest = jax.vmap(cut_region)(to_blocks(coarse_fields[0:3]), extents)
        for substep in range(1, 4):
            weight = substep / 3.0
            driven = earlier + weight * (latest - earlier)
            fine_fields = lax.map(lambda items: fine_update(items[0], items[1], items[2], items[3], upsample(items[4])), (fine_fields, fine_factors, inside, border, driven))
        restricted = jax.vmap(restrict)(fine_fields[:, 0:3])
        blocks = jax.vmap(overwrite)(to_blocks(coarse_fields), restricted, extents)
        coarse_fields = from_blocks(blocks)
    return jnp.stack([coarse_fields, from_blocks(fine_fields)])
```

```python
import functools

import jax
import jax.numpy as jnp
from jax import lax
from jax.experimental import pallas as pl
from jax.experimental.pallas import tpu as pltpu
from jax.sharding import PartitionSpec as P

MESH = pl.DeviceIdType.MESH
STEPS = 3
F32 = jnp.float32

TO_NEXT = ((-1, 0), (0, -1), (1, 0), (0, 1), (1, -1), (-1, 1))
XE, YE, XG, YG, C1, C2 = range(6)


def lane_iota():
    return lax.broadcasted_iota(jnp.int32, (8, 128), 1)


def row_iota():
    return lax.broadcasted_iota(jnp.int32, (8, 128), 0)


def pick(tile, index):
    return jnp.take_along_axis(tile, index, axis=1, mode="promise_in_bounds")


def zfwd(v):
    n = v.shape[-1]
    lanes = lax.broadcasted_iota(jnp.int32, v.shape, v.ndim - 1)
    return jnp.where(lanes == n - 1, 0.0, pltpu.roll(v, n - 1, v.ndim - 1))


def zbwd(v):
    lanes = lax.broadcasted_iota(jnp.int32, v.shape, v.ndim - 1)
    return jnp.where(lanes == 0, 0.0, pltpu.roll(v, 1, v.ndim - 1))


def yfwd(t):
    return jnp.where(row_iota() == 7, 0.0, pltpu.roll(t, 7, 0))


def ybwd(t):
    return jnp.where(row_iota() == 0, 0.0, pltpu.roll(t, 1, 0))


def tables(permit, conduct, relax, debye, factor, courant):
    lane = lane_iota()

    def spread(ref):
        out = jnp.ones((8, 128), F32)
        for m in range(8):
            out = jnp.where(lane == m, ref[m], out)
        return out

    eps = spread(permit)
    damping = spread(conduct) * factor / (2.0 * eps)
    f0 = (1.0 - damping) / (1.0 + damping)
    f1 = 1.0 / (eps * (1.0 + damping))
    f2 = spread(relax) * factor
    f3 = jnp.exp(-f2)
    f4 = spread(debye)
    return f0 - f1 * f2 * f4, courant * f1, f1 * f2, f3, (1.0 - f3) * f4


def kernel(
    nx, ny,
    fields, material, permit, conduct, relax, debye, subgrids, out,
    e, h, p, k, stage, mat, ff, fk, pk, pln, ear, drv,
    xe_s, ye_s, xg_s, yg_s, c1_s, c2_s,
    xe_r, ye_r, xg_r, yg_r, c1_r, c2_r,
    lat_s, lat_r, del_s, del_r,
    lsem, hs, hr, bs, br, ds, dr,
):
    grid = lax.axis_index("grid")
    ga = lax.axis_index("gx")
    gb = lax.axis_index("gy")
    coarse = grid == 0
    x0, y0, z0 = subgrids[0, 0, 0], subgrids[0, 0, 1], subgrids[0, 0, 2]
    lx, ly, lz = subgrids[0, 0, 3], subgrids[0, 0, 4], subgrids[0, 0, 5]
    sends = (xe_s, ye_s, xg_s, yg_s, c1_s, c2_s)
    recvs = (xe_r, ye_r, xg_r, yg_r, c1_r, c2_r)

    def exists(dx, dy):
        return (ga + dx >= 0) & (ga + dx < nx) & (gb + dy >= 0) & (gb + dy < ny)

    partner = (1 - grid, ga, gb)

    def local_copies():
        e_in = pltpu.make_async_copy(fields.at[0, 0:3], e.at[:, 0:6, 0:24, :], lsem.at[0])
        h_in = pltpu.make_async_copy(fields.at[0, 3:6], h.at[:, 1:7, 8:32, :], lsem.at[1])
        p_in = pltpu.make_async_copy(fields.at[0, 6:9], p, lsem.at[2])
        return e_in, h_in, p_in

    m_in = [pltpu.make_async_copy(material.at[0, :, :, pl.ds(128 * v, 128)], mat.at[v], lsem.at[3 + v]) for v in range(3)]
    for cp in m_in:
        cp.start()

    @pl.when(coarse)
    def _():
        for cp in local_copies():
            cp.start()
        for ref in (ye_s, yg_s, pk, pln) + recvs:
            ref[...] = jnp.zeros_like(ref)

    f_in = [pltpu.make_async_copy(fields.at[0, :, :, :, pl.ds(128 * v, 128)], stage.at[v], lsem.at[v]) for v in range(3)]

    @pl.when(jnp.logical_not(coarse))
    def _():
        for cp in f_in:
            cp.start()

    barrier = pltpu.get_barrier_semaphore()
    pl.semaphore_signal(barrier, inc=1, device_id=partner, device_id_type=MESH)
    count = jnp.int32(1)
    for dx, dy in TO_NEXT:
        there = exists(dx, dy) & coarse
        count = count + there.astype(jnp.int32)

        @pl.when(there)
        def _():
            pl.semaphore_signal(barrier, inc=1, device_id=(grid, ga + dx, gb + dy), device_id_type=MESH)

    pl.semaphore_wait(barrier, count)

    def halo_copy(m, n):
        dx, dy = TO_NEXT[m]
        return pltpu.make_async_remote_copy(
            src_ref=sends[m].at[n], dst_ref=recvs[m].at[n], send_sem=hs.at[m, n], recv_sem=hr.at[m, n],
            device_id=(grid, jnp.clip(ga + dx, 0, nx - 1), jnp.clip(gb + dy, 0, ny - 1)), device_id_type=MESH)

    def lat_copy(n):
        return pltpu.make_async_remote_copy(
            src_ref=lat_s.at[n], dst_ref=lat_r.at[n], send_sem=bs.at[n], recv_sem=br.at[n],
            device_id=partner, device_id_type=MESH)

    def del_copy(n):
        return pltpu.make_async_remote_copy(
            src_ref=del_s.at[n], dst_ref=del_r.at[n], send_sem=ds.at[n], recv_sem=dr.at[n],
            device_id=partner, device_id_type=MESH)

    rows, lanes = row_iota(), lane_iota()
    row_ok = [(rows + 8 * u >= y0) & (rows + 8 * u < y0 + 8) for u in range(3)]
    lane_ok = [(lanes + 128 * v >= z0) & (lanes + 128 * v < z0 + 128) for v in range(3)]

    @pl.when(coarse)
    def _():
        e_in, h_in, p_in = local_copies()
        flag_x = jnp.where(ga > 0, 1.0, 0.0).astype(F32)
        flag_y = jnp.where(gb > 0, 1.0, 0.0).astype(F32)

        def cut(n):
            for i in range(2):
                for c in range(3):
                    tile = jnp.zeros((8, 128), F32)
                    for u in range(3):
                        for v in range(3):
                            here = e[c, x0 + i, 8 * u:8 * u + 8, 128 * v:128 * v + 128]
                            tile = jnp.where(row_ok[u] & lane_ok[v], here, tile)
                    lat_s[n, c, i] = tile
            lat_copy(n).start()

        def place(n):
            def at_x(x, carry):
                s0 = jnp.where(x == x0, 1.0, 0.0).astype(F32)
                s1 = jnp.where(x == x0 + 1, 1.0, 0.0).astype(F32)
                for c in range(3):
                    tile = s0 * del_r[n, c, 0] + s1 * del_r[n, c, 1]
                    for u in range(3):
                        for v in range(3):
                            spot = (c, x, slice(8 * u, 8 * u + 8), slice(128 * v, 128 * v + 128))
                            e[spot] = e[spot] + jnp.where(row_ok[u] & lane_ok[v], tile, 0.0)
                return carry

            lax.fori_loop(0, 6, at_x, 0)

        def send_halos(n):
            for x in range(6):
                ye_s[n, 0, x:x + 1, :] = e[0, x, 0:1, :]
                ye_s[n, 1, x:x + 1, :] = e[2, x, 0:1, :]
                for c in range(3):
                    pk[c, x:x + 1, :] = e[c, x, 23:24, :]
                pk[3, x:x + 1, :] = h[0, x + 1, 31:32, :]
                pk[4, x:x + 1, :] = h[2, x + 1, 31:32, :]
            xe_s[n] = e[1:3, 0, 0:24, :]
            ex, ey, ez = e[0, 5, 0:24, :], e[1, 5, 0:24, :], e[2, 5, 0:24, :]
            wide = lax.broadcasted_iota(jnp.int32, (24, 384), 0)
            exy = jnp.where(wide == 23, 0.0, e[0, 5, 1:25, :])
            xg_s[n, 0] = h[1, 6, 8:32, :] - 0.5 * (zfwd(ex) - ex + ez)
            xg_s[n, 1] = h[2, 6, 8:32, :] + 0.5 * (ey + exy - ex)
            px, py, pz = pk[0, 0:8, :], pk[1, 0:8, :], pk[2, 0:8, :]
            yg_s[n, 0] = pk[3, 0:8, :] + 0.5 * (pz + zfwd(py) - py)
            yg_s[n, 1] = pk[4, 0:8, :] - 0.5 * (pk[1, 1:9, :] - py + px)
            c1_s[n] = jnp.broadcast_to(e[0, 5, 0:1, :], (8, 384))
            c2_s[n] = jnp.broadcast_to(e[1, 0, 23:24, :], (8, 384))
            for m, (dx, dy) in enumerate(TO_NEXT):
                @pl.when(exists(dx, dy))
                def _():
                    halo_copy(m, n).start()

        def take_halos(n):
            for m, (dx, dy) in enumerate(TO_NEXT):
                @pl.when(exists(-dx, -dy))
                def _():
                    halo_copy(m, n).wait_recv()
            e[1:3, 6, 0:24, :] = xe_r[n]
            h[1, 0, 8:32, :] = flag_x * (xg_r[n, 0] + 0.5 * e[2, 0, 0:24, :])
            wide = lax.broadcasted_iota(jnp.int32, (24, 384), 0)
            corner = jnp.where(wide == 23, jnp.broadcast_to(c1_r[n, 0:1, :], (24, 384)), 0.0)
            h[2, 0, 8:32, :] = flag_x * (xg_r[n, 1] - 0.5 * (e[1, 0, 0:24, :] - corner))
            plane = lax.broadcasted_iota(jnp.int32, (8, 384), 0)
            pln[0] = flag_y * (yg_r[n, 0] - 0.5 * ye_s[n, 1])
            pln[1] = flag_y * (yg_r[n, 1] + 0.5 * (ye_s[n, 0] - jnp.where(plane == 5, c2_r[n], 0.0)))
            for x in range(6):
                e[0, x, 24:25, :] = ye_r[n, 0, x:x + 1, :]
                e[2, x, 24:25, :] = ye_r[n, 1, x:x + 1, :]
                h[0, x + 1, 7:8, :] = pln[0, x:x + 1, :]
                h[2, x + 1, 7:8, :] = pln[1, x:x + 1, :]

        def update():
            def at_x(x, carry):
                for u in range(3):
                    r = slice(8 * u, 8 * u + 8)
                    ra = slice(8 * u + 1, 8 * u + 9)
                    hr_ = slice(8 * u + 8, 8 * u + 16)
                    hb = slice(8 * u + 7, 8 * u + 15)
                    ex, ey, ez = e[0, x, r, :], e[1, x, r, :], e[2, x, r, :]
                    hx = h[0, x + 1, hr_, :] - 0.5 * ((e[2, x, ra, :] - ez) - (zfwd(ey) - ey))
                    hy = h[1, x + 1, hr_, :] - 0.5 * ((zfwd(ex) - ex) - (e[2, x + 1, r, :] - ez))
                    hz = h[2, x + 1, hr_, :] - 0.5 * ((e[1, x + 1, r, :] - ey) - (e[0, x, ra, :] - ex))
                    h[0, x + 1, hr_, :] = hx
                    h[1, x + 1, hr_, :] = hy
                    h[2, x + 1, hr_, :] = hz
                    cx = (hz - h[2, x + 1, hb, :]) - (hy - zbwd(hy))
                    cy = (hx - zbwd(hx)) - (hz - h[2, x, hr_, :])
                    cz = (hy - h[1, x, hr_, :]) - (hx - h[0, x + 1, hb, :])
                    ka, kc, kb, kf, kg = (k[q, x, r, :] for q in range(5))
                    for c, (old, curl) in enumerate(((ex, cx), (ey, cy), (ez, cz))):
                        pol = p[c, x, r, :]
                        new = ka * old + kc * curl + kb * pol
                        e[c, x, r, :] = new
                        p[c, x, r, :] = kf * pol + kg * new
                return carry

            lax.fori_loop(0, 6, at_x, 0)

        e_in.wait()
        cut(STEPS)
        h_in.wait()
        send_halos(0)
        for cp in m_in:
            cp.wait()
        tabs = tables(permit, conduct, relax, debye, 1.0, 0.5)

        def factors(x, carry):
            for u in range(3):
                for v in range(3):
                    spot = (x, slice(8 * u, 8 * u + 8), slice(128 * v, 128 * v + 128))
                    here = mat[v, x, 8 * u:8 * u + 8, :]
                    for q in range(5):
                        k[(q,) + spot] = pick(tabs[q], here)
            return carry

        lax.fori_loop(0, 6, factors, 0)
        p_in.wait()

        def step(n, carry):
            @pl.when(n > 0)
            def _():
                del_copy(n - 1).wait_recv()
                place(n - 1)
                send_halos(n)

            take_halos(n)
            update()
            cut(n)
            return carry

        lax.fori_loop(0, STEPS, step, 0)
        h_out = pltpu.make_async_copy(h.at[:, 1:7, 8:32, :], out.at[0, 3:6], lsem.at[1])
        p_out = pltpu.make_async_copy(p, out.at[0, 6:9], lsem.at[2])
        h_out.start()
        p_out.start()
        del_copy(STEPS - 1).wait_recv()
        place(STEPS - 1)
        e_out = pltpu.make_async_copy(e.at[:, 0:6, 0:24, :], out.at[0, 0:3], lsem.at[0])
        e_out.start()

        def drain(n, carry):
            for m, (dx, dy) in enumerate(TO_NEXT):
                @pl.when(exists(dx, dy))
                def _():
                    halo_copy(m, n).wait_send()
            return carry

        lax.fori_loop(0, STEPS, drain, 0)
        for n in range(STEPS + 1):
            lat_copy(n).wait_send()
        h_out.wait()
        p_out.wait()
        e_out.wait()

    @pl.when(jnp.logical_not(coarse))
    def _():
        inside = (rows < ly) & (lanes < lz)
        two = lx == 2

        def inside_x(x):
            return jnp.where((x < 3) | two, 1, 0).astype(jnp.int32)

        tabs = tables(permit, conduct, relax, debye, 1.0 / 3.0, 0.25)
        spread = [3 * lanes + r for r in range(3)]
        packed = [(lanes + 128 * v) for v in range(3)]
        third = [q // 3 for q in packed]
        phase = [q - 3 * t for q, t in zip(packed, third)]

        def gather_in(ref, lead, ry):
            parts = [ref[(v,) + lead + (pl.ds(ry, 8, stride=3), slice(None))] for v in range(3)]
            tiles = []
            for r in range(3):
                at, src = spread[r] & 127, spread[r] >> 7
                got = [pick(part, at) for part in parts]
                tiles.append(jnp.where(src == 0, got[0], jnp.where(src == 1, got[1], got[2])))
            return tiles

        for cp in m_in:
            cp.wait()

        def fine_factors(x, carry):
            ok = inside & (inside_x(x) + jnp.zeros((8, 128), jnp.int32) > 0)
            for ry in range(3):
                for r, here in enumerate(gather_in(mat, (x,), ry)):
                    for q in range(5):
                        value = pick(tabs[q], here)
                        if q == 1 or q == 2:
                            value = jnp.where(ok, value, 0.0)
                        fk[q, x, 3 * ry + r] = value
            return carry

        lax.fori_loop(0, 6, fine_factors, 0)
        for cp in f_in:
            cp.wait()
        for c in range(3):
            ff[c, 6] = jnp.zeros((9, 8, 128), F32)
            ff[3 + c, 0] = jnp.zeros((9, 8, 128), F32)

        def load_fine(x, carry):
            ok = inside & (inside_x(x) + jnp.zeros((8, 128), jnp.int32) > 0)
            for c in range(9):
                for ry in range(3):
                    for r, here in enumerate(gather_in(stage, (c, x), ry)):
                        if 3 <= c < 6:
                            ff[c, x + 1, 3 * ry + r] = jnp.where(ok, 2.0 * here, 0.0)
                        else:
                            ff[c, x, 3 * ry + r] = jnp.where(ok, here, 0.0)
            return carry

        lax.fori_loop(0, 6, load_fine, 0)

        back_y, back_z = (8 - y0 % 8) % 8, (128 - z0 % 128) % 128
        lat_copy(STEPS).wait_recv()
        for c in range(3):
            for i in range(2):
                ear[0, c, i] = pltpu.roll(pltpu.roll(lat_r[STEPS, c, i], back_y, 0), back_z, 1)

        edge_y = {0: rows == 0, 2: rows == ly - 1}
        edge_z = {0: lanes == 0, 2: lanes == lz - 1}

        def at_layer(x, carry):
            ok = inside & (inside_x(x) + jnp.zeros((8, 128), jnp.int32) > 0)
            edge = jnp.where((x == 0) | (x == 3 * lx - 1), 1, 0).astype(jnp.int32)
            edge_x = ok & (edge + jnp.zeros((8, 128), jnp.int32) > 0)
            ok_y = {q: m & ok for q, m in edge_y.items()}
            ok_z = {q: m & ok for q, m in edge_z.items()}
            xc = x // 3
            for ry in range(3):
                for rz in range(3):
                    t = 3 * ry + rz
                    ex, ey, ez = ff[0, x, t], ff[1, x, t], ff[2, x, t]
                    if ry < 2:
                        exy, ezy = ff[0, x, t + 3], ff[2, x, t + 3]
                    else:
                        exy, ezy = yfwd(ff[0, x, rz]), yfwd(ff[2, x, rz])
                    if rz < 2:
                        exz, eyz = ff[0, x, t + 1], ff[1, x, t + 1]
                    else:
                        exz, eyz = zfwd(ff[0, x, 3 * ry]), zfwd(ff[1, x, 3 * ry])
                    eyx, ezx = ff[1, x + 1, t], ff[2, x + 1, t]
                    ff[3, x + 1, t] = ff[3, x + 1, t] - ((ezy - ez) - (eyz - ey))
                    ff[4, x + 1, t] = ff[4, x + 1, t] - ((exz - ex) - (ezx - ez))
                    ff[5, x + 1, t] = ff[5, x + 1, t] - ((eyx - ey) - (exy - ex))
            for ry in range(3):
                for rz in range(3):
                    t = 3 * ry + rz
                    hx, hy, hz = ff[3, x + 1, t], ff[4, x + 1, t], ff[5, x + 1, t]
                    if ry > 0:
                        hxy, hzy = ff[3, x + 1, t - 3], ff[5, x + 1, t - 3]
                    else:
                        hxy, hzy = ybwd(ff[3, x + 1, 6 + rz]), ybwd(ff[5, x + 1, 6 + rz])
                    if rz > 0:
                        hxz, hyz = ff[3, x + 1, t - 1], ff[4, x + 1, t - 1]
                    else:
                        hxz, hyz = zbwd(ff[3, x + 1, 3 * ry + 2]), zbwd(ff[4, x + 1, 3 * ry + 2])
                    hyx, hzx = ff[4, x, t], ff[5, x, t]
                    curls = ((hz - hzy) - (hy - hyz), (hx - hxz) - (hz - hzx), (hy - hyx) - (hx - hxy))
                    ka, kc, kb, kf, kg = (fk[q, x, t] for q in range(5))
                    for c in range(3):
                        pol = ff[6 + c, x, t]
                        new = ka * ff[c, x, t] + kc * curls[c] + kb * pol
                        marks = []
                        if c != 0:
                            marks.append(edge_x)
                        if c != 1 and ry in ok_y:
                            marks.append(ok_y[ry])
                        if c != 2 and rz in ok_z:
                            marks.append(ok_z[rz])
                        if marks:
                            new = jnp.where(functools.reduce(jnp.logical_or, marks), drv[c, xc], new)
                        ff[c, x, t] = new
                        ff[6 + c, x, t] = kf * pol + kg * new
            return carry

        def fine_step(n, carry):
            lat_copy(n).wait_recv()
            for c in range(3):
                for i in range(2):
                    ear[1, c, i] = pltpu.roll(pltpu.roll(lat_r[n, c, i], back_y, 0), back_z, 1)

            def substep(s, carry):
                weight = (s + 1).astype(F32) * (1.0 / 3.0)
                drv[...] = ear[0] + weight * (ear[1] - ear[0])
                return lax.fori_loop(0, 6, at_layer, carry)

            lax.fori_loop(0, 3, substep, 0)
            for i in range(2):
                ok = inside & (inside_x(3 * i) + jnp.zeros((8, 128), jnp.int32) > 0)
                for c in range(3):
                    total = functools.reduce(
                        jnp.add, [ff[c, 3 * i + j, t] for j in range(3) for t in range(9)])
                    latest = ear[1, c, i]
                    delta = jnp.where(ok, total * (1.0 / 27.0) - latest, 0.0)
                    ear[0, c, i] = latest + delta
                    del_s[n, c, i] = pltpu.roll(pltpu.roll(delta, y0 % 8, 0), z0 % 128, 1)
            del_copy(n).start()
            return carry

        lax.fori_loop(0, STEPS, fine_step, 0)

        def save_fine(x, carry):
            for c in range(9):
                for ry in range(3):
                    lift = 1 if 3 <= c < 6 else 0
                    parts = [ff[c, x + lift, 3 * ry + r] for r in range(3)]
                    for v in range(3):
                        got = [pick(part, third[v]) for part in parts]
                        value = jnp.where(phase[v] == 0, got[0], jnp.where(phase[v] == 1, got[1], got[2]))
                        if lift:
                            value = 0.5 * value
                        stage[v, c, x, pl.ds(ry, 8, stride=3), :] = value
            return carry

        lax.fori_loop(0, 6, save_fine, 0)
        f_out = [pltpu.make_async_copy(stage.at[v], out.at[0, :, :, :, pl.ds(128 * v, 128)], lsem.at[v]) for v in range(3)]
        for cp in f_out:
            cp.start()
        for n in range(STEPS):
            del_copy(n).wait_send()
        for cp in f_out:
            cp.wait()


def solution(mesh):
    nx, ny = mesh.shape["gx"], mesh.shape["gy"]

    def body(fields, material, permit, conduct, relax, debye, subgrids):
        vm = pltpu.VMEM
        dma = pltpu.SemaphoreType.DMA
        slots = [
            vm((STEPS, 2, 24, 384), F32), vm((STEPS, 2, 8, 384), F32),
            vm((STEPS, 2, 24, 384), F32), vm((STEPS, 2, 8, 384), F32),
            vm((STEPS, 8, 384), F32), vm((STEPS, 8, 384), F32),
        ]
        region = (3, 2, 8, 128)
        return pl.pallas_call(
            functools.partial(kernel, nx, ny),
            out_shape=jax.ShapeDtypeStruct(fields.shape, F32),
            in_specs=[pl.BlockSpec(memory_space=pl.ANY)] * 2 + [pl.BlockSpec(memory_space=pltpu.SMEM)] * 5,
            out_specs=pl.BlockSpec(memory_space=pl.ANY),
            scratch_shapes=[
                vm((3, 7, 32, 384), F32), vm((3, 7, 32, 384), F32), vm((3, 6, 24, 384), F32), vm((5, 6, 24, 384), F32),
                vm((3, 9, 6, 24, 128), F32), vm((3, 6, 24, 128), jnp.int32),
                vm((9, 7, 9, 8, 128), F32), vm((5, 6, 9, 8, 128), F32),
                vm((5, 16, 384), F32), vm((2, 8, 384), F32), vm((2,) + region, F32), vm(region, F32),
                *slots, *slots,
                vm((STEPS + 1,) + region, F32), vm((STEPS + 1,) + region, F32),
                vm((STEPS,) + region, F32), vm((STEPS,) + region, F32),
                dma((6,)), dma((6, STEPS)), dma((6, STEPS)),
                dma((STEPS + 1,)), dma((STEPS + 1,)), dma((STEPS,)), dma((STEPS,)),
            ],
            compiler_params=pltpu.CompilerParams(
                collective_id=0, has_side_effects=True, vmem_limit_bytes=40 * 1024 * 1024),
        )(fields, material, permit, conduct, relax, debye, subgrids)

    return jax.shard_map(
        body,
        mesh=mesh,
        in_specs=(P("grid", None, "gx", "gy", None), P("grid", "gx", "gy", None), P(), P(), P(), P(), P("gx", "gy", None)),
        out_specs=P("grid", None, "gx", "gy", None),
        check_vma=False,
    )
```

```python
import functools

import jax
import jax.numpy as jnp
from jax import lax
from jax.experimental import pallas as pl
from jax.experimental.pallas import tpu as pltpu
from jax.sharding import PartitionSpec as P

MESH = pl.DeviceIdType.MESH
STEPS = 3
F32 = jnp.float32

TO_NEXT = ((-1, 0), (0, -1), (1, 0), (0, 1), (1, -1), (-1, 1))
XE, YE, XG, YG, C1, C2 = range(6)


def lane_iota():
    return lax.broadcasted_iota(jnp.int32, (8, 128), 1)


def row_iota():
    return lax.broadcasted_iota(jnp.int32, (8, 128), 0)


def pick(tile, index):
    return jnp.take_along_axis(tile, index, axis=1, mode="promise_in_bounds")


def zfwd(v):
    n = v.shape[-1]
    lanes = lax.broadcasted_iota(jnp.int32, v.shape, v.ndim - 1)
    return jnp.where(lanes == n - 1, 0.0, pltpu.roll(v, n - 1, v.ndim - 1))


def zbwd(v):
    lanes = lax.broadcasted_iota(jnp.int32, v.shape, v.ndim - 1)
    return jnp.where(lanes == 0, 0.0, pltpu.roll(v, 1, v.ndim - 1))


def yfwd(t):
    return jnp.where(row_iota() == 7, 0.0, pltpu.roll(t, 7, 0))


def ybwd(t):
    return jnp.where(row_iota() == 0, 0.0, pltpu.roll(t, 1, 0))


def tables(permit, conduct, relax, debye, factor, courant):
    lane = lane_iota()

    def spread(ref):
        out = jnp.ones((8, 128), F32)
        for m in range(8):
            out = jnp.where(lane == m, ref[m], out)
        return out

    eps = spread(permit)
    damping = spread(conduct) * factor / (2.0 * eps)
    f0 = (1.0 - damping) / (1.0 + damping)
    f1 = 1.0 / (eps * (1.0 + damping))
    f2 = spread(relax) * factor
    f3 = jnp.exp(-f2)
    f4 = spread(debye)
    return f0 - f1 * f2 * f4, courant * f1, f1 * f2, f3, (1.0 - f3) * f4


def kernel(
    nx, ny,
    fields, material, permit, conduct, relax, debye, subgrids, out,
    e2, h2, p2, k, stage, mat, ff, fk, pk, pln, own, dl, pd, ear, drv, fkr,
    xe_s, ye_s, xg_s, yg_s, c1_s, c2_s,
    xe_r, ye_r, xg_r, yg_r, c1_r, c2_r,
    lat_s, lat_r, ini_s, ini_r, del_s, del_r,
    nx_s, ny_s, nd_s, nx_r, ny_r, nd_r, pos_s, pos_r, place_of,
    lsem, hs, hr, bs, br, ds, dr, ns, nr, ps, pr,
):
    grid = lax.axis_index("grid")
    ga = lax.axis_index("gx")
    gb = lax.axis_index("gy")
    coarse = grid == 0
    x0, y0, z0 = subgrids[0, 0, 0], subgrids[0, 0, 1], subgrids[0, 0, 2]
    lx, ly, lz = subgrids[0, 0, 3], subgrids[0, 0, 4], subgrids[0, 0, 5]
    sends = (xe_s, ye_s, xg_s, yg_s, c1_s, c2_s)
    recvs = (xe_r, ye_r, xg_r, yg_r, c1_r, c2_r)
    delta_s = (nx_s.at[0], ny_s.at[0], nx_s.at[1], ny_s.at[1], nd_s.at[0], nd_s.at[1])
    delta_r = (nx_r.at[0], ny_r.at[0], nx_r.at[1], ny_r.at[1], nd_r.at[0], nd_r.at[1])

    def exists(dx, dy):
        return (ga + dx >= 0) & (ga + dx < nx) & (gb + dy >= 0) & (gb + dy < ny)

    def device(g, dx, dy):
        return (g, jnp.clip(ga + dx, 0, nx - 1), jnp.clip(gb + dy, 0, ny - 1))

    partner = (1 - grid, ga, gb)
    rows, lanes = row_iota(), lane_iota()

    e_in = pltpu.make_async_copy(fields.at[0, 0:3], e2.at[0, :, 0:6, 0:24, :], lsem.at[0])
    h_in = pltpu.make_async_copy(fields.at[0, 3:6], h2.at[0, :, 1:7, 8:32, :], lsem.at[1])
    p_in = pltpu.make_async_copy(fields.at[0, 6:9], p2.at[0], lsem.at[2])
    f_in = [pltpu.make_async_copy(fields.at[0, :, :, :, pl.ds(128 * v, 128)], stage.at[v], lsem.at[v]) for v in range(3)]
    m_in = [pltpu.make_async_copy(material.at[0, :, :, pl.ds(128 * v, 128)], mat.at[v], lsem.at[3 + v]) for v in range(3)]

    @pl.when(coarse)
    def _():
        for cp in (e_in, h_in, p_in):
            cp.start()

    @pl.when(jnp.logical_not(coarse))
    def _():
        for cp in f_in:
            cp.start()

    for cp in m_in:
        cp.start()
    for ref in (nx_r, ny_r, nd_r, pos_r):
        ref[...] = jnp.zeros_like(ref)

    @pl.when(coarse)
    def _():
        for ref in (ye_s, yg_s, pk, pln, own) + recvs:
            ref[...] = jnp.zeros_like(ref)

    barrier = pltpu.get_barrier_semaphore()
    pl.semaphore_signal(barrier, inc=1, device_id=partner, device_id_type=MESH)
    count = jnp.int32(1)
    for dx, dy in TO_NEXT:
        count = count + exists(dx, dy).astype(jnp.int32)

        @pl.when(exists(dx, dy))
        def _():
            pl.semaphore_signal(barrier, inc=1, device_id=(grid, ga + dx, gb + dy), device_id_type=MESH)

    pos_s[...] = jnp.where(rows == 0, x0, jnp.where(rows == 1, y0, z0))
    pl.semaphore_wait(barrier, count)

    def remote(src, dst, send, recv, target):
        return pltpu.make_async_remote_copy(
            src_ref=src, dst_ref=dst, send_sem=send, recv_sem=recv, device_id=target, device_id_type=MESH)

    def halo_copy(m, n):
        return remote(sends[m].at[n], recvs[m].at[n], hs.at[m, n], hr.at[m, n], device(grid, *TO_NEXT[m]))

    def lat_copy(n):
        return remote(lat_s.at[n], lat_r.at[n], bs.at[n], br.at[n], partner)

    def ini_copy():
        return remote(ini_s, ini_r, bs.at[STEPS], br.at[STEPS], partner)

    def del_copy(n):
        return remote(del_s.at[n], del_r.at[n], ds.at[n], dr.at[n], partner)

    def near_copy(g, m, n):
        return remote(delta_s[m].at[n], delta_r[m].at[n], ns.at[g, m, n], nr.at[m, n], device(g, *TO_NEXT[m]))

    def pos_copy(m):
        return remote(pos_s, pos_r.at[m], ps.at[m], pr.at[m], device(grid, *TO_NEXT[m]))

    def each(turn, fun):
        for m, (dx, dy) in enumerate(TO_NEXT):
            @pl.when(exists(turn * dx, turn * dy))
            def _():
                fun(m)

    def learn_places():
        each(-1, lambda m: pos_copy(m).wait_recv())
        cp = pltpu.make_async_copy(pos_r, place_of, lsem.at[6])
        cp.start()
        cp.wait()

    def row_in(low, u):
        return (rows + 8 * u >= low) & (rows + 8 * u < low + 8)

    def lane_in(low, v):
        return (lanes + 128 * v >= low) & (lanes + 128 * v < low + 128)

    def tile_at(u, v):
        return (slice(8 * u, 8 * u + 8), slice(128 * v, 128 * v + 128))

    @pl.when(coarse)
    def _():
        flag_x = jnp.where(ga > 0, 1.0, 0.0).astype(F32)
        flag_y = jnp.where(gb > 0, 1.0, 0.0).astype(F32)
        row_ok = [row_in(y0, u) for u in range(3)]
        lane_ok = [lane_in(z0, v) for v in range(3)]
        wide = lax.broadcasted_iota(jnp.int32, (24, 384), 0)
        plane = lax.broadcasted_iota(jnp.int32, (8, 384), 0)

        def cut(load, i):
            tile = jnp.zeros((8, 128), F32)
            for u in range(3):
                for v in range(3):
                    tile = jnp.where(row_ok[u] & lane_ok[v], load(x0 + i, *tile_at(u, v)), tile)
            return tile

        def cut_latest(n, e):
            for i in range(2):
                for c in range(3):
                    lat_s[n, c, i] = cut(lambda x, r, l: e[c, x, r, l], i)
            lat_copy(n).start()

        def place(n, e):
            def at_x(x, carry):
                s0 = jnp.where(x == x0, 1.0, 0.0).astype(F32)
                s1 = jnp.where(x == x0 + 1, 1.0, 0.0).astype(F32)
                for c in range(3):
                    tile = s0 * del_r[n, c, 0] + s1 * del_r[n, c, 1]
                    for u in range(3):
                        for v in range(3):
                            spot = (c, x) + tile_at(u, v)
                            e[spot] = e[spot] + jnp.where(row_ok[u] & lane_ok[v], tile, 0.0)
                return carry

            lax.fori_loop(0, 6, at_x, 0)

        def send_halos(n, e, h):
            for x in range(6):
                ye_s[n, 0, x:x + 1, :] = e[0, x, 0:1, :]
                ye_s[n, 1, x:x + 1, :] = e[2, x, 0:1, :]
                for c in range(3):
                    pk[c, x:x + 1, :] = e[c, x, 23:24, :]
                pk[3, x:x + 1, :] = h[0, x + 1, 31:32, :]
                pk[4, x:x + 1, :] = h[2, x + 1, 31:32, :]
            xe_s[n] = e[1:3, 0, 0:24, :]
            ex, ey, ez = e[0, 5, 0:24, :], e[1, 5, 0:24, :], e[2, 5, 0:24, :]
            exy = jnp.where(wide == 23, 0.0, e[0, 5, 1:25, :])
            xg_s[n, 0] = h[1, 6, 8:32, :] - 0.5 * (zfwd(ex) - ex + ez)
            xg_s[n, 1] = h[2, 6, 8:32, :] + 0.5 * (ey + exy - ex)
            px, py, pz = pk[0, 0:8, :], pk[1, 0:8, :], pk[2, 0:8, :]
            yg_s[n, 0] = pk[3, 0:8, :] + 0.5 * (pz + zfwd(py) - py)
            yg_s[n, 1] = pk[4, 0:8, :] - 0.5 * (pk[1, 1:9, :] - py + px)
            c1_s[n] = jnp.broadcast_to(e[0, 5, 0:1, :], (8, 384))
            c2_s[n] = jnp.broadcast_to(e[1, 0, 23:24, :], (8, 384))
            each(1, lambda m: halo_copy(m, n).start())

        def put_halos(n, e, h):
            e[1:3, 6, 0:24, :] = xe_r[n]
            h[1, 0, 8:32, :] = flag_x * (xg_r[n, 0] + 0.5 * e[2, 0, 0:24, :])
            corner = jnp.where(wide == 23, jnp.broadcast_to(c1_r[n, 0:1, :], (24, 384)), 0.0)
            h[2, 0, 8:32, :] = flag_x * (xg_r[n, 1] - 0.5 * (e[1, 0, 0:24, :] - corner))
            for x in range(6):
                own[0, x:x + 1, :] = e[0, x, 0:1, :]
                own[1, x:x + 1, :] = e[2, x, 0:1, :]
            pln[0] = flag_y * (yg_r[n, 0] - 0.5 * own[1])
            pln[1] = flag_y * (yg_r[n, 1] + 0.5 * (own[0] - jnp.where(plane == 5, c2_r[n], 0.0)))
            for x in range(6):
                e[0, x, 24:25, :] = ye_r[n, 0, x:x + 1, :]
                e[2, x, 24:25, :] = ye_r[n, 1, x:x + 1, :]
                h[0, x + 1, 7:8, :] = pln[0, x:x + 1, :]
                h[2, x + 1, 7:8, :] = pln[1, x:x + 1, :]

        def mend_halos(n):
            d = n - 1
            each(-1, lambda m: near_copy(0, m, d).wait_recv())
            for u in range(3):
                for v in range(3):
                    spot = tile_at(u, v)
                    ok = row_in(place_of[XE, 1, 0], u) & lane_in(place_of[XE, 2, 0], v)
                    for q in range(2):
                        xe_r[(n, q) + spot] = xe_r[(n, q) + spot] + jnp.where(ok, nx_r[0, d, 1 + q], 0.0)
                    ok = row_in(place_of[XG, 1, 0], u) & lane_in(place_of[XG, 2, 0], v)
                    for c in range(3):
                        dl[(c,) + spot] = jnp.where(ok, nx_r[1, d, c], 0.0)
            tx, ty, tz = dl[0, 0:24, :], dl[1, 0:24, :], dl[2, 0:24, :]
            dl[0, 24:32, :] = jnp.zeros((8, 384), F32)
            xg_r[n, 0] = xg_r[n, 0] - 0.5 * (zfwd(tx) - tx + tz)
            xg_r[n, 1] = xg_r[n, 1] + 0.5 * (ty + dl[0, 1:25, :] - tx)
            for m, keep in ((YE, ny_r.at[0]), (YG, ny_r.at[1])):
                at = place_of[m, 0, 0]
                for c in range(3):
                    two = [jnp.broadcast_to(keep[d, 2 * c + i:2 * c + i + 1, :], (8, 128)) for i in range(2)]
                    both = jnp.where(rows == at, two[0], jnp.where(rows == at + 1, two[1], 0.0))
                    for v in range(3):
                        pd[c, :, 128 * v:128 * v + 128] = jnp.where(lane_in(place_of[m, 2, 0], v), both, 0.0)
                if m == YE:
                    ye_r[n, 0] = ye_r[n, 0] + pd[0]
                    ye_r[n, 1] = ye_r[n, 1] + pd[2]
                else:
                    yg_r[n, 0] = yg_r[n, 0] + 0.5 * (pd[2] + zfwd(pd[1]) - pd[1])
                    yg_r[n, 1] = yg_r[n, 1] - 0.5 * (pltpu.roll(pd[1], 7, 0) - pd[1] + pd[0])
            for m, ref, keep in ((C1, c1_r, nd_r.at[0]), (C2, c2_r, nd_r.at[1])):
                for v in range(3):
                    spot = (n, slice(0, 8), slice(128 * v, 128 * v + 128))
                    ref[spot] = ref[spot] + jnp.where(lane_in(place_of[m, 2, 0], v), keep[d], 0.0)

        def update(e, h, p, ed, hd, pd_):
            def at_x(x, carry):
                for u in range(3):
                    r = slice(8 * u, 8 * u + 8)
                    ra = slice(8 * u + 1, 8 * u + 9)
                    rh = slice(8 * u + 8, 8 * u + 16)
                    rb = slice(8 * u + 7, 8 * u + 15)
                    ex, ey, ez = e[0, x, r, :], e[1, x, r, :], e[2, x, r, :]
                    hx = h[0, x + 1, rh, :] - 0.5 * ((e[2, x, ra, :] - ez) - (zfwd(ey) - ey))
                    hy = h[1, x + 1, rh, :] - 0.5 * ((zfwd(ex) - ex) - (e[2, x + 1, r, :] - ez))
                    hz = h[2, x + 1, rh, :] - 0.5 * ((e[1, x + 1, r, :] - ey) - (e[0, x, ra, :] - ex))
                    hd[0, x + 1, rh, :] = hx
                    hd[1, x + 1, rh, :] = hy
                    hd[2, x + 1, rh, :] = hz
                    cx = (hz - hd[2, x + 1, rb, :]) - (hy - zbwd(hy))
                    cy = (hx - zbwd(hx)) - (hz - hd[2, x, rh, :])
                    cz = (hy - hd[1, x, rh, :]) - (hx - hd[0, x + 1, rb, :])
                    ka, kc, kb, kf, kg = (k[q, x, r, :] for q in range(5))
                    for c, (old, curl) in enumerate(((ex, cx), (ey, cy), (ez, cz))):
                        pol = p[c, x, r, :]
                        new = ka * old + kc * curl + kb * pol
                        ed[c, x, r, :] = new
                        if pd_ is not None:
                            pd_[c, x, r, :] = kf * pol + kg * new
                return carry

            lax.fori_loop(0, 6, at_x, 0)

        sets = [(e2.at[q], h2.at[q], p2.at[q]) for q in range(2)]
        each(1, lambda m: pos_copy(m).start())
        e_in.wait()
        h_in.wait()
        send_halos(0, sets[0][0], sets[0][1])
        for cp in m_in:
            cp.wait()
        tabs = tables(permit, conduct, relax, debye, 1.0, 0.5)

        def factors(x, carry):
            for u in range(3):
                for v in range(3):
                    here = mat[v, x, 8 * u:8 * u + 8, :]
                    for q in range(5):
                        k[(q, x) + tile_at(u, v)] = pick(tabs[q], here)
            return carry

        lax.fori_loop(0, 6, factors, 0)
        for i in range(2):
            for c in range(3):
                ini_s[c, i] = cut(lambda x, r, l: e2[0, c, x, r, l], i)
            for q in range(2):
                ini_s[3 + q, i] = cut(lambda x, r, l: k[q, x, r, l], i)
        ini_copy().start()
        p_in.wait()
        for n in range(STEPS):
            now, then = sets[n % 2], sets[(n + 1) % 2]
            each(-1, lambda m: halo_copy(m, n).wait_recv())
            if n == 0:
                put_halos(n, now[0], then[1])
                update(*now, *then)
                cut_latest(0, then[0])
                learn_places()
            else:
                put_halos(n, now[0], then[1])
                update(*now, then[0], then[1], None)
                cut_latest(n, then[0])
                del_copy(n - 1).wait_recv()
                place(n - 1, now[0])
                mend_halos(n)
                put_halos(n, now[0], then[1])
                update(*now, *then)
            if n + 1 < STEPS:
                send_halos(n + 1, then[0], then[1])
        e, h, p = sets[STEPS % 2]
        h_out = pltpu.make_async_copy(h.at[:, 1:7, 8:32, :], out.at[0, 3:6], lsem.at[1])
        p_out = pltpu.make_async_copy(p, out.at[0, 6:9], lsem.at[2])
        h_out.start()
        p_out.start()
        del_copy(STEPS - 1).wait_recv()
        place(STEPS - 1, e)
        e_out = pltpu.make_async_copy(e.at[:, 0:6, 0:24, :], out.at[0, 0:3], lsem.at[0])
        e_out.start()

        each(1, lambda m: pos_copy(m).wait_send())
        for n in range(STEPS):
            each(1, lambda m: halo_copy(m, n).wait_send())
            lat_copy(n).wait_send()
        ini_copy().wait_send()
        h_out.wait()
        p_out.wait()
        e_out.wait()

    @pl.when(jnp.logical_not(coarse))
    def _():
        none = jnp.zeros((8, 128), jnp.int32)
        inside = (rows < ly) & (lanes < lz)
        two = lx == 2

        def inside_x(x):
            return jnp.where((x < 3) | two, 1, 0).astype(jnp.int32)

        each(1, lambda m: pos_copy(m).start())
        tabs = tables(permit, conduct, relax, debye, 1.0 / 3.0, 0.25)
        spread = [3 * lanes + r for r in range(3)]
        packed = [(lanes + 128 * v) for v in range(3)]
        third = [q // 3 for q in packed]
        phase = [q - 3 * t for q, t in zip(packed, third)]

        def gather_in(ref, lead, ry):
            parts = [ref[(v,) + lead + (pl.ds(ry, 8, stride=3), slice(None))] for v in range(3)]
            tiles = []
            for r in range(3):
                at, src = spread[r] & 127, spread[r] >> 7
                got = [pick(part, at) for part in parts]
                tiles.append(jnp.where(src == 0, got[0], jnp.where(src == 1, got[1], got[2])))
            return tiles

        for cp in m_in:
            cp.wait()

        def fine_factors(x, carry):
            ok = inside & (inside_x(x) + none > 0)
            for ry in range(3):
                for r, here in enumerate(gather_in(mat, (x,), ry)):
                    ka, kc, kb, kf, kg = (pick(tabs[q], here) for q in range(5))
                    t = 3 * ry + r
                    fk[0, x, t] = ka
                    fk[1, x, t] = jnp.where(ok, kc, 0.0)
                    fk[2, x, t] = jnp.where(ok, kb * kg, 0.0)
                    fk[3, x, t] = kf
                    fk[4, x, t] = kg
                    fkr[x, t] = 1.0 / kg
            return carry

        lax.fori_loop(0, 6, fine_factors, 0)
        for cp in f_in:
            cp.wait()
        for c in range(3):
            ff[c, 6] = jnp.zeros((9, 8, 128), F32)
            ff[3 + c, 0] = jnp.zeros((9, 8, 128), F32)

        def load_fine(x, carry):
            ok = inside & (inside_x(x) + none > 0)
            for c in range(9):
                for ry in range(3):
                    for r, here in enumerate(gather_in(stage, (c, x), ry)):
                        t = 3 * ry + r
                        if 3 <= c < 6:
                            ff[c, x + 1, t] = jnp.where(ok, 2.0 * here, 0.0)
                        elif c < 3:
                            ff[c, x, t] = jnp.where(ok, here, 0.0)
                        else:
                            ff[c, x, t] = jnp.where(ok, here * fkr[x, t], 0.0)
            return carry

        lax.fori_loop(0, 6, load_fine, 0)

        back_y, back_z = (8 - y0 % 8) % 8, (128 - z0 % 128) % 128

        def to_box(tile):
            return pltpu.roll(pltpu.roll(tile, back_y, 0), back_z, 1)

        def from_box(tile):
            return pltpu.roll(pltpu.roll(tile, y0 % 8, 0), z0 % 128, 1)

        edge_y = {0: rows == 0, 2: rows == ly - 1}
        edge_z = {0: lanes == 0, 2: lanes == lz - 1}

        def at_layer(x, carry):
            ok = inside & (inside_x(x) + none > 0)
            edge = jnp.where((x == 0) | (x == 3 * lx - 1), 1, 0).astype(jnp.int32)
            edge_x = ok & (edge + none > 0)
            ok_y = {q: m & ok for q, m in edge_y.items()}
            ok_z = {q: m & ok for q, m in edge_z.items()}
            xc = x // 3
            tiles = [(ry, rz) for ry in range(3) for rz in range(3)]
            E = {(c, t): ff[c, x, t] for c in range(3) for t in range(9)}
            F = {(c, t): ff[c, x + 1, t] for c in (1, 2) for t in range(9)}
            H = {}
            for ry, rz in tiles:
                t = 3 * ry + rz
                ex, ey, ez = (E[c, t] for c in range(3))
                if ry < 2:
                    exy, ezy = E[0, t + 3], E[2, t + 3]
                else:
                    exy, ezy = yfwd(E[0, rz]), yfwd(E[2, rz])
                if rz < 2:
                    exz, eyz = E[0, t + 1], E[1, t + 1]
                else:
                    exz, eyz = zfwd(E[0, 3 * ry]), zfwd(E[1, 3 * ry])
                H[0, t] = ff[3, x + 1, t] - ((ezy - ez) - (eyz - ey))
                H[1, t] = ff[4, x + 1, t] - ((exz - ex) - (F[2, t] - ez))
                H[2, t] = ff[5, x + 1, t] - ((F[1, t] - ey) - (exy - ex))
                for c in range(3):
                    ff[3 + c, x + 1, t] = H[c, t]
            for ry, rz in tiles:
                t = 3 * ry + rz
                hx, hy, hz = (H[c, t] for c in range(3))
                if ry > 0:
                    hxy, hzy = H[0, t - 3], H[2, t - 3]
                else:
                    hxy, hzy = ybwd(H[0, 6 + rz]), ybwd(H[2, 6 + rz])
                if rz > 0:
                    hxz, hyz = H[0, t - 1], H[1, t - 1]
                else:
                    hxz, hyz = zbwd(H[0, 3 * ry + 2]), zbwd(H[1, 3 * ry + 2])
                hyx, hzx = ff[4, x, t], ff[5, x, t]
                curls = ((hz - hzy) - (hy - hyz), (hx - hxz) - (hz - hzx), (hy - hyx) - (hx - hxy))
                ka, kc, kb, kf = (fk[q, x, t] for q in range(4))
                for c in range(3):
                    pol = ff[6 + c, x, t]
                    new = ka * E[c, t] + kc * curls[c] + kb * pol
                    marks = []
                    if c != 0:
                        marks.append(edge_x)
                    if c != 1 and ry in ok_y:
                        marks.append(ok_y[ry])
                    if c != 2 and rz in ok_z:
                        marks.append(ok_z[rz])
                    if marks:
                        new = jnp.where(functools.reduce(jnp.logical_or, marks), drv[c, xc], new)
                    ff[c, x, t] = new
                    ff[6 + c, x, t] = kf * pol + new
            return carry

        wrows = lax.broadcasted_iota(jnp.int32, (16, 256), 0)
        wlanes = lax.broadcasted_iota(jnp.int32, (16, 256), 1)
        at_y = y0 - 4 + ((wrows - (y0 - 4)) & 15)
        at_z = z0 - 64 + ((wlanes - (z0 - 64)) & 255)

        def w_in(at, low, size):
            return (at >= low) & (at < low + size)

        def twice(tile):
            return jnp.concatenate([jnp.concatenate([tile, tile], axis=1)] * 2, axis=0)

        def as_int(flag):
            return jnp.where(flag, 1, 0).astype(jnp.int32)

        def correction(n):
            each(-1, lambda m: near_copy(1, m, n - 1).wait_recv())
            d = n - 1
            region = w_in(at_y, y0, 8) & w_in(at_z, z0, 128)
            wide_none = jnp.zeros((16, 256), jnp.int32)
            w = {}
            for c in range(3):
                for xr in range(-1, 3):
                    w[c, xr] = jnp.where(region, twice(del_s[d, c, xr]), 0.0) if 0 <= xr < 2 else jnp.zeros((16, 256), F32)
            for m, xr, at_edge in ((XE, 2, x0 == 4), (XG, -1, x0 == 0)):
                ok = w_in(at_y, place_of[m, 1, 0], 8) & w_in(at_z, place_of[m, 2, 0], 128)
                ok = ok & (as_int(at_edge) + wide_none > 0)
                for c in range(3):
                    w[c, xr] = w[c, xr] + jnp.where(ok, twice(nx_r[m // 2, d, c]), 0.0)
            for m, y in ((YE, 24), (YG, -1)):
                ok = (at_y == y) & w_in(at_z, place_of[m, 2, 0], 128)
                for c in range(3):
                    two_rows = [ny_r[m // 2, d, 2 * c + i:2 * c + i + 1, :] for i in range(2)]
                    for xr in range(-1, 3):
                        i = x0 + xr - place_of[m, 0, 0]
                        s0 = jnp.where(i == 0, 1.0, 0.0).astype(F32)
                        s1 = jnp.where(i == 1, 1.0, 0.0).astype(F32)
                        row = jnp.broadcast_to(s0 * two_rows[0] + s1 * two_rows[1], (8, 128))
                        w[c, xr] = w[c, xr] + jnp.where(ok, twice(row), 0.0)
            for m, c, xr, y, at_edge in ((C1, 0, -1, 24, x0 == 0), (C2, 1, 2, -1, x0 == 4)):
                ok = (at_y == y) & w_in(at_z, place_of[m, 2, 0], 128) & (as_int(at_edge) + wide_none > 0)
                w[c, xr] = w[c, xr] + jnp.where(ok, twice(nd_r[m - 4, d]), 0.0)

            def up_y(a):
                return pltpu.roll(a, 15, 0)

            def up_z(a):
                return pltpu.roll(a, 255, 1)

            def down_y(a):
                return pltpu.roll(a, 1, 0)

            def down_z(a):
                return pltpu.roll(a, 1, 1)

            held = (at_z >= 0) & (at_y + 24 * gb >= 0)
            hh = {}
            for xr in range(-1, 2):
                ok = held & (as_int(x0 + xr + 6 * ga >= 0) + wide_none > 0)
                ex, ey, ez = (w[c, xr] for c in range(3))
                moved = ((up_y(ez) - ez) - (up_z(ey) - ey), (up_z(ex) - ex) - (w[2, xr + 1] - ez),
                         (w[1, xr + 1] - ey) - (up_y(ex) - ex))
                for c in range(3):
                    hh[c, xr] = jnp.where(ok, -0.5 * moved[c], 0.0)
            for xr in range(2):
                hx, hy, hz = (hh[c, xr] for c in range(3))
                curls = ((hz - down_y(hz)) - (hy - down_z(hy)), (hx - down_z(hx)) - (hz - hh[2, xr - 1]),
                         (hy - hh[1, xr - 1]) - (hx - down_y(hx)))
                for c in range(3):
                    kept = jnp.where(region, curls[c], 0.0)
                    tile = (kept[0:8, 0:128] + kept[0:8, 128:256]) + (kept[8:16, 0:128] + kept[8:16, 128:256])
                    ear[1, c, xr] = to_box(lat_r[n, c, xr] + ini_r[3, xr] * del_s[d, c, xr] + ini_r[4, xr] * tile)

        learn_places()
        ini_copy().wait_recv()
        for c in range(3):
            for i in range(2):
                ear[0, c, i] = to_box(ini_r[c, i])

        for n in range(STEPS):
            lat_copy(n).wait_recv()
            if n == 0:
                for c in range(3):
                    for i in range(2):
                        ear[1, c, i] = to_box(lat_r[0, c, i])
            else:
                correction(n)

            def substep(s, carry):
                weight = (s + 1).astype(F32) * (1.0 / 3.0)
                drv[...] = ear[0] + weight * (ear[1] - ear[0])
                return lax.fori_loop(0, 6, at_layer, carry)

            lax.fori_loop(0, 3, substep, 0)
            for i in range(2):
                ok = inside & (inside_x(3 * i) + none > 0)
                for c in range(3):
                    total = functools.reduce(
                        jnp.add, [ff[c, 3 * i + j, t] for j in range(3) for t in range(9)])
                    latest = ear[1, c, i]
                    delta = jnp.where(ok, total * (1.0 / 27.0) - latest, 0.0)
                    ear[0, c, i] = latest + delta
                    del_s[n, c, i] = from_box(delta)
            if n + 1 < STEPS:
                low, high = (jnp.where(x0 == q, 1.0, 0.0).astype(F32) for q in (0, 4))
                left, right = (jnp.where(y0 == q, 1.0, 0.0).astype(F32) for q in (0, 16))
                for c in range(3):
                    nx_s[0, n, c] = low * del_s[n, c, 0]
                    nx_s[1, n, c] = high * del_s[n, c, 1]
                    for i in range(2):
                        ny_s[0, n, 2 * c + i:2 * c + i + 1, :] = left * del_s[n, c, i, 0:1, :]
                        ny_s[1, n, 2 * c + i:2 * c + i + 1, :] = right * del_s[n, c, i, 7:8, :]
                for q in range(2):
                    ny_s[q, n, 6:8, :] = jnp.zeros((2, 128), F32)
                nd_s[0, n] = jnp.broadcast_to((high * left) * del_s[n, 0, 1, 0:1, :], (8, 128))
                nd_s[1, n] = jnp.broadcast_to((low * right) * del_s[n, 1, 0, 7:8, :], (8, 128))
                each(1, lambda m: near_copy(1, m, n).start())
                del_copy(n).start()
                each(1, lambda m: near_copy(0, m, n).start())
            else:
                del_copy(n).start()

        def save_fine(x, carry):
            for c in range(9):
                for ry in range(3):
                    lift = 1 if 3 <= c < 6 else 0
                    parts = [ff[c, x + lift, 3 * ry + r] for r in range(3)]
                    if c >= 6:
                        parts = [part * fk[4, x, 3 * ry + r] for r, part in enumerate(parts)]
                    for v in range(3):
                        got = [pick(part, third[v]) for part in parts]
                        value = jnp.where(phase[v] == 0, got[0], jnp.where(phase[v] == 1, got[1], got[2]))
                        if lift:
                            value = 0.5 * value
                        stage[v, c, x, pl.ds(ry, 8, stride=3), :] = value
            return carry

        lax.fori_loop(0, 6, save_fine, 0)
        f_out = [pltpu.make_async_copy(stage.at[v], out.at[0, :, :, :, pl.ds(128 * v, 128)], lsem.at[v]) for v in range(3)]
        for cp in f_out:
            cp.start()
        each(1, lambda m: pos_copy(m).wait_send())
        for n in range(STEPS):
            del_copy(n).wait_send()
            if n + 1 < STEPS:
                for g in range(2):
                    each(1, lambda m: near_copy(g, m, n).wait_send())
        for cp in f_out:
            cp.wait()


def solution(mesh):
    nx, ny = mesh.shape["gx"], mesh.shape["gy"]

    def body(fields, material, permit, conduct, relax, debye, subgrids):
        vm = pltpu.VMEM
        dma = pltpu.SemaphoreType.DMA
        slots = [
            vm((STEPS, 2, 24, 384), F32), vm((STEPS, 2, 8, 384), F32),
            vm((STEPS, 2, 24, 384), F32), vm((STEPS, 2, 8, 384), F32),
            vm((STEPS, 8, 384), F32), vm((STEPS, 8, 384), F32),
        ]
        region = (3, 2, 8, 128)
        near = [vm((2, STEPS - 1, 3, 8, 128), F32), vm((2, STEPS - 1, 8, 128), F32), vm((2, STEPS - 1, 8, 128), F32)]
        return pl.pallas_call(
            functools.partial(kernel, nx, ny),
            out_shape=jax.ShapeDtypeStruct(fields.shape, F32),
            in_specs=[pl.BlockSpec(memory_space=pl.ANY)] * 2 + [pl.BlockSpec(memory_space=pltpu.SMEM)] * 5,
            out_specs=pl.BlockSpec(memory_space=pl.ANY),
            scratch_shapes=[
                vm((2, 3, 7, 32, 384), F32), vm((2, 3, 7, 32, 384), F32), vm((2, 3, 6, 24, 384), F32), vm((5, 6, 24, 384), F32),
                vm((3, 9, 6, 24, 128), F32), vm((3, 6, 24, 128), jnp.int32),
                vm((9, 7, 9, 8, 128), F32), vm((5, 6, 9, 8, 128), F32),
                vm((5, 16, 384), F32), vm((2, 8, 384), F32), vm((2, 8, 384), F32), vm((3, 32, 384), F32), vm((3, 8, 384), F32),
                vm((2,) + region, F32), vm(region, F32), vm((6, 9, 8, 128), F32),
                *slots, *slots,
                vm((STEPS,) + region, F32), vm((STEPS,) + region, F32), vm((5, 2, 8, 128), F32), vm((5, 2, 8, 128), F32),
                vm((STEPS,) + region, F32), vm((STEPS,) + region, F32),
                *near, *near, vm((8, 128), jnp.int32), vm((6, 8, 128), jnp.int32), pltpu.SMEM((6, 8, 128), jnp.int32),
                dma((7,)), dma((6, STEPS)), dma((6, STEPS)),
                dma((STEPS + 1,)), dma((STEPS + 1,)), dma((STEPS,)), dma((STEPS,)),
                dma((2, 6, STEPS)), dma((6, STEPS)), dma((6,)), dma((6,)),
            ],
            compiler_params=pltpu.CompilerParams(
                collective_id=0, has_side_effects=True, vmem_limit_bytes=63 * 1024 * 1024),
        )(fields, material, permit, conduct, relax, debye, subgrids)

    return jax.shard_map(
        body,
        mesh=mesh,
        in_specs=(P("grid", None, "gx", "gy", None), P("grid", "gx", "gy", None), P(), P(), P(), P(), P("gx", "gy", None)),
        out_specs=P("grid", None, "gx", "gy", None),
        check_vma=False,
    )
```

```python
import functools

import jax
import jax.numpy as jnp
from jax import lax
from jax.experimental import pallas as pl
from jax.experimental.pallas import tpu as pltpu
from jax.sharding import PartitionSpec as P

MESH = pl.DeviceIdType.MESH
STEPS = 3
F32 = jnp.float32

TO_NEXT = ((-1, 0), (0, -1), (1, 0), (0, 1), (1, -1), (-1, 1))
XE, YE, XG, YG, C1, C2 = range(6)


def lane_iota():
    return lax.broadcasted_iota(jnp.int32, (8, 128), 1)


def row_iota():
    return lax.broadcasted_iota(jnp.int32, (8, 128), 0)


def pick(tile, index):
    return jnp.take_along_axis(tile, index, axis=1, mode="promise_in_bounds")


def zfwd(v):
    n = v.shape[-1]
    lanes = lax.broadcasted_iota(jnp.int32, v.shape, v.ndim - 1)
    return jnp.where(lanes == n - 1, 0.0, pltpu.roll(v, n - 1, v.ndim - 1))


def zbwd(v):
    lanes = lax.broadcasted_iota(jnp.int32, v.shape, v.ndim - 1)
    return jnp.where(lanes == 0, 0.0, pltpu.roll(v, 1, v.ndim - 1))


def yfwd(t):
    return jnp.where(row_iota() == 7, 0.0, pltpu.roll(t, 7, 0))


def ybwd(t):
    return jnp.where(row_iota() == 0, 0.0, pltpu.roll(t, 1, 0))


def tables(permit, conduct, relax, debye, factor, courant):
    lane = lane_iota()

    def spread(ref):
        out = jnp.ones((8, 128), F32)
        for m in range(8):
            out = jnp.where(lane == m, ref[m], out)
        return out

    eps = spread(permit)
    damping = spread(conduct) * factor / (2.0 * eps)
    f0 = (1.0 - damping) / (1.0 + damping)
    f1 = 1.0 / (eps * (1.0 + damping))
    f2 = spread(relax) * factor
    f3 = jnp.exp(-f2)
    f4 = spread(debye)
    return f0 - f1 * f2 * f4, courant * f1, f1 * f2, f3, (1.0 - f3) * f4


def kernel(
    nx, ny,
    fields, material, permit, conduct, relax, debye, subgrids, out,
    e2, h2, p2, k, stage, mat, ff, fk, pk, pln, own, dl, pd, ear, drv, fkr,
    xe_s, ye_s, xg_s, yg_s, c1_s, c2_s,
    xe_r, ye_r, xg_r, yg_r, c1_r, c2_r,
    lat_s, lat_r, ini_s, ini_r, del_s, del_r,
    nx_s, ny_s, nd_s, nx_r, ny_r, nd_r, pos_s, pos_r, place_of,
    lsem, hs, hr, bs, br, ds, dr, ns, nr, ps, pr,
):
    grid = lax.axis_index("grid")
    ga = lax.axis_index("gx")
    gb = lax.axis_index("gy")
    coarse = grid == 0
    x0, y0, z0 = subgrids[0, 0, 0], subgrids[0, 0, 1], subgrids[0, 0, 2]
    lx, ly, lz = subgrids[0, 0, 3], subgrids[0, 0, 4], subgrids[0, 0, 5]
    sends = (xe_s, ye_s, xg_s, yg_s, c1_s, c2_s)
    recvs = (xe_r, ye_r, xg_r, yg_r, c1_r, c2_r)
    delta_s = (nx_s.at[0], ny_s.at[0], nx_s.at[1], ny_s.at[1], nd_s.at[0], nd_s.at[1])
    delta_r = (nx_r.at[0], ny_r.at[0], nx_r.at[1], ny_r.at[1], nd_r.at[0], nd_r.at[1])

    def exists(dx, dy):
        return (ga + dx >= 0) & (ga + dx < nx) & (gb + dy >= 0) & (gb + dy < ny)

    def device(g, dx, dy):
        return (g, jnp.clip(ga + dx, 0, nx - 1), jnp.clip(gb + dy, 0, ny - 1))

    partner = (1 - grid, ga, gb)
    rows, lanes = row_iota(), lane_iota()

    e_in = pltpu.make_async_copy(fields.at[0, 0:3], e2.at[0, :, 0:6, 0:24, :], lsem.at[0])
    h_in = pltpu.make_async_copy(fields.at[0, 3:6], h2.at[0, :, 1:7, 8:32, :], lsem.at[1])
    p_in = pltpu.make_async_copy(fields.at[0, 6:9], p2.at[0], lsem.at[2])
    f_in = [pltpu.make_async_copy(fields.at[0, :, :, :, pl.ds(128 * v, 128)], stage.at[v], lsem.at[v]) for v in range(3)]
    m_in = [pltpu.make_async_copy(material.at[0, :, :, pl.ds(128 * v, 128)], mat.at[v], lsem.at[3 + v]) for v in range(3)]

    @pl.when(coarse)
    def _():
        for cp in (e_in, h_in, p_in):
            cp.start()

    @pl.when(jnp.logical_not(coarse))
    def _():
        for cp in f_in:
            cp.start()

    for cp in m_in:
        cp.start()
    for ref in (nx_r, ny_r, nd_r, pos_r):
        ref[...] = jnp.zeros_like(ref)

    @pl.when(coarse)
    def _():
        for ref in (ye_s, yg_s, pk, pln, own) + recvs:
            ref[...] = jnp.zeros_like(ref)

    barrier = pltpu.get_barrier_semaphore()
    pl.semaphore_signal(barrier, inc=1, device_id=partner, device_id_type=MESH)
    count = jnp.int32(1)
    for dx, dy in TO_NEXT:
        count = count + exists(dx, dy).astype(jnp.int32)

        @pl.when(exists(dx, dy))
        def _():
            pl.semaphore_signal(barrier, inc=1, device_id=(grid, ga + dx, gb + dy), device_id_type=MESH)

    pos_s[...] = jnp.where(rows == 0, x0, jnp.where(rows == 1, y0, z0))

    def all_here():
        pl.semaphore_wait(barrier, count)

    def remote(src, dst, send, recv, target):
        return pltpu.make_async_remote_copy(
            src_ref=src, dst_ref=dst, send_sem=send, recv_sem=recv, device_id=target, device_id_type=MESH)

    def halo_copy(m, n):
        return remote(sends[m].at[n], recvs[m].at[n], hs.at[m, n], hr.at[m, n], device(grid, *TO_NEXT[m]))

    def lat_copy(n):
        return remote(lat_s.at[n], lat_r.at[n], bs.at[n], br.at[n], partner)

    def ini_copy():
        return remote(ini_s, ini_r, bs.at[STEPS], br.at[STEPS], partner)

    def del_copy(n):
        return remote(del_s.at[n], del_r.at[n], ds.at[n], dr.at[n], partner)

    def near_copy(g, m, n):
        return remote(delta_s[m].at[n], delta_r[m].at[n], ns.at[g, m, n], nr.at[m, n], device(g, *TO_NEXT[m]))

    def pos_copy(m):
        return remote(pos_s, pos_r.at[m], ps.at[m], pr.at[m], device(grid, *TO_NEXT[m]))

    def each(turn, fun):
        for m, (dx, dy) in enumerate(TO_NEXT):
            @pl.when(exists(turn * dx, turn * dy))
            def _():
                fun(m)

    def learn_places():
        each(-1, lambda m: pos_copy(m).wait_recv())
        cp = pltpu.make_async_copy(pos_r, place_of, lsem.at[6])
        cp.start()
        cp.wait()

    def row_in(low, u):
        return (rows + 8 * u >= low) & (rows + 8 * u < low + 8)

    def lane_in(low, v):
        return (lanes + 128 * v >= low) & (lanes + 128 * v < low + 128)

    def tile_at(u, v):
        return (slice(8 * u, 8 * u + 8), slice(128 * v, 128 * v + 128))

    @pl.when(coarse)
    def _():
        flag_x = jnp.where(ga > 0, 1.0, 0.0).astype(F32)
        flag_y = jnp.where(gb > 0, 1.0, 0.0).astype(F32)
        row_ok = [row_in(y0, u) for u in range(3)]
        lane_ok = [lane_in(z0, v) for v in range(3)]
        wide = lax.broadcasted_iota(jnp.int32, (24, 384), 0)
        plane = lax.broadcasted_iota(jnp.int32, (8, 384), 0)

        def cut(load, i):
            tile = jnp.zeros((8, 128), F32)
            for u in range(3):
                for v in range(3):
                    tile = jnp.where(row_ok[u] & lane_ok[v], load(x0 + i, *tile_at(u, v)), tile)
            return tile

        def cut_latest(n, e):
            for i in range(2):
                for c in range(3):
                    lat_s[n, c, i] = cut(lambda x, r, l: e[c, x, r, l], i)
            lat_copy(n).start()

        def place(n, e):
            def at_x(x, carry):
                s0 = jnp.where(x == x0, 1.0, 0.0).astype(F32)
                s1 = jnp.where(x == x0 + 1, 1.0, 0.0).astype(F32)
                for c in range(3):
                    tile = s0 * del_r[n, c, 0] + s1 * del_r[n, c, 1]
                    for u in range(3):
                        for v in range(3):
                            spot = (c, x) + tile_at(u, v)
                            e[spot] = e[spot] + jnp.where(row_ok[u] & lane_ok[v], tile, 0.0)
                return carry

            lax.fori_loop(0, 6, at_x, 0)

        def pack_halos(n, e, h):
            for x in range(6):
                ye_s[n, 0, x:x + 1, :] = e[0, x, 0:1, :]
                ye_s[n, 1, x:x + 1, :] = e[2, x, 0:1, :]
                for c in range(3):
                    pk[c, x:x + 1, :] = e[c, x, 23:24, :]
                pk[3, x:x + 1, :] = h[0, x + 1, 31:32, :]
                pk[4, x:x + 1, :] = h[2, x + 1, 31:32, :]
            xe_s[n] = e[1:3, 0, 0:24, :]
            ex, ey, ez = e[0, 5, 0:24, :], e[1, 5, 0:24, :], e[2, 5, 0:24, :]
            exy = jnp.where(wide == 23, 0.0, e[0, 5, 1:25, :])
            xg_s[n, 0] = h[1, 6, 8:32, :] - 0.5 * (zfwd(ex) - ex + ez)
            xg_s[n, 1] = h[2, 6, 8:32, :] + 0.5 * (ey + exy - ex)
            px, py, pz = pk[0, 0:8, :], pk[1, 0:8, :], pk[2, 0:8, :]
            yg_s[n, 0] = pk[3, 0:8, :] + 0.5 * (pz + zfwd(py) - py)
            yg_s[n, 1] = pk[4, 0:8, :] - 0.5 * (pk[1, 1:9, :] - py + px)
            c1_s[n] = jnp.broadcast_to(e[0, 5, 0:1, :], (8, 384))
            c2_s[n] = jnp.broadcast_to(e[1, 0, 23:24, :], (8, 384))

        def send_halos(n):
            each(1, lambda m: halo_copy(m, n).start())

        def put_halos(n, e, h):
            e[1:3, 6, 0:24, :] = xe_r[n]
            h[1, 0, 8:32, :] = flag_x * (xg_r[n, 0] + 0.5 * e[2, 0, 0:24, :])
            corner = jnp.where(wide == 23, jnp.broadcast_to(c1_r[n, 0:1, :], (24, 384)), 0.0)
            h[2, 0, 8:32, :] = flag_x * (xg_r[n, 1] - 0.5 * (e[1, 0, 0:24, :] - corner))
            for x in range(6):
                own[0, x:x + 1, :] = e[0, x, 0:1, :]
                own[1, x:x + 1, :] = e[2, x, 0:1, :]
            pln[0] = flag_y * (yg_r[n, 0] - 0.5 * own[1])
            pln[1] = flag_y * (yg_r[n, 1] + 0.5 * (own[0] - jnp.where(plane == 5, c2_r[n], 0.0)))
            for x in range(6):
                e[0, x, 24:25, :] = ye_r[n, 0, x:x + 1, :]
                e[2, x, 24:25, :] = ye_r[n, 1, x:x + 1, :]
                h[0, x + 1, 7:8, :] = pln[0, x:x + 1, :]
                h[2, x + 1, 7:8, :] = pln[1, x:x + 1, :]

        def mend_halos(n):
            d = n - 1
            each(-1, lambda m: near_copy(0, m, d).wait_recv())
            for u in range(3):
                for v in range(3):
                    spot = tile_at(u, v)
                    ok = row_in(place_of[XE, 1, 0], u) & lane_in(place_of[XE, 2, 0], v)
                    for q in range(2):
                        xe_r[(n, q) + spot] = xe_r[(n, q) + spot] + jnp.where(ok, nx_r[0, d, 1 + q], 0.0)
                    ok = row_in(place_of[XG, 1, 0], u) & lane_in(place_of[XG, 2, 0], v)
                    for c in range(3):
                        dl[(c,) + spot] = jnp.where(ok, nx_r[1, d, c], 0.0)
            tx, ty, tz = dl[0, 0:24, :], dl[1, 0:24, :], dl[2, 0:24, :]
            dl[0, 24:32, :] = jnp.zeros((8, 384), F32)
            xg_r[n, 0] = xg_r[n, 0] - 0.5 * (zfwd(tx) - tx + tz)
            xg_r[n, 1] = xg_r[n, 1] + 0.5 * (ty + dl[0, 1:25, :] - tx)
            for m, keep in ((YE, ny_r.at[0]), (YG, ny_r.at[1])):
                at = place_of[m, 0, 0]
                for c in range(3):
                    two = [jnp.broadcast_to(keep[d, 2 * c + i:2 * c + i + 1, :], (8, 128)) for i in range(2)]
                    both = jnp.where(rows == at, two[0], jnp.where(rows == at + 1, two[1], 0.0))
                    for v in range(3):
                        pd[c, :, 128 * v:128 * v + 128] = jnp.where(lane_in(place_of[m, 2, 0], v), both, 0.0)
                if m == YE:
                    ye_r[n, 0] = ye_r[n, 0] + pd[0]
                    ye_r[n, 1] = ye_r[n, 1] + pd[2]
                else:
                    yg_r[n, 0] = yg_r[n, 0] + 0.5 * (pd[2] + zfwd(pd[1]) - pd[1])
                    yg_r[n, 1] = yg_r[n, 1] - 0.5 * (pltpu.roll(pd[1], 7, 0) - pd[1] + pd[0])
            for m, ref, keep in ((C1, c1_r, nd_r.at[0]), (C2, c2_r, nd_r.at[1])):
                for v in range(3):
                    spot = (n, slice(0, 8), slice(128 * v, 128 * v + 128))
                    ref[spot] = ref[spot] + jnp.where(lane_in(place_of[m, 2, 0], v), keep[d], 0.0)

        def update(e, h, p, ed, hd, pd_):
            def at_x(x, carry):
                for u in range(3):
                    r = slice(8 * u, 8 * u + 8)
                    ra = slice(8 * u + 1, 8 * u + 9)
                    rh = slice(8 * u + 8, 8 * u + 16)
                    rb = slice(8 * u + 7, 8 * u + 15)
                    ex, ey, ez = e[0, x, r, :], e[1, x, r, :], e[2, x, r, :]
                    hx = h[0, x + 1, rh, :] - 0.5 * ((e[2, x, ra, :] - ez) - (zfwd(ey) - ey))
                    hy = h[1, x + 1, rh, :] - 0.5 * ((zfwd(ex) - ex) - (e[2, x + 1, r, :] - ez))
                    hz = h[2, x + 1, rh, :] - 0.5 * ((e[1, x + 1, r, :] - ey) - (e[0, x, ra, :] - ex))
                    hd[0, x + 1, rh, :] = hx
                    hd[1, x + 1, rh, :] = hy
                    hd[2, x + 1, rh, :] = hz
                    cx = (hz - hd[2, x + 1, rb, :]) - (hy - zbwd(hy))
                    cy = (hx - zbwd(hx)) - (hz - hd[2, x, rh, :])
                    cz = (hy - hd[1, x, rh, :]) - (hx - hd[0, x + 1, rb, :])
                    ka, kc, kb, kf, kg = (k[q, x, r, :] for q in range(5))
                    for c, (old, curl) in enumerate(((ex, cx), (ey, cy), (ez, cz))):
                        pol = p[c, x, r, :]
                        new = ka * old + kc * curl + kb * pol
                        ed[c, x, r, :] = new
                        if pd_ is not None:
                            pd_[c, x, r, :] = kf * pol + kg * new
                return carry

            lax.fori_loop(0, 6, at_x, 0, unroll=True)

        sets = [(e2.at[q], h2.at[q], p2.at[q]) for q in range(2)]
        e_in.wait()
        h_in.wait()
        pack_halos(0, sets[0][0], sets[0][1])
        all_here()
        send_halos(0)
        each(1, lambda m: pos_copy(m).start())
        for cp in m_in:
            cp.wait()
        tabs = tables(permit, conduct, relax, debye, 1.0, 0.5)

        def factors(x, carry):
            for u in range(3):
                for v in range(3):
                    here = mat[v, x, 8 * u:8 * u + 8, :]
                    for q in range(5):
                        k[(q, x) + tile_at(u, v)] = pick(tabs[q], here)
            return carry

        lax.fori_loop(0, 6, factors, 0)
        for i in range(2):
            for c in range(3):
                ini_s[c, i] = cut(lambda x, r, l: e2[0, c, x, r, l], i)
            for q in range(2):
                ini_s[3 + q, i] = cut(lambda x, r, l: k[q, x, r, l], i)
        ini_copy().start()
        p_in.wait()
        for n in range(STEPS):
            now, then = sets[n % 2], sets[(n + 1) % 2]
            each(-1, lambda m: halo_copy(m, n).wait_recv())
            if n == 0:
                put_halos(n, now[0], then[1])
                update(*now, *then)
                cut_latest(0, then[0])
                learn_places()
            else:
                put_halos(n, now[0], then[1])
                update(*now, then[0], then[1], None)
                cut_latest(n, then[0])
                del_copy(n - 1).wait_recv()
                place(n - 1, now[0])
                mend_halos(n)
                put_halos(n, now[0], then[1])
                update(*now, *then)
            if n + 1 < STEPS:
                pack_halos(n + 1, then[0], then[1])
                send_halos(n + 1)
        e, h, p = sets[STEPS % 2]
        h_out = pltpu.make_async_copy(h.at[:, 1:7, 8:32, :], out.at[0, 3:6], lsem.at[1])
        p_out = pltpu.make_async_copy(p, out.at[0, 6:9], lsem.at[2])
        h_out.start()
        p_out.start()
        del_copy(STEPS - 1).wait_recv()
        place(STEPS - 1, e)
        e_out = pltpu.make_async_copy(e.at[:, 0:6, 0:24, :], out.at[0, 0:3], lsem.at[0])
        e_out.start()

        each(1, lambda m: pos_copy(m).wait_send())
        for n in range(STEPS):
            each(1, lambda m: halo_copy(m, n).wait_send())
            lat_copy(n).wait_send()
        ini_copy().wait_send()
        h_out.wait()
        p_out.wait()
        e_out.wait()

    @pl.when(jnp.logical_not(coarse))
    def _():
        none = jnp.zeros((8, 128), jnp.int32)
        inside = (rows < ly) & (lanes < lz)
        two = lx == 2

        def inside_x(x):
            return jnp.where((x < 3) | two, 1, 0).astype(jnp.int32)

        tabs = tables(permit, conduct, relax, debye, 1.0 / 3.0, 0.25)
        spread = [3 * lanes + r for r in range(3)]
        phase = lanes % 3
        source = [(128 * ((phase + 3 - r) % 3) + lanes) // 3 for r in range(3)]

        def gather_in(ref, lead, ry):
            parts = [ref[(v,) + lead + (pl.ds(ry, 8, stride=3), slice(None))] for v in range(3)]
            tiles = []
            for r in range(3):
                at, src = spread[r] & 127, spread[r] >> 7
                got = [pick(part, at) for part in parts]
                tiles.append(jnp.where(src == 0, got[0], jnp.where(src == 1, got[1], got[2])))
            return tiles

        for cp in m_in:
            cp.wait()

        def fine_factors(x, carry):
            ok = inside & (inside_x(x) + none > 0)
            for ry in range(3):
                for r, here in enumerate(gather_in(mat, (x,), ry)):
                    ka, kc, kb, kf, kg = (pick(tabs[q], here) for q in range(5))
                    t = 3 * ry + r
                    fk[0, x, t] = ka
                    fk[1, x, t] = jnp.where(ok, kc, 0.0)
                    fk[2, x, t] = jnp.where(ok, kb * kg, 0.0)
                    fk[3, x, t] = kf
                    fk[4, x, t] = kg
                    fkr[x, t] = 1.0 / kg
            return carry

        lax.fori_loop(0, 6, fine_factors, 0)
        all_here()
        each(1, lambda m: pos_copy(m).start())
        for cp in f_in:
            cp.wait()
        for c in range(3):
            ff[c, 6] = jnp.zeros((9, 8, 128), F32)
            ff[3 + c, 0] = jnp.zeros((9, 8, 128), F32)

        def load_fine(x, carry):
            ok = inside & (inside_x(x) + none > 0)
            for c in range(9):
                for ry in range(3):
                    for r, here in enumerate(gather_in(stage, (c, x), ry)):
                        t = 3 * ry + r
                        if 3 <= c < 6:
                            ff[c, x + 1, t] = jnp.where(ok, 2.0 * here, 0.0)
                        elif c < 3:
                            ff[c, x, t] = jnp.where(ok, here, 0.0)
                        else:
                            ff[c, x, t] = jnp.where(ok, here * fkr[x, t], 0.0)
            return carry

        lax.fori_loop(0, 6, load_fine, 0)

        back_y, back_z = (8 - y0 % 8) % 8, (128 - z0 % 128) % 128

        def to_box(tile):
            return pltpu.roll(pltpu.roll(tile, back_y, 0), back_z, 1)

        def from_box(tile):
            return pltpu.roll(pltpu.roll(tile, y0 % 8, 0), z0 % 128, 1)

        edge_y = {0: rows == 0, 2: rows == ly - 1}
        edge_z = {0: lanes == 0, 2: lanes == lz - 1}

        def at_layer(x, carry):
            ok = inside & (inside_x(x) + none > 0)
            edge = jnp.where((x == 0) | (x == 3 * lx - 1), 1, 0).astype(jnp.int32)
            edge_x = ok & (edge + none > 0)
            ok_y = {q: m & ok for q, m in edge_y.items()}
            ok_z = {q: m & ok for q, m in edge_z.items()}
            xc = x // 3
            tiles = [(ry, rz) for ry in range(3) for rz in range(3)]
            E = {(c, t): ff[c, x, t] for c in range(3) for t in range(9)}
            F = {(c, t): ff[c, x + 1, t] for c in (1, 2) for t in range(9)}
            H = {}
            for ry, rz in tiles:
                t = 3 * ry + rz
                ex, ey, ez = (E[c, t] for c in range(3))
                if ry < 2:
                    exy, ezy = E[0, t + 3], E[2, t + 3]
                else:
                    exy, ezy = yfwd(E[0, rz]), yfwd(E[2, rz])
                if rz < 2:
                    exz, eyz = E[0, t + 1], E[1, t + 1]
                else:
                    exz, eyz = zfwd(E[0, 3 * ry]), zfwd(E[1, 3 * ry])
                H[0, t] = ff[3, x + 1, t] - ((ezy - ez) - (eyz - ey))
                H[1, t] = ff[4, x + 1, t] - ((exz - ex) - (F[2, t] - ez))
                H[2, t] = ff[5, x + 1, t] - ((F[1, t] - ey) - (exy - ex))
                for c in range(3):
                    ff[3 + c, x + 1, t] = H[c, t]
            for ry, rz in tiles:
                t = 3 * ry + rz
                hx, hy, hz = (H[c, t] for c in range(3))
                if ry > 0:
                    hxy, hzy = H[0, t - 3], H[2, t - 3]
                else:
                    hxy, hzy = ybwd(H[0, 6 + rz]), ybwd(H[2, 6 + rz])
                if rz > 0:
                    hxz, hyz = H[0, t - 1], H[1, t - 1]
                else:
                    hxz, hyz = zbwd(H[0, 3 * ry + 2]), zbwd(H[1, 3 * ry + 2])
                hyx, hzx = ff[4, x, t], ff[5, x, t]
                curls = ((hz - hzy) - (hy - hyz), (hx - hxz) - (hz - hzx), (hy - hyx) - (hx - hxy))
                ka, kc, kb, kf = (fk[q, x, t] for q in range(4))
                for c in range(3):
                    pol = ff[6 + c, x, t]
                    new = ka * E[c, t] + kc * curls[c] + kb * pol
                    marks = []
                    if c != 0:
                        marks.append(edge_x)
                    if c != 1 and ry in ok_y:
                        marks.append(ok_y[ry])
                    if c != 2 and rz in ok_z:
                        marks.append(ok_z[rz])
                    if marks:
                        new = jnp.where(functools.reduce(jnp.logical_or, marks), drv[c, xc], new)
                    ff[c, x, t] = new
                    ff[6 + c, x, t] = kf * pol + new
            return carry

        wrows = lax.broadcasted_iota(jnp.int32, (16, 256), 0)
        wlanes = lax.broadcasted_iota(jnp.int32, (16, 256), 1)
        at_y = y0 - 4 + ((wrows - (y0 - 4)) & 15)
        at_z = z0 - 64 + ((wlanes - (z0 - 64)) & 255)

        def w_in(at, low, size):
            return (at >= low) & (at < low + size)

        def twice(tile):
            return jnp.concatenate([jnp.concatenate([tile, tile], axis=1)] * 2, axis=0)

        def as_int(flag):
            return jnp.where(flag, 1, 0).astype(jnp.int32)

        def correction(n):
            each(-1, lambda m: near_copy(1, m, n - 1).wait_recv())
            d = n - 1
            region = w_in(at_y, y0, 8) & w_in(at_z, z0, 128)
            wide_none = jnp.zeros((16, 256), jnp.int32)
            w = {}
            for c in range(3):
                for xr in range(-1, 3):
                    w[c, xr] = jnp.where(region, twice(del_s[d, c, xr]), 0.0) if 0 <= xr < 2 else jnp.zeros((16, 256), F32)
            for m, xr, at_edge in ((XE, 2, x0 == 4), (XG, -1, x0 == 0)):
                ok = w_in(at_y, place_of[m, 1, 0], 8) & w_in(at_z, place_of[m, 2, 0], 128)
                ok = ok & (as_int(at_edge) + wide_none > 0)
                for c in range(3):
                    w[c, xr] = w[c, xr] + jnp.where(ok, twice(nx_r[m // 2, d, c]), 0.0)
            for m, y in ((YE, 24), (YG, -1)):
                ok = (at_y == y) & w_in(at_z, place_of[m, 2, 0], 128)
                for c in range(3):
                    two_rows = [ny_r[m // 2, d, 2 * c + i:2 * c + i + 1, :] for i in range(2)]
                    for xr in range(-1, 3):
                        i = x0 + xr - place_of[m, 0, 0]
                        s0 = jnp.where(i == 0, 1.0, 0.0).astype(F32)
                        s1 = jnp.where(i == 1, 1.0, 0.0).astype(F32)
                        row = jnp.broadcast_to(s0 * two_rows[0] + s1 * two_rows[1], (8, 128))
                        w[c, xr] = w[c, xr] + jnp.where(ok, twice(row), 0.0)
            for m, c, xr, y, at_edge in ((C1, 0, -1, 24, x0 == 0), (C2, 1, 2, -1, x0 == 4)):
                ok = (at_y == y) & w_in(at_z, place_of[m, 2, 0], 128) & (as_int(at_edge) + wide_none > 0)
                w[c, xr] = w[c, xr] + jnp.where(ok, twice(nd_r[m - 4, d]), 0.0)

            def up_y(a):
                return pltpu.roll(a, 15, 0)

            def up_z(a):
                return pltpu.roll(a, 255, 1)

            def down_y(a):
                return pltpu.roll(a, 1, 0)

            def down_z(a):
                return pltpu.roll(a, 1, 1)

            held = (at_z >= 0) & (at_y + 24 * gb >= 0)
            hh = {}
            for xr in range(-1, 2):
                ok = held & (as_int(x0 + xr + 6 * ga >= 0) + wide_none > 0)
                ex, ey, ez = (w[c, xr] for c in range(3))
                moved = ((up_y(ez) - ez) - (up_z(ey) - ey), (up_z(ex) - ex) - (w[2, xr + 1] - ez),
                         (w[1, xr + 1] - ey) - (up_y(ex) - ex))
                for c in range(3):
                    hh[c, xr] = jnp.where(ok, -0.5 * moved[c], 0.0)
            for xr in range(2):
                hx, hy, hz = (hh[c, xr] for c in range(3))
                curls = ((hz - down_y(hz)) - (hy - down_z(hy)), (hx - down_z(hx)) - (hz - hh[2, xr - 1]),
                         (hy - hh[1, xr - 1]) - (hx - down_y(hx)))
                for c in range(3):
                    kept = jnp.where(region, curls[c], 0.0)
                    tile = (kept[0:8, 0:128] + kept[0:8, 128:256]) + (kept[8:16, 0:128] + kept[8:16, 128:256])
                    ear[1, c, xr] = to_box(lat_r[n, c, xr] + ini_r[3, xr] * del_s[d, c, xr] + ini_r[4, xr] * tile)

        learn_places()
        ini_copy().wait_recv()
        for c in range(3):
            for i in range(2):
                ear[0, c, i] = to_box(ini_r[c, i])

        for n in range(STEPS):
            lat_copy(n).wait_recv()
            if n == 0:
                for c in range(3):
                    for i in range(2):
                        ear[1, c, i] = to_box(lat_r[0, c, i])
            else:
                correction(n)

            def substep(s, carry):
                weight = (s + 1).astype(F32) * (1.0 / 3.0)
                drv[...] = ear[0] + weight * (ear[1] - ear[0])
                return lax.fori_loop(0, 6, at_layer, carry, unroll=True)

            lax.fori_loop(0, 3, substep, 0)
            for i in range(2):
                ok = inside & (inside_x(3 * i) + none > 0)
                for c in range(3):
                    total = functools.reduce(
                        jnp.add, [ff[c, 3 * i + j, t] for j in range(3) for t in range(9)])
                    latest = ear[1, c, i]
                    delta = jnp.where(ok, total * (1.0 / 27.0) - latest, 0.0)
                    ear[0, c, i] = latest + delta
                    del_s[n, c, i] = from_box(delta)
            if n + 1 < STEPS:
                low, high = (jnp.where(x0 == q, 1.0, 0.0).astype(F32) for q in (0, 4))
                left, right = (jnp.where(y0 == q, 1.0, 0.0).astype(F32) for q in (0, 16))
                for c in range(3):
                    nx_s[0, n, c] = low * del_s[n, c, 0]
                    nx_s[1, n, c] = high * del_s[n, c, 1]
                    for i in range(2):
                        ny_s[0, n, 2 * c + i:2 * c + i + 1, :] = left * del_s[n, c, i, 0:1, :]
                        ny_s[1, n, 2 * c + i:2 * c + i + 1, :] = right * del_s[n, c, i, 7:8, :]
                for q in range(2):
                    ny_s[q, n, 6:8, :] = jnp.zeros((2, 128), F32)
                nd_s[0, n] = jnp.broadcast_to((high * left) * del_s[n, 0, 1, 0:1, :], (8, 128))
                nd_s[1, n] = jnp.broadcast_to((low * right) * del_s[n, 1, 0, 7:8, :], (8, 128))
                each(1, lambda m: near_copy(1, m, n).start())
                del_copy(n).start()
                each(1, lambda m: near_copy(0, m, n).start())
            else:
                del_copy(n).start()

        def save_fine(x, carry):
            for c in range(9):
                for ry in range(3):
                    lift = 1 if 3 <= c < 6 else 0
                    parts = [ff[c, x + lift, 3 * ry + r] for r in range(3)]
                    if c >= 6:
                        parts = [part * fk[4, x, 3 * ry + r] for r, part in enumerate(parts)]
                    got = [pick(part, source[r]) for r, part in enumerate(parts)]
                    for v in range(3):
                        a, b, d = (got[(q + 2 * v) % 3] for q in range(3))
                        value = jnp.where(phase == 0, a, jnp.where(phase == 1, b, d))
                        if lift:
                            value = 0.5 * value
                        stage[v, c, x, pl.ds(ry, 8, stride=3), :] = value
            return carry

        lax.fori_loop(0, 6, save_fine, 0)
        f_out = [pltpu.make_async_copy(stage.at[v], out.at[0, :, :, :, pl.ds(128 * v, 128)], lsem.at[v]) for v in range(3)]
        for cp in f_out:
            cp.start()
        each(1, lambda m: pos_copy(m).wait_send())
        for n in range(STEPS):
            del_copy(n).wait_send()
            if n + 1 < STEPS:
                for g in range(2):
                    each(1, lambda m: near_copy(g, m, n).wait_send())
        for cp in f_out:
            cp.wait()


def solution(mesh):
    nx, ny = mesh.shape["gx"], mesh.shape["gy"]

    def body(fields, material, permit, conduct, relax, debye, subgrids):
        vm = pltpu.VMEM
        dma = pltpu.SemaphoreType.DMA
        slots = [
            vm((STEPS, 2, 24, 384), F32), vm((STEPS, 2, 8, 384), F32),
            vm((STEPS, 2, 24, 384), F32), vm((STEPS, 2, 8, 384), F32),
            vm((STEPS, 8, 384), F32), vm((STEPS, 8, 384), F32),
        ]
        region = (3, 2, 8, 128)
        near = [vm((2, STEPS - 1, 3, 8, 128), F32), vm((2, STEPS - 1, 8, 128), F32), vm((2, STEPS - 1, 8, 128), F32)]
        return pl.pallas_call(
            functools.partial(kernel, nx, ny),
            out_shape=jax.ShapeDtypeStruct(fields.shape, F32),
            in_specs=[pl.BlockSpec(memory_space=pl.ANY)] * 2 + [pl.BlockSpec(memory_space=pltpu.SMEM)] * 5,
            out_specs=pl.BlockSpec(memory_space=pl.ANY),
            scratch_shapes=[
                vm((2, 3, 7, 32, 384), F32), vm((2, 3, 7, 32, 384), F32), vm((2, 3, 6, 24, 384), F32), vm((5, 6, 24, 384), F32),
                vm((3, 9, 6, 24, 128), F32), vm((3, 6, 24, 128), jnp.int32),
                vm((9, 7, 9, 8, 128), F32), vm((5, 6, 9, 8, 128), F32),
                vm((5, 16, 384), F32), vm((2, 8, 384), F32), vm((2, 8, 384), F32), vm((3, 32, 384), F32), vm((3, 8, 384), F32),
                vm((2,) + region, F32), vm(region, F32), vm((6, 9, 8, 128), F32),
                *slots, *slots,
                vm((STEPS,) + region, F32), vm((STEPS,) + region, F32), vm((5, 2, 8, 128), F32), vm((5, 2, 8, 128), F32),
                vm((STEPS,) + region, F32), vm((STEPS,) + region, F32),
                *near, *near, vm((8, 128), jnp.int32), vm((6, 8, 128), jnp.int32), pltpu.SMEM((6, 8, 128), jnp.int32),
                dma((7,)), dma((6, STEPS)), dma((6, STEPS)),
                dma((STEPS + 1,)), dma((STEPS + 1,)), dma((STEPS,)), dma((STEPS,)),
                dma((2, 6, STEPS)), dma((6, STEPS)), dma((6,)), dma((6,)),
            ],
            compiler_params=pltpu.CompilerParams(
                collective_id=0, has_side_effects=True, vmem_limit_bytes=63 * 1024 * 1024),
        )(fields, material, permit, conduct, relax, debye, subgrids)

    return jax.shard_map(
        body,
        mesh=mesh,
        in_specs=(P("grid", None, "gx", "gy", None), P("grid", "gx", "gy", None), P(), P(), P(), P(), P("gx", "gy", None)),
        out_specs=P("grid", None, "gx", "gy", None),
        check_vma=False,
    )
```

```python
import functools

import jax
import jax.numpy as jnp
from jax import lax
from jax.experimental import pallas as pl
from jax.experimental.pallas import tpu as pltpu
from jax.sharding import PartitionSpec as P

MESH = pl.DeviceIdType.MESH
STEPS = 3
F32 = jnp.float32

TO_NEXT = ((-1, 0), (0, -1), (1, 0), (0, 1), (1, -1), (-1, 1))
XE, YE, XG, YG, C1, C2 = range(6)
AROUND = TO_NEXT + ((1, 1), (-1, -1))
SETS = STEPS + 1


def lane_iota():
    return lax.broadcasted_iota(jnp.int32, (8, 128), 1)


def row_iota():
    return lax.broadcasted_iota(jnp.int32, (8, 128), 0)


def pick(tile, index):
    return jnp.take_along_axis(tile, index, axis=1, mode="promise_in_bounds")


def zfwd(v):
    n = v.shape[-1]
    lanes = lax.broadcasted_iota(jnp.int32, v.shape, v.ndim - 1)
    return jnp.where(lanes == n - 1, 0.0, pltpu.roll(v, n - 1, v.ndim - 1))


def zbwd(v):
    lanes = lax.broadcasted_iota(jnp.int32, v.shape, v.ndim - 1)
    return jnp.where(lanes == 0, 0.0, pltpu.roll(v, 1, v.ndim - 1))


def yfwd(t):
    return jnp.where(row_iota() == 7, 0.0, pltpu.roll(t, 7, 0))


def ybwd(t):
    return jnp.where(row_iota() == 0, 0.0, pltpu.roll(t, 1, 0))


def tables(permit, conduct, relax, debye, factor, courant):
    lane = lane_iota()

    def spread(ref):
        out = jnp.ones((8, 128), F32)
        for m in range(8):
            out = jnp.where(lane == m, ref[m], out)
        return out

    eps = spread(permit)
    damping = spread(conduct) * factor / (2.0 * eps)
    f0 = (1.0 - damping) / (1.0 + damping)
    f1 = 1.0 / (eps * (1.0 + damping))
    f2 = spread(relax) * factor
    f3 = jnp.exp(-f2)
    f4 = spread(debye)
    return f0 - f1 * f2 * f4, courant * f1, f1 * f2, f3, (1.0 - f3) * f4


def kernel(
    nx, ny,
    fields, material, permit, conduct, relax, debye, subgrids, out,
    e2, h2, p2, k, stage, mat, ff, fk, pk, pln, own, dl, pd, ear, drv, fkr, mext, ew, hw, kw,
    xe_s, ye_s, xg_s, yg_s, c1_s, c2_s,
    xe_r, ye_r, xg_r, yg_r, c1_r, c2_r,
    lat_s, lat_r, ini_s, ini_r, del_s, del_r,
    nx_s, ny_s, nd_s, nx_r, ny_r, nd_r, pos_s, pos_r, place_of,
    fy_s, fx_r, fy_r, my_s, mx_r, my_r, wm_s, wm_r,
    lsem, hs, hr, bs, br, ds, dr, ns, nr, ps, pr, fs, fr, ms, mr, ws, wr,
):
    grid = lax.axis_index("grid")
    ga = lax.axis_index("gx")
    gb = lax.axis_index("gy")
    coarse = grid == 0
    x0, y0, z0 = subgrids[0, 0, 0], subgrids[0, 0, 1], subgrids[0, 0, 2]
    lx, ly, lz = subgrids[0, 0, 3], subgrids[0, 0, 4], subgrids[0, 0, 5]
    sends = (xe_s, ye_s, xg_s, yg_s, c1_s, c2_s)
    recvs = (xe_r, ye_r, xg_r, yg_r, c1_r, c2_r)
    delta_s = (nx_s.at[0], ny_s.at[0], nx_s.at[1], ny_s.at[1], nd_s.at[0], nd_s.at[1])
    delta_r = (nx_r.at[0], ny_r.at[0], nx_r.at[1], ny_r.at[1], nd_r.at[0], nd_r.at[1])

    def exists(dx, dy):
        return (ga + dx >= 0) & (ga + dx < nx) & (gb + dy >= 0) & (gb + dy < ny)

    def device(g, dx, dy):
        return (g, jnp.clip(ga + dx, 0, nx - 1), jnp.clip(gb + dy, 0, ny - 1))

    partner = (1 - grid, ga, gb)
    rows, lanes = row_iota(), lane_iota()

    e_in = pltpu.make_async_copy(fields.at[0, 0:3], e2.at[0, :, 0:6, 0:24, :], lsem.at[0])
    h_in = pltpu.make_async_copy(fields.at[0, 3:6], h2.at[0, :, 1:7, 8:32, :], lsem.at[1])
    p_in = pltpu.make_async_copy(fields.at[0, 6:9], p2.at[0], lsem.at[2])
    f_in = [pltpu.make_async_copy(fields.at[0, :, :, :, pl.ds(128 * v, 128)], stage.at[v], lsem.at[v]) for v in range(3)]
    m_in = [pltpu.make_async_copy(material.at[0, :, :, pl.ds(128 * v, 128)], mat.at[v], lsem.at[3 + v]) for v in range(3)]

    @pl.when(coarse)
    def _():
        for cp in (e_in, h_in, p_in):
            cp.start()

    @pl.when(jnp.logical_not(coarse))
    def _():
        for cp in f_in:
            cp.start()

    for cp in m_in:
        cp.start()
    for ref in (nx_r, ny_r, nd_r, pos_r, fx_r, fy_r):
        ref[...] = jnp.zeros_like(ref)

    @pl.when(coarse)
    def _():
        for ref in (ye_s, yg_s, pk, pln, own, mx_r, my_r, my_s, mext) + recvs:
            ref[...] = jnp.zeros_like(ref)

    barrier = pltpu.get_barrier_semaphore()
    pl.semaphore_signal(barrier, inc=1, device_id=partner, device_id_type=MESH)
    count = jnp.int32(1)
    for dx, dy in AROUND:
        count = count + exists(dx, dy).astype(jnp.int32)

        @pl.when(exists(dx, dy))
        def _():
            pl.semaphore_signal(barrier, inc=1, device_id=(grid, ga + dx, gb + dy), device_id_type=MESH)

    pos_s[...] = jnp.where(rows == 0, x0, jnp.where(rows == 1, y0, z0))

    def all_here():
        pl.semaphore_wait(barrier, count)

    def remote(src, dst, send, recv, target):
        return pltpu.make_async_remote_copy(
            src_ref=src, dst_ref=dst, send_sem=send, recv_sem=recv, device_id=target, device_id_type=MESH)

    def halo_copy(m, n):
        return remote(sends[m].at[n], recvs[m].at[n], hs.at[m, n], hr.at[m, n], device(grid, *TO_NEXT[m]))

    def lat_copy(n):
        return remote(lat_s.at[n], lat_r.at[n], bs.at[n], br.at[n], partner)

    def ini_copy():
        return remote(ini_s, ini_r, bs.at[STEPS], br.at[STEPS], partner)

    def del_copy(n):
        return remote(del_s.at[n], del_r.at[n], ds.at[n], dr.at[n], partner)

    def near_copy(m, n):
        return remote(delta_s[m].at[n], delta_r[m].at[n], ns.at[m, n], nr.at[m, n], device(0, *TO_NEXT[m]))

    def box_copy(m, n):
        dx, dy = AROUND[m]
        if dy == 0:
            src, dst = del_s.at[n], fx_r.at[m // 2, n]
        else:
            src, dst = fy_s.at[0 if dy < 0 else 1, n], fy_r.at[m, n]
        return remote(src, dst, fs.at[m, n], fr.at[m, n], device(1, dx, dy))

    def pos_copy(m):
        return remote(pos_s, pos_r.at[m], ps.at[m], pr.at[m], device(grid, *AROUND[m]))

    def mat_copy(m):
        dx, dy = TO_NEXT[m]
        if dy == 0:
            src, dst = mat.at[:, 0 if dx < 0 else 5], mx_r.at[m // 2]
        else:
            src, dst = my_s.at[m], my_r.at[m]
        return remote(src, dst, ms.at[m], mr.at[m], device(0, dx, dy))

    def win_copy():
        return remote(wm_s, wm_r, ws.at[0], wr.at[0], partner)

    def each(turn, fun, over=TO_NEXT):
        for m, (dx, dy) in enumerate(over):
            @pl.when(exists(turn * dx, turn * dy))
            def _():
                fun(m)

    def learn_places():
        each(-1, lambda m: pos_copy(m).wait_recv(), AROUND)
        cp = pltpu.make_async_copy(pos_r, place_of, lsem.at[6])
        cp.start()
        cp.wait()

    def row_in(low, u):
        return (rows + 8 * u >= low) & (rows + 8 * u < low + 8)

    def lane_in(low, v):
        return (lanes + 128 * v >= low) & (lanes + 128 * v < low + 128)

    def tile_at(u, v):
        return (slice(8 * u, 8 * u + 8), slice(128 * v, 128 * v + 128))

    @pl.when(coarse)
    def _():
        flag_x = jnp.where(ga > 0, 1.0, 0.0).astype(F32)
        flag_y = jnp.where(gb > 0, 1.0, 0.0).astype(F32)
        row_ok = [row_in(y0, u) for u in range(3)]
        lane_ok = [lane_in(z0, v) for v in range(3)]
        wide = lax.broadcasted_iota(jnp.int32, (24, 384), 0)
        plane = lax.broadcasted_iota(jnp.int32, (8, 384), 0)

        def cut(load, i):
            tile = jnp.zeros((8, 128), F32)
            for u in range(3):
                for v in range(3):
                    tile = jnp.where(row_ok[u] & lane_ok[v], load(x0 + i, *tile_at(u, v)), tile)
            return tile

        def cut_latest(n, e):
            for i in range(2):
                for c in range(3):
                    lat_s[n, c, i] = cut(lambda x, r, l: e[c, x, r, l], i)
            lat_copy(n).start()

        def place(n, e):
            def at_x(x, carry):
                s0 = jnp.where(x == x0, 1.0, 0.0).astype(F32)
                s1 = jnp.where(x == x0 + 1, 1.0, 0.0).astype(F32)
                for c in range(3):
                    tile = s0 * del_r[n, c, 0] + s1 * del_r[n, c, 1]
                    for u in range(3):
                        for v in range(3):
                            spot = (c, x) + tile_at(u, v)
                            e[spot] = e[spot] + jnp.where(row_ok[u] & lane_ok[v], tile, 0.0)
                return carry

            lax.fori_loop(0, 6, at_x, 0)

        def pack_halos(n, e, h):
            for x in range(6):
                ye_s[n, 0, x:x + 1, :] = e[0, x, 0:1, :]
                ye_s[n, 1, x:x + 1, :] = e[2, x, 0:1, :]
                for c in range(3):
                    pk[c, x:x + 1, :] = e[c, x, 23:24, :]
                pk[3, x:x + 1, :] = h[0, x + 1, 31:32, :]
                pk[4, x:x + 1, :] = h[2, x + 1, 31:32, :]
            xe_s[n] = e[1:3, 0, 0:24, :]
            ex, ey, ez = e[0, 5, 0:24, :], e[1, 5, 0:24, :], e[2, 5, 0:24, :]
            exy = jnp.where(wide == 23, 0.0, e[0, 5, 1:25, :])
            xg_s[n, 0] = h[1, 6, 8:32, :] - 0.5 * (zfwd(ex) - ex + ez)
            xg_s[n, 1] = h[2, 6, 8:32, :] + 0.5 * (ey + exy - ex)
            px, py, pz = pk[0, 0:8, :], pk[1, 0:8, :], pk[2, 0:8, :]
            yg_s[n, 0] = pk[3, 0:8, :] + 0.5 * (pz + zfwd(py) - py)
            yg_s[n, 1] = pk[4, 0:8, :] - 0.5 * (pk[1, 1:9, :] - py + px)
            c1_s[n] = jnp.broadcast_to(e[0, 5, 0:1, :], (8, 384))
            c2_s[n] = jnp.broadcast_to(e[1, 0, 23:24, :], (8, 384))

        def send_halos(n):
            each(1, lambda m: halo_copy(m, n).start())

        def put_halos(n, e, h):
            e[1:3, 6, 0:24, :] = xe_r[n]
            h[1, 0, 8:32, :] = flag_x * (xg_r[n, 0] + 0.5 * e[2, 0, 0:24, :])
            corner = jnp.where(wide == 23, jnp.broadcast_to(c1_r[n, 0:1, :], (24, 384)), 0.0)
            h[2, 0, 8:32, :] = flag_x * (xg_r[n, 1] - 0.5 * (e[1, 0, 0:24, :] - corner))
            for x in range(6):
                own[0, x:x + 1, :] = e[0, x, 0:1, :]
                own[1, x:x + 1, :] = e[2, x, 0:1, :]
            pln[0] = flag_y * (yg_r[n, 0] - 0.5 * own[1])
            pln[1] = flag_y * (yg_r[n, 1] + 0.5 * (own[0] - jnp.where(plane == 5, c2_r[n], 0.0)))
            for x in range(6):
                e[0, x, 24:25, :] = ye_r[n, 0, x:x + 1, :]
                e[2, x, 24:25, :] = ye_r[n, 1, x:x + 1, :]
                h[0, x + 1, 7:8, :] = pln[0, x:x + 1, :]
                h[2, x + 1, 7:8, :] = pln[1, x:x + 1, :]

        def mend_halos(n, d):
            each(-1, lambda m: near_copy(m, d).wait_recv())
            for u in range(3):
                for v in range(3):
                    spot = tile_at(u, v)
                    ok = row_in(place_of[XE, 1, 0], u) & lane_in(place_of[XE, 2, 0], v)
                    for q in range(2):
                        xe_r[(n, q) + spot] = xe_r[(n, q) + spot] + jnp.where(ok, nx_r[0, d, 1 + q], 0.0)
                    ok = row_in(place_of[XG, 1, 0], u) & lane_in(place_of[XG, 2, 0], v)
                    for c in range(3):
                        dl[(c,) + spot] = jnp.where(ok, nx_r[1, d, c], 0.0)
            tx, ty, tz = dl[0, 0:24, :], dl[1, 0:24, :], dl[2, 0:24, :]
            dl[0, 24:32, :] = jnp.zeros((8, 384), F32)
            xg_r[n, 0] = xg_r[n, 0] - 0.5 * (zfwd(tx) - tx + tz)
            xg_r[n, 1] = xg_r[n, 1] + 0.5 * (ty + dl[0, 1:25, :] - tx)
            for m, keep in ((YE, ny_r.at[0]), (YG, ny_r.at[1])):
                at = place_of[m, 0, 0]
                for c in range(3):
                    two = [jnp.broadcast_to(keep[d, 2 * c + i:2 * c + i + 1, :], (8, 128)) for i in range(2)]
                    both = jnp.where(rows == at, two[0], jnp.where(rows == at + 1, two[1], 0.0))
                    for v in range(3):
                        pd[c, :, 128 * v:128 * v + 128] = jnp.where(lane_in(place_of[m, 2, 0], v), both, 0.0)
                if m == YE:
                    ye_r[n, 0] = ye_r[n, 0] + pd[0]
                    ye_r[n, 1] = ye_r[n, 1] + pd[2]
                else:
                    yg_r[n, 0] = yg_r[n, 0] + 0.5 * (pd[2] + zfwd(pd[1]) - pd[1])
                    yg_r[n, 1] = yg_r[n, 1] - 0.5 * (pltpu.roll(pd[1], 7, 0) - pd[1] + pd[0])
            for m, ref, keep in ((C1, c1_r, nd_r.at[0]), (C2, c2_r, nd_r.at[1])):
                for v in range(3):
                    spot = (n, slice(0, 8), slice(128 * v, 128 * v + 128))
                    ref[spot] = ref[spot] + jnp.where(lane_in(place_of[m, 2, 0], v), keep[d], 0.0)

        def update(e, h, p, ed, hd, pd_):
            def at_x(x, carry):
                for u in range(3):
                    r = slice(8 * u, 8 * u + 8)
                    ra = slice(8 * u + 1, 8 * u + 9)
                    rh = slice(8 * u + 8, 8 * u + 16)
                    rb = slice(8 * u + 7, 8 * u + 15)
                    ex, ey, ez = e[0, x, r, :], e[1, x, r, :], e[2, x, r, :]
                    hx = h[0, x + 1, rh, :] - 0.5 * ((e[2, x, ra, :] - ez) - (zfwd(ey) - ey))
                    hy = h[1, x + 1, rh, :] - 0.5 * ((zfwd(ex) - ex) - (e[2, x + 1, r, :] - ez))
                    hz = h[2, x + 1, rh, :] - 0.5 * ((e[1, x + 1, r, :] - ey) - (e[0, x, ra, :] - ex))
                    hd[0, x + 1, rh, :] = hx
                    hd[1, x + 1, rh, :] = hy
                    hd[2, x + 1, rh, :] = hz
                    cx = (hz - hd[2, x + 1, rb, :]) - (hy - zbwd(hy))
                    cy = (hx - zbwd(hx)) - (hz - hd[2, x, rh, :])
                    cz = (hy - hd[1, x, rh, :]) - (hx - hd[0, x + 1, rb, :])
                    ka, kc, kb, kf, kg = (k[q, x, r, :] for q in range(5))
                    for c, (old, curl) in enumerate(((ex, cx), (ey, cy), (ez, cz))):
                        pol = p[c, x, r, :]
                        new = ka * old + kc * curl + kb * pol
                        ed[c, x, r, :] = new
                        if pd_ is not None:
                            pd_[c, x, r, :] = kf * pol + kg * new
                return carry

            lax.fori_loop(0, 6, at_x, 0, unroll=True)

        def material_window():
            each(-1, lambda m: mat_copy(m).wait_recv())
            for v in range(3):
                mext[v, 1:7, 8:32, :] = mat[v]
                mext[v, 7, 8:32, :] = mx_r[0, v]
                mext[v, 0, 8:32, :] = mx_r[1, v]
                for x in range(6):
                    mext[v, x + 1, 32:33, :] = my_r[YE, v, x:x + 1, :]
                    mext[v, x + 1, 7:8, :] = my_r[YG, v, x:x + 1, :]
                mext[v, 0, 32:33, :] = my_r[C1, v, 0:1, :]
                mext[v, 7, 7:8, :] = my_r[C2, v, 0:1, :]
            for u2 in range(2):
                for v2 in range(2):
                    found = [jnp.zeros((8, 128), jnp.int32)] * 4
                    for u in range(-1, 4):
                        for v in range(3):
                            if u % 2 != u2 or v % 2 != v2:
                                continue
                            ok = (rows + 8 * u >= y0 - 1) & (rows + 8 * u < y0 + 9)
                            ok = ok & (lanes + 128 * v >= z0 - 1) & (lanes + 128 * v < z0 + 129)
                            for xr in range(4):
                                found[xr] = jnp.where(ok, mext[v, x0 + xr, 8 * u + 8:8 * u + 16, :], found[xr])
                    for xr in range(4):
                        wm_s[xr, u2, v2] = found[xr]
            win_copy().start()

        sets = [(e2.at[q], h2.at[q], p2.at[q]) for q in range(3)]
        e_in.wait()
        h_in.wait()
        pack_halos(0, sets[0][0], sets[0][1])
        all_here()
        send_halos(0)
        each(1, lambda m: pos_copy(m).start(), AROUND)
        for cp in m_in:
            cp.wait()
        for v in range(3):
            for x in range(6):
                my_s[YE, v, x:x + 1, :] = mat[v, x, 0:1, :]
                my_s[YG, v, x:x + 1, :] = mat[v, x, 23:24, :]
            my_s[C1, v] = jnp.broadcast_to(mat[v, 5, 0:1, :], (8, 128))
            my_s[C2, v] = jnp.broadcast_to(mat[v, 0, 23:24, :], (8, 128))
        each(1, lambda m: mat_copy(m).start())
        tabs = tables(permit, conduct, relax, debye, 1.0, 0.5)

        def factors(x, carry):
            for u in range(3):
                for v in range(3):
                    here = mat[v, x, 8 * u:8 * u + 8, :]
                    for q in range(5):
                        k[(q, x) + tile_at(u, v)] = pick(tabs[q], here)
            return carry

        lax.fori_loop(0, 6, factors, 0)
        for i in range(2):
            for c in range(3):
                ini_s[c, i] = cut(lambda x, r, l: e2[0, c, x, r, l], i)
        ini_copy().start()
        p_in.wait()

        def advance(slot, source, target):
            put_halos(slot, source[0], target[1])
            update(*source, *target)

        def arrive(slot):
            each(-1, lambda m: halo_copy(m, slot).wait_recv())

        def leave(slot, state):
            pack_halos(slot, state[0], state[1])
            send_halos(slot)

        arrive(0)
        advance(0, sets[0], sets[1])
        cut_latest(0, sets[1][0])
        leave(1, sets[1])
        learn_places()
        material_window()
        arrive(1)
        advance(1, sets[1], sets[2])
        cut_latest(1, sets[2][0])
        leave(2, sets[2])
        arrive(2)
        put_halos(2, sets[2][0], sets[0][1])
        update(*sets[2], sets[0][0], sets[0][1], None)
        cut_latest(2, sets[0][0])
        del_copy(0).wait_recv()
        place(0, sets[1][0])
        mend_halos(1, 0)
        advance(1, sets[1], sets[0])
        leave(3, sets[0])
        arrive(3)
        del_copy(1).wait_recv()
        place(1, sets[0][0])
        mend_halos(3, 1)
        advance(3, sets[0], sets[2])
        e, h, p = sets[2]
        h_out = pltpu.make_async_copy(h.at[:, 1:7, 8:32, :], out.at[0, 3:6], lsem.at[1])
        p_out = pltpu.make_async_copy(p, out.at[0, 6:9], lsem.at[2])
        h_out.start()
        p_out.start()
        del_copy(STEPS - 1).wait_recv()
        place(STEPS - 1, e)
        e_out = pltpu.make_async_copy(e.at[:, 0:6, 0:24, :], out.at[0, 0:3], lsem.at[0])
        e_out.start()

        each(1, lambda m: pos_copy(m).wait_send(), AROUND)
        each(1, lambda m: mat_copy(m).wait_send())
        win_copy().wait_send()
        for n in range(SETS):
            each(1, lambda m: halo_copy(m, n).wait_send())
        for n in range(STEPS):
            lat_copy(n).wait_send()
        ini_copy().wait_send()
        h_out.wait()
        p_out.wait()
        e_out.wait()

    @pl.when(jnp.logical_not(coarse))
    def _():
        for ref in (ny_s, fy_s):
            ref[...] = jnp.zeros_like(ref)
        none = jnp.zeros((8, 128), jnp.int32)
        inside = (rows < ly) & (lanes < lz)
        two = lx == 2

        def inside_x(x):
            return jnp.where((x < 3) | two, 1, 0).astype(jnp.int32)

        tabs = tables(permit, conduct, relax, debye, 1.0 / 3.0, 0.25)
        spread = [3 * lanes + r for r in range(3)]
        phase = lanes % 3
        source = [(128 * ((phase + 3 - r) % 3) + lanes) // 3 for r in range(3)]

        def gather_in(ref, lead, ry):
            parts = [ref[(v,) + lead + (pl.ds(ry, 8, stride=3), slice(None))] for v in range(3)]
            tiles = []
            for r in range(3):
                at, src = spread[r] & 127, spread[r] >> 7
                got = [pick(part, at) for part in parts]
                tiles.append(jnp.where(src == 0, got[0], jnp.where(src == 1, got[1], got[2])))
            return tiles

        for cp in m_in:
            cp.wait()

        def fine_factors(x, carry):
            ok = inside & (inside_x(x) + none > 0)
            for ry in range(3):
                for r, here in enumerate(gather_in(mat, (x,), ry)):
                    ka, kc, kb, kf, kg = (pick(tabs[q], here) for q in range(5))
                    t = 3 * ry + r
                    fk[0, x, t] = ka
                    fk[1, x, t] = jnp.where(ok, kc, 0.0)
                    fk[2, x, t] = jnp.where(ok, kb * kg, 0.0)
                    fk[3, x, t] = kf
                    fk[4, x, t] = kg
                    fkr[x, t] = 1.0 / kg
            return carry

        lax.fori_loop(0, 6, fine_factors, 0)
        all_here()
        each(1, lambda m: pos_copy(m).start(), AROUND)
        for cp in f_in:
            cp.wait()
        for c in range(3):
            ff[c, 6] = jnp.zeros((9, 8, 128), F32)
            ff[3 + c, 0] = jnp.zeros((9, 8, 128), F32)

        def load_fine(x, carry):
            ok = inside & (inside_x(x) + none > 0)
            for c in range(9):
                for ry in range(3):
                    for r, here in enumerate(gather_in(stage, (c, x), ry)):
                        t = 3 * ry + r
                        if 3 <= c < 6:
                            ff[c, x + 1, t] = jnp.where(ok, 2.0 * here, 0.0)
                        elif c < 3:
                            ff[c, x, t] = jnp.where(ok, here, 0.0)
                        else:
                            ff[c, x, t] = jnp.where(ok, here * fkr[x, t], 0.0)
            return carry

        lax.fori_loop(0, 6, load_fine, 0)

        back_y, back_z = (8 - y0 % 8) % 8, (128 - z0 % 128) % 128

        def to_box(tile):
            return pltpu.roll(pltpu.roll(tile, back_y, 0), back_z, 1)

        def from_box(tile):
            return pltpu.roll(pltpu.roll(tile, y0 % 8, 0), z0 % 128, 1)

        edge_y = {0: rows == 0, 2: rows == ly - 1}
        edge_z = {0: lanes == 0, 2: lanes == lz - 1}

        def at_layer(x, carry):
            ok = inside & (inside_x(x) + none > 0)
            edge = jnp.where((x == 0) | (x == 3 * lx - 1), 1, 0).astype(jnp.int32)
            edge_x = ok & (edge + none > 0)
            ok_y = {q: m & ok for q, m in edge_y.items()}
            ok_z = {q: m & ok for q, m in edge_z.items()}
            xc = x // 3
            tiles = [(ry, rz) for ry in range(3) for rz in range(3)]
            E = {(c, t): ff[c, x, t] for c in range(3) for t in range(9)}
            F = {(c, t): ff[c, x + 1, t] for c in (1, 2) for t in range(9)}
            H = {}
            for ry, rz in tiles:
                t = 3 * ry + rz
                ex, ey, ez = (E[c, t] for c in range(3))
                if ry < 2:
                    exy, ezy = E[0, t + 3], E[2, t + 3]
                else:
                    exy, ezy = yfwd(E[0, rz]), yfwd(E[2, rz])
                if rz < 2:
                    exz, eyz = E[0, t + 1], E[1, t + 1]
                else:
                    exz, eyz = zfwd(E[0, 3 * ry]), zfwd(E[1, 3 * ry])
                H[0, t] = ff[3, x + 1, t] - ((ezy - ez) - (eyz - ey))
                H[1, t] = ff[4, x + 1, t] - ((exz - ex) - (F[2, t] - ez))
                H[2, t] = ff[5, x + 1, t] - ((F[1, t] - ey) - (exy - ex))
                for c in range(3):
                    ff[3 + c, x + 1, t] = H[c, t]
            for ry, rz in tiles:
                t = 3 * ry + rz
                hx, hy, hz = (H[c, t] for c in range(3))
                if ry > 0:
                    hxy, hzy = H[0, t - 3], H[2, t - 3]
                else:
                    hxy, hzy = ybwd(H[0, 6 + rz]), ybwd(H[2, 6 + rz])
                if rz > 0:
                    hxz, hyz = H[0, t - 1], H[1, t - 1]
                else:
                    hxz, hyz = zbwd(H[0, 3 * ry + 2]), zbwd(H[1, 3 * ry + 2])
                hyx, hzx = ff[4, x, t], ff[5, x, t]
                curls = ((hz - hzy) - (hy - hyz), (hx - hxz) - (hz - hzx), (hy - hyx) - (hx - hxy))
                ka, kc, kb, kf = (fk[q, x, t] for q in range(4))
                for c in range(3):
                    pol = ff[6 + c, x, t]
                    new = ka * E[c, t] + kc * curls[c] + kb * pol
                    marks = []
                    if c != 0:
                        marks.append(edge_x)
                    if c != 1 and ry in ok_y:
                        marks.append(ok_y[ry])
                    if c != 2 and rz in ok_z:
                        marks.append(ok_z[rz])
                    if marks:
                        new = jnp.where(functools.reduce(jnp.logical_or, marks), drv[c, xc], new)
                    ff[c, x, t] = new
                    ff[6 + c, x, t] = kf * pol + new
            return carry

        wrows = lax.broadcasted_iota(jnp.int32, (16, 256), 0)
        wlanes = lax.broadcasted_iota(jnp.int32, (16, 256), 1)
        at_y = y0 - 4 + ((wrows - (y0 - 4)) & 15)
        at_z = z0 - 64 + ((wlanes - (z0 - 64)) & 255)

        def w_in(at, low, size):
            return (at >= low) & (at < low + size)

        def twice(tile):
            return jnp.concatenate([jnp.concatenate([tile, tile], axis=1)] * 2, axis=0)

        def as_int(flag):
            return jnp.where(flag, 1, 0).astype(jnp.int32)

        def up_y(a):
            return pltpu.roll(a, 15, 0)

        def up_z(a):
            return pltpu.roll(a, 255, 1)

        def down_y(a):
            return pltpu.roll(a, 1, 0)

        def down_z(a):
            return pltpu.roll(a, 1, 1)

        region = w_in(at_y, y0, 8) & w_in(at_z, z0, 128)
        w_none = jnp.zeros((16, 256), jnp.int32)
        global_y = at_y + 24 * gb
        held_yz = (at_z >= 0) & (global_y >= 0)
        in_yz = held_yz & (at_z < 384) & (global_y < 24 * ny)

        def changes(d, reach):
            w = {}
            for c in range(3):
                for xr in range(-reach, 2 + reach):
                    w[c, xr] = jnp.where(region, twice(del_s[d, c, xr]), 0.0) if 0 <= xr < 2 else jnp.zeros((16, 256), F32)
            for m, (dx, dy) in enumerate(AROUND):
                far_x, far_y, far_z = place_of[m, 0, 0], place_of[m, 1, 0], place_of[m, 2, 0]
                ok = w_in(at_z, far_z, 128)
                if dy == 0:
                    ok = ok & w_in(at_y, far_y, 8)
                else:
                    ok = ok & w_in(at_y, 24 if dy < 0 else -2, 2)
                for xr in {0: range(-reach, 2 + reach), -1: range(2, 2 + reach), 1: range(-reach, 0)}[dx]:
                    i = x0 + xr + 6 * dx - far_x
                    s0 = jnp.where(i == 0, 1.0, 0.0).astype(F32)
                    s1 = jnp.where(i == 1, 1.0, 0.0).astype(F32)
                    for c in range(3):
                        if dy == 0:
                            tile = s0 * fx_r[m // 2, d, c, 0] + s1 * fx_r[m // 2, d, c, 1]
                        else:
                            pair = [s0 * fy_r[m, d, 6 * r + 2 * c:6 * r + 2 * c + 1, :]
                                    + s1 * fy_r[m, d, 6 * r + 2 * c + 1:6 * r + 2 * c + 2, :] for r in range(2)]
                            low = 0 if dy < 0 else 6
                            tile = jnp.where(rows == low, jnp.broadcast_to(pair[0], (8, 128)),
                                             jnp.broadcast_to(pair[1], (8, 128)))
                        w[c, xr] = w[c, xr] + jnp.where(ok, twice(tile), 0.0)
            return w

        def turned_ahead(w, xr):
            ex, ey, ez = (w[c, xr] for c in range(3))
            moved = ((up_y(ez) - ez) - (up_z(ey) - ey), (up_z(ex) - ex) - (w[2, xr + 1] - ez),
                     (w[1, xr + 1] - ey) - (up_y(ex) - ex))
            ok = held_yz & (as_int(x0 + xr + 6 * ga >= 0) + w_none > 0)
            return [jnp.where(ok, -0.5 * part, 0.0) for part in moved]

        def turned_behind(hh, xr):
            hx, hy, hz = (hh[c, xr] for c in range(3))
            return ((hz - down_y(hz)) - (hy - down_z(hy)), (hx - down_z(hx)) - (hz - hh[2, xr - 1]),
                    (hy - hh[1, xr - 1]) - (hx - down_y(hx)))

        def on_region(wide):
            kept = jnp.where(region, wide, 0.0)
            return (kept[0:8, 0:128] + kept[0:8, 128:256]) + (kept[8:16, 0:128] + kept[8:16, 128:256])

        def window_factors():
            win_copy().wait_recv()
            slab = tables(permit, conduct, relax, debye, 1.0, 0.5)
            for xr in range(4):
                for u2 in range(2):
                    for v2 in range(2):
                        here = wm_r[xr, u2, v2]
                        spot = (xr, slice(8 * u2, 8 * u2 + 8), slice(128 * v2, 128 * v2 + 128))
                        for q in range(2):
                            kw[(q,) + spot] = pick(slab[q], here)
                        kw[(2,) + spot] = pick(slab[2], here) * pick(slab[4], here)

        def respond(n):
            each(-1, lambda m: box_copy(m, n - 1).wait_recv(), AROUND)
            hh = {}
            if n == 1:
                w = changes(0, 2)
                for xr in range(-2, 3):
                    for c, part in enumerate(turned_ahead(w, xr)):
                        hh[c, xr] = part
                        if -1 <= xr <= 1:
                            hw[c, xr + 1] = part
                layers = range(-1, 3)
            else:
                w = changes(1, 1)
                for c in range(3):
                    for xr in range(-1, 3):
                        w[c, xr] = w[c, xr] + ew[c, xr + 1]
                for xr in range(-1, 2):
                    for c, part in enumerate(turned_ahead(w, xr)):
                        hh[c, xr] = hw[c, xr + 1] + part
                layers = range(2)
            for xr in layers:
                ok = in_yz & (as_int((x0 + xr + 6 * ga >= 0) & (x0 + xr + 6 * ga < 6 * nx)) + w_none > 0)
                for c, curl in enumerate(turned_behind(hh, xr)):
                    value = kw[0, xr + 1] * w[c, xr] + kw[1, xr + 1] * curl
                    if n == 1:
                        value = jnp.where(ok, value, 0.0)
                        ew[c, xr + 1] = value
                    else:
                        value = value + kw[2, xr + 1] * ew[c, xr + 1]
                    if 0 <= xr < 2:
                        ear[1, c, xr] = to_box(lat_r[n, c, xr] + on_region(value))

        learn_places()
        ini_copy().wait_recv()
        for c in range(3):
            for i in range(2):
                ear[0, c, i] = to_box(ini_r[c, i])

        for n in range(STEPS):
            lat_copy(n).wait_recv()
            if n == 0:
                for c in range(3):
                    for i in range(2):
                        ear[1, c, i] = to_box(lat_r[0, c, i])
            else:
                if n == 1:
                    window_factors()
                respond(n)

            def substep(s, carry):
                weight = (s + 1).astype(F32) * (1.0 / 3.0)
                drv[...] = ear[0] + weight * (ear[1] - ear[0])
                return lax.fori_loop(0, 6, at_layer, carry, unroll=True)

            lax.fori_loop(0, 3, substep, 0)
            for i in range(2):
                ok = inside & (inside_x(3 * i) + none > 0)
                for c in range(3):
                    total = functools.reduce(
                        jnp.add, [ff[c, 3 * i + j, t] for j in range(3) for t in range(9)])
                    latest = ear[1, c, i]
                    delta = jnp.where(ok, total * (1.0 / 27.0) - latest, 0.0)
                    ear[0, c, i] = latest + delta
                    del_s[n, c, i] = from_box(delta)
            if n + 1 < STEPS:
                for r in range(2):
                    low = jnp.where(y0 <= r, 1.0, 0.0).astype(F32)
                    high = jnp.where(y0 >= 15 + r, 1.0, 0.0).astype(F32)
                    for c in range(3):
                        for i in range(2):
                            row = 6 * r + 2 * c + i
                            fy_s[0, n, row:row + 1, :] = low * del_s[n, c, i, r:r + 1, :]
                            fy_s[1, n, row:row + 1, :] = high * del_s[n, c, i, 6 + r:7 + r, :]
                for m in (4, 5, 6, 7, 0, 2, 1, 3):
                    dx, dy = AROUND[m]

                    @pl.when(exists(dx, dy))
                    def _():
                        box_copy(m, n).start()
                low, high = (jnp.where(x0 == q, 1.0, 0.0).astype(F32) for q in (0, 4))
                left, right = (jnp.where(y0 == q, 1.0, 0.0).astype(F32) for q in (0, 16))
                for c in range(3):
                    nx_s[0, n, c] = low * del_s[n, c, 0]
                    nx_s[1, n, c] = high * del_s[n, c, 1]
                    for i in range(2):
                        ny_s[0, n, 2 * c + i:2 * c + i + 1, :] = left * del_s[n, c, i, 0:1, :]
                        ny_s[1, n, 2 * c + i:2 * c + i + 1, :] = right * del_s[n, c, i, 7:8, :]
                nd_s[0, n] = jnp.broadcast_to((high * left) * del_s[n, 0, 1, 0:1, :], (8, 128))
                nd_s[1, n] = jnp.broadcast_to((low * right) * del_s[n, 1, 0, 7:8, :], (8, 128))
                del_copy(n).start()
                each(1, lambda m: near_copy(m, n).start())
            else:
                del_copy(n).start()

        def save_fine(x, carry):
            for c in range(9):
                for ry in range(3):
                    lift = 1 if 3 <= c < 6 else 0
                    parts = [ff[c, x + lift, 3 * ry + r] for r in range(3)]
                    if c >= 6:
                        parts = [part * fk[4, x, 3 * ry + r] for r, part in enumerate(parts)]
                    got = [pick(part, source[r]) for r, part in enumerate(parts)]
                    for v in range(3):
                        a, b, d = (got[(q + 2 * v) % 3] for q in range(3))
                        value = jnp.where(phase == 0, a, jnp.where(phase == 1, b, d))
                        if lift:
                            value = 0.5 * value
                        stage[v, c, x, pl.ds(ry, 8, stride=3), :] = value
            return carry

        lax.fori_loop(0, 6, save_fine, 0)
        f_out = [pltpu.make_async_copy(stage.at[v], out.at[0, :, :, :, pl.ds(128 * v, 128)], lsem.at[v]) for v in range(3)]
        for cp in f_out:
            cp.start()
        each(1, lambda m: pos_copy(m).wait_send(), AROUND)
        for n in range(STEPS):
            del_copy(n).wait_send()
            if n + 1 < STEPS:
                each(1, lambda m: near_copy(m, n).wait_send())
                each(1, lambda m: box_copy(m, n).wait_send(), AROUND)
        for cp in f_out:
            cp.wait()


def solution(mesh):
    nx, ny = mesh.shape["gx"], mesh.shape["gy"]

    def body(fields, material, permit, conduct, relax, debye, subgrids):
        vm = pltpu.VMEM
        dma = pltpu.SemaphoreType.DMA
        slots = [
            vm((SETS, 2, 24, 384), F32), vm((SETS, 2, 8, 384), F32),
            vm((SETS, 2, 24, 384), F32), vm((SETS, 2, 8, 384), F32),
            vm((SETS, 8, 384), F32), vm((SETS, 8, 384), F32),
        ]
        region = (3, 2, 8, 128)
        near = [vm((2, STEPS - 1, 3, 8, 128), F32), vm((2, STEPS - 1, 8, 128), F32), vm((2, STEPS - 1, 8, 128), F32)]
        return pl.pallas_call(
            functools.partial(kernel, nx, ny),
            out_shape=jax.ShapeDtypeStruct(fields.shape, F32),
            in_specs=[pl.BlockSpec(memory_space=pl.ANY)] * 2 + [pl.BlockSpec(memory_space=pltpu.SMEM)] * 5,
            out_specs=pl.BlockSpec(memory_space=pl.ANY),
            scratch_shapes=[
                vm((3, 3, 7, 32, 384), F32), vm((3, 3, 7, 32, 384), F32), vm((3, 3, 6, 24, 384), F32), vm((5, 6, 24, 384), F32),
                vm((3, 9, 6, 24, 128), F32), vm((3, 6, 24, 128), jnp.int32),
                vm((9, 7, 9, 8, 128), F32), vm((5, 6, 9, 8, 128), F32),
                vm((5, 16, 384), F32), vm((2, 8, 384), F32), vm((2, 8, 384), F32), vm((3, 32, 384), F32), vm((3, 8, 384), F32),
                vm((2,) + region, F32), vm(region, F32), vm((6, 9, 8, 128), F32),
                vm((3, 8, 40, 128), jnp.int32), vm((3, 4, 16, 256), F32), vm((3, 3, 16, 256), F32), vm((3, 4, 16, 256), F32),
                *slots, *slots,
                vm((STEPS,) + region, F32), vm((STEPS,) + region, F32), vm(region, F32), vm(region, F32),
                vm((STEPS,) + region, F32), vm((STEPS,) + region, F32),
                *near, *near, vm((8, 128), jnp.int32), vm((8, 8, 128), jnp.int32), pltpu.SMEM((8, 8, 128), jnp.int32),
                vm((2, STEPS - 1, 16, 128), F32), vm((2, STEPS - 1) + region, F32), vm((8, STEPS - 1, 16, 128), F32),
                vm((6, 3, 8, 128), jnp.int32), vm((2, 3, 24, 128), jnp.int32), vm((6, 3, 8, 128), jnp.int32),
                vm((4, 2, 2, 8, 128), jnp.int32), vm((4, 2, 2, 8, 128), jnp.int32),
                dma((7,)), dma((6, SETS)), dma((6, SETS)),
                dma((STEPS + 1,)), dma((STEPS + 1,)), dma((STEPS,)), dma((STEPS,)),
                dma((6, STEPS)), dma((6, STEPS)), dma((8,)), dma((8,)),
                dma((8, STEPS)), dma((8, STEPS)), dma((6,)), dma((6,)), dma((1,)), dma((1,)),
            ],
            compiler_params=pltpu.CompilerParams(
                collective_id=0, has_side_effects=True, vmem_limit_bytes=63 * 1024 * 1024),
        )(fields, material, permit, conduct, relax, debye, subgrids)

    return jax.shard_map(
        body,
        mesh=mesh,
        in_specs=(P("grid", None, "gx", "gy", None), P("grid", "gx", "gy", None), P(), P(), P(), P(), P("gx", "gy", None)),
        out_specs=P("grid", None, "gx", "gy", None),
        check_vma=False,
    )
```

```python
import functools

import jax
import jax.numpy as jnp
from jax import lax
from jax.experimental import pallas as pl
from jax.experimental.pallas import tpu as pltpu
from jax.sharding import PartitionSpec as P

MESH = pl.DeviceIdType.MESH
STEPS = 3
F32 = jnp.float32

TO_NEXT = ((-1, 0), (0, -1), (1, 0), (0, 1), (1, -1), (-1, 1))
XE, YE, XG, YG, C1, C2 = range(6)
AROUND = TO_NEXT + ((1, 1), (-1, -1))
SETS = STEPS + 1


def lane_iota():
    return lax.broadcasted_iota(jnp.int32, (8, 128), 1)


def row_iota():
    return lax.broadcasted_iota(jnp.int32, (8, 128), 0)


def pick(tile, index):
    return jnp.take_along_axis(tile, index, axis=1, mode="promise_in_bounds")


def zfwd(v):
    n = v.shape[-1]
    lanes = lax.broadcasted_iota(jnp.int32, v.shape, v.ndim - 1)
    return jnp.where(lanes == n - 1, 0.0, pltpu.roll(v, n - 1, v.ndim - 1))


def zbwd(v):
    lanes = lax.broadcasted_iota(jnp.int32, v.shape, v.ndim - 1)
    return jnp.where(lanes == 0, 0.0, pltpu.roll(v, 1, v.ndim - 1))


def yfwd(t):
    return jnp.where(row_iota() == 7, 0.0, pltpu.roll(t, 7, 0))


def ybwd(t):
    return jnp.where(row_iota() == 0, 0.0, pltpu.roll(t, 1, 0))


def tables(permit, conduct, relax, debye, factor, courant):
    lane = lane_iota()

    def spread(ref):
        out = jnp.ones((8, 128), F32)
        for m in range(8):
            out = jnp.where(lane == m, ref[m], out)
        return out

    eps = spread(permit)
    damping = spread(conduct) * factor / (2.0 * eps)
    f0 = (1.0 - damping) / (1.0 + damping)
    f1 = 1.0 / (eps * (1.0 + damping))
    f2 = spread(relax) * factor
    f3 = jnp.exp(-f2)
    f4 = spread(debye)
    return f0 - f1 * f2 * f4, courant * f1, f1 * f2, f3, (1.0 - f3) * f4


def kernel(
    nx, ny,
    fields, material, permit_in, conduct_in, relax_in, debye_in, subgrids_in, out,
    permit, conduct, relax, debye, subgrids, e2, h2, p2, k, stage, mat, ff, fk, pk, pln, own, dl, pd, ear, drv, fkr, mext, ew, hw, kw,
    xe_s, ye_s, xg_s, yg_s, c1_s, c2_s,
    xe_r, ye_r, xg_r, yg_r, c1_r, c2_r,
    lat_s, lat_r, ini_s, ini_r, del_s, del_r,
    nx_s, ny_s, nd_s, nx_r, ny_r, nd_r, pos_s, pos_r, place_of,
    fy_s, fx_r, fy_r, my_s, mx_r, my_r, wm_s, wm_r,
    lsem, hs, hr, bs, br, ds, dr, ns, nr, ps, pr, fs, fr, ms, mr, ws, wr,
):
    grid = lax.axis_index("grid")
    ga = lax.axis_index("gx")
    gb = lax.axis_index("gy")
    coarse = grid == 0
    sends = (xe_s, ye_s, xg_s, yg_s, c1_s, c2_s)
    recvs = (xe_r, ye_r, xg_r, yg_r, c1_r, c2_r)
    delta_s = (nx_s.at[0], ny_s.at[0], nx_s.at[1], ny_s.at[1], nd_s.at[0], nd_s.at[1])
    delta_r = (nx_r.at[0], ny_r.at[0], nx_r.at[1], ny_r.at[1], nd_r.at[0], nd_r.at[1])

    def exists(dx, dy):
        return (ga + dx >= 0) & (ga + dx < nx) & (gb + dy >= 0) & (gb + dy < ny)

    def device(g, dx, dy):
        return (g, jnp.clip(ga + dx, 0, nx - 1), jnp.clip(gb + dy, 0, ny - 1))

    partner = (1 - grid, ga, gb)
    rows, lanes = row_iota(), lane_iota()

    e_in = pltpu.make_async_copy(fields.at[0, 0:3], e2.at[0, :, 0:6, 0:24, :], lsem.at[0])
    h_in = pltpu.make_async_copy(fields.at[0, 3:6], h2.at[0, :, 1:7, 8:32, :], lsem.at[1])
    p_in = pltpu.make_async_copy(fields.at[0, 6:9], p2.at[0], lsem.at[2])
    f_in = [pltpu.make_async_copy(fields.at[0, :, :, :, pl.ds(128 * v, 128)], stage.at[v], lsem.at[v]) for v in range(3)]
    m_in = [pltpu.make_async_copy(material.at[0, :, :, pl.ds(128 * v, 128)], mat.at[v], lsem.at[3 + v]) for v in range(3)]

    @pl.when(coarse)
    def _():
        for cp in (e_in, h_in, p_in):
            cp.start()

    @pl.when(jnp.logical_not(coarse))
    def _():
        for cp in f_in:
            cp.start()

    for cp in m_in:
        cp.start()
    scalars = [
        pltpu.make_async_copy(a, b, lsem.at[7 + q])
        for q, (a, b) in enumerate(((permit_in, permit), (conduct_in, conduct), (relax_in, relax), (debye_in, debye),
                                    (subgrids_in, subgrids)))]
    for cp in scalars:
        cp.start()
    for ref in (nx_r, ny_r, nd_r, pos_r, fx_r, fy_r):
        ref[...] = jnp.zeros_like(ref)

    @pl.when(coarse)
    def _():
        for ref in (mx_r, my_r) + recvs:
            ref[...] = jnp.zeros_like(ref)

    barrier = pltpu.get_barrier_semaphore()
    pl.semaphore_signal(barrier, inc=1, device_id=partner, device_id_type=MESH)
    count = jnp.int32(1)
    for dx, dy in AROUND:
        count = count + exists(dx, dy).astype(jnp.int32)

        @pl.when(exists(dx, dy))
        def _():
            pl.semaphore_signal(barrier, inc=1, device_id=(grid, ga + dx, gb + dy), device_id_type=MESH)

    @pl.when(coarse)
    def _():
        for ref in (ye_s, yg_s, pk, pln, own, my_s, mext):
            ref[...] = jnp.zeros_like(ref)

    for cp in scalars:
        cp.wait()
    x0, y0, z0 = subgrids[0, 0, 0], subgrids[0, 0, 1], subgrids[0, 0, 2]
    lx, ly, lz = subgrids[0, 0, 3], subgrids[0, 0, 4], subgrids[0, 0, 5]
    pos_s[...] = jnp.where(rows == 0, x0, jnp.where(rows == 1, y0, z0))

    def all_here():
        pl.semaphore_wait(barrier, count)

    def remote(src, dst, send, recv, target):
        return pltpu.make_async_remote_copy(
            src_ref=src, dst_ref=dst, send_sem=send, recv_sem=recv, device_id=target, device_id_type=MESH)

    def halo_copy(m, n):
        if m in (C1, C2):
            return remote(sends[m].at[n, 0:1], recvs[m].at[n, 0:1], hs.at[m, n], hr.at[m, n], device(grid, *TO_NEXT[m]))
        return remote(sends[m].at[n], recvs[m].at[n], hs.at[m, n], hr.at[m, n], device(grid, *TO_NEXT[m]))

    def lat_copy(n):
        return remote(lat_s.at[n], lat_r.at[n], bs.at[n], br.at[n], partner)

    def ini_copy():
        return remote(ini_s, ini_r, bs.at[STEPS], br.at[STEPS], partner)

    def del_copy(n):
        return remote(del_s.at[n], del_r.at[n], ds.at[n], dr.at[n], partner)

    def near_copy(m, n):
        return remote(delta_s[m].at[n], delta_r[m].at[n], ns.at[m, n], nr.at[m, n], device(0, *TO_NEXT[m]))

    def box_copy(m, n):
        dx, dy = AROUND[m]
        if dy == 0:
            src, dst = del_s.at[n], fx_r.at[m // 2, n]
        else:
            src, dst = fy_s.at[0 if dy < 0 else 1, n], fy_r.at[m, n]
        return remote(src, dst, fs.at[m, n], fr.at[m, n], device(1, dx, dy))

    def pos_copy(m):
        return remote(pos_s, pos_r.at[m], ps.at[m], pr.at[m], device(grid, *AROUND[m]))

    def mat_copy(m):
        dx, dy = TO_NEXT[m]
        if dy == 0:
            src, dst = mat.at[:, 0 if dx < 0 else 5], mx_r.at[m // 2]
        else:
            src, dst = my_s.at[m], my_r.at[m]
        return remote(src, dst, ms.at[m], mr.at[m], device(0, dx, dy))

    def win_copy():
        return remote(wm_s, wm_r, ws.at[0], wr.at[0], partner)

    def each(turn, fun, over=TO_NEXT):
        for m, (dx, dy) in enumerate(over):
            @pl.when(exists(turn * dx, turn * dy))
            def _():
                fun(m)

    def learn_places():
        each(-1, lambda m: pos_copy(m).wait_recv(), AROUND)
        cp = pltpu.make_async_copy(pos_r, place_of, lsem.at[6])
        cp.start()
        cp.wait()

    def row_in(low, u):
        return (rows + 8 * u >= low) & (rows + 8 * u < low + 8)

    def lane_in(low, v):
        return (lanes + 128 * v >= low) & (lanes + 128 * v < low + 128)

    def tile_at(u, v):
        return (slice(8 * u, 8 * u + 8), slice(128 * v, 128 * v + 128))

    @pl.when(coarse)
    def _():
        flag_x = jnp.where(ga > 0, 1.0, 0.0).astype(F32)
        flag_y = jnp.where(gb > 0, 1.0, 0.0).astype(F32)
        row_ok = [row_in(y0, u) for u in range(3)]
        lane_ok = [lane_in(z0, v) for v in range(3)]
        wide = lax.broadcasted_iota(jnp.int32, (24, 384), 0)
        plane = lax.broadcasted_iota(jnp.int32, (8, 384), 0)

        def cut(load, i):
            tile = jnp.zeros((8, 128), F32)
            for u in range(3):
                for v in range(3):
                    tile = jnp.where(row_ok[u] & lane_ok[v], load(x0 + i, *tile_at(u, v)), tile)
            return tile

        def cut_latest(n, e):
            for i in range(2):
                for c in range(3):
                    lat_s[n, c, i] = cut(lambda x, r, l: e[c, x, r, l], i)
            lat_copy(n).start()

        def place(n, e, done=None):
            for x in range(6):
                s0 = jnp.where(x == x0, 1.0, 0.0).astype(F32)
                s1 = jnp.where(x == x0 + 1, 1.0, 0.0).astype(F32)
                for c in range(3):
                    tile = s0 * del_r[n, c, 0] + s1 * del_r[n, c, 1]
                    for u in range(3):
                        for v in range(3):
                            spot = (c, x) + tile_at(u, v)
                            e[spot] = e[spot] + jnp.where(row_ok[u] & lane_ok[v], tile, 0.0)
                if done is not None:
                    done[x].start()

        def send_halo(m, n):
            @pl.when(exists(*TO_NEXT[m]))
            def _():
                halo_copy(m, n).start()

        def leave_high(n, e, h):
            c1_s[n, 0:1, :] = e[0, 5, 0:1, :]
            send_halo(C1, n)
            ex, ey, ez = e[0, 5, 0:24, :], e[1, 5, 0:24, :], e[2, 5, 0:24, :]
            exy = jnp.where(wide == 23, 0.0, e[0, 5, 1:25, :])
            xg_s[n, 0] = h[1, 6, 8:32, :] - 0.5 * (zfwd(ex) - ex + ez)
            xg_s[n, 1] = h[2, 6, 8:32, :] + 0.5 * (ey + exy - ex)
            send_halo(XG, n)

        def leave_low(n, e):
            c2_s[n, 0:1, :] = e[1, 0, 23:24, :]
            send_halo(C2, n)
            xe_s[n] = e[1:3, 0, 0:24, :]
            send_halo(XE, n)

        def leave_y(n, e, h):
            for x in range(6):
                ye_s[n, 0, x:x + 1, :] = e[0, x, 0:1, :]
                ye_s[n, 1, x:x + 1, :] = e[2, x, 0:1, :]
            send_halo(YE, n)
            for x in range(6):
                for c in range(3):
                    pk[c, x:x + 1, :] = e[c, x, 23:24, :]
                pk[3, x:x + 1, :] = h[0, x + 1, 31:32, :]
                pk[4, x:x + 1, :] = h[2, x + 1, 31:32, :]
            px, py, pz = pk[0, 0:8, :], pk[1, 0:8, :], pk[2, 0:8, :]
            yg_s[n, 0] = pk[3, 0:8, :] + 0.5 * (pz + zfwd(py) - py)
            yg_s[n, 1] = pk[4, 0:8, :] - 0.5 * (pk[1, 1:9, :] - py + px)
            send_halo(YG, n)

        def put_halos(n, e, h):
            e[1:3, 6, 0:24, :] = xe_r[n]
            h[1, 0, 8:32, :] = flag_x * (xg_r[n, 0] + 0.5 * e[2, 0, 0:24, :])
            corner = jnp.where(wide == 23, jnp.broadcast_to(c1_r[n, 0:1, :], (24, 384)), 0.0)
            h[2, 0, 8:32, :] = flag_x * (xg_r[n, 1] - 0.5 * (e[1, 0, 0:24, :] - corner))
            for x in range(6):
                own[0, x:x + 1, :] = e[0, x, 0:1, :]
                own[1, x:x + 1, :] = e[2, x, 0:1, :]
            pln[0] = flag_y * (yg_r[n, 0] - 0.5 * own[1])
            pln[1] = flag_y * (yg_r[n, 1] + 0.5 * (own[0] - jnp.where(plane == 5, jnp.broadcast_to(c2_r[n, 0:1, :], (8, 384)), 0.0)))
            for x in range(6):
                e[0, x, 24:25, :] = ye_r[n, 0, x:x + 1, :]
                e[2, x, 24:25, :] = ye_r[n, 1, x:x + 1, :]
                h[0, x + 1, 7:8, :] = pln[0, x:x + 1, :]
                h[2, x + 1, 7:8, :] = pln[1, x:x + 1, :]

        def mend_halos(n, d):
            each(-1, lambda m: near_copy(m, d).wait_recv())
            for u in range(3):
                for v in range(3):
                    spot = tile_at(u, v)
                    ok = row_in(place_of[XE, 1, 0], u) & lane_in(place_of[XE, 2, 0], v)
                    for q in range(2):
                        xe_r[(n, q) + spot] = xe_r[(n, q) + spot] + jnp.where(ok, nx_r[0, d, 1 + q], 0.0)
                    ok = row_in(place_of[XG, 1, 0], u) & lane_in(place_of[XG, 2, 0], v)
                    for c in range(3):
                        dl[(c,) + spot] = jnp.where(ok, nx_r[1, d, c], 0.0)
            tx, ty, tz = dl[0, 0:24, :], dl[1, 0:24, :], dl[2, 0:24, :]
            dl[0, 24:32, :] = jnp.zeros((8, 384), F32)
            xg_r[n, 0] = xg_r[n, 0] - 0.5 * (zfwd(tx) - tx + tz)
            xg_r[n, 1] = xg_r[n, 1] + 0.5 * (ty + dl[0, 1:25, :] - tx)
            for m, keep in ((YE, ny_r.at[0]), (YG, ny_r.at[1])):
                at = place_of[m, 0, 0]
                for c in range(3):
                    two = [jnp.broadcast_to(keep[d, 2 * c + i:2 * c + i + 1, :], (8, 128)) for i in range(2)]
                    both = jnp.where(rows == at, two[0], jnp.where(rows == at + 1, two[1], 0.0))
                    for v in range(3):
                        pd[c, :, 128 * v:128 * v + 128] = jnp.where(lane_in(place_of[m, 2, 0], v), both, 0.0)
                if m == YE:
                    ye_r[n, 0] = ye_r[n, 0] + pd[0]
                    ye_r[n, 1] = ye_r[n, 1] + pd[2]
                else:
                    yg_r[n, 0] = yg_r[n, 0] + 0.5 * (pd[2] + zfwd(pd[1]) - pd[1])
                    yg_r[n, 1] = yg_r[n, 1] - 0.5 * (pltpu.roll(pd[1], 7, 0) - pd[1] + pd[0])
            for m, ref, keep in ((C1, c1_r, nd_r.at[0]), (C2, c2_r, nd_r.at[1])):
                for v in range(3):
                    spot = (n, slice(0, 8), slice(128 * v, 128 * v + 128))
                    ref[spot] = ref[spot] + jnp.where(lane_in(place_of[m, 2, 0], v), keep[d], 0.0)

        def update(e, h, p, ed, hd, pd_, slot=None, cut_to=None):
            def magnetic(x):
                for u in range(3):
                    r = slice(8 * u, 8 * u + 8)
                    ra = slice(8 * u + 1, 8 * u + 9)
                    rh = slice(8 * u + 8, 8 * u + 16)
                    ex, ey, ez = e[0, x, r, :], e[1, x, r, :], e[2, x, r, :]
                    hd[0, x + 1, rh, :] = h[0, x + 1, rh, :] - 0.5 * ((e[2, x, ra, :] - ez) - (zfwd(ey) - ey))
                    hd[1, x + 1, rh, :] = h[1, x + 1, rh, :] - 0.5 * ((zfwd(ex) - ex) - (e[2, x + 1, r, :] - ez))
                    hd[2, x + 1, rh, :] = h[2, x + 1, rh, :] - 0.5 * ((e[1, x + 1, r, :] - ey) - (e[0, x, ra, :] - ex))

            def electric(x):
                for u in range(3):
                    r = slice(8 * u, 8 * u + 8)
                    rh = slice(8 * u + 8, 8 * u + 16)
                    rb = slice(8 * u + 7, 8 * u + 15)
                    hx, hy, hz = hd[0, x + 1, rh, :], hd[1, x + 1, rh, :], hd[2, x + 1, rh, :]
                    cx = (hz - hd[2, x + 1, rb, :]) - (hy - zbwd(hy))
                    cy = (hx - zbwd(hx)) - (hz - hd[2, x, rh, :])
                    cz = (hy - hd[1, x, rh, :]) - (hx - hd[0, x + 1, rb, :])
                    ka, kc, kb, kf, kg = (k[q, x, r, :] for q in range(5))
                    for c, curl in enumerate((cx, cy, cz)):
                        pol = p[c, x, r, :]
                        new = ka * e[c, x, r, :] + kc * curl + kb * pol
                        ed[c, x, r, :] = new
                        if pd_ is not None:
                            pd_[c, x, r, :] = kf * pol + kg * new

            magnetic(4)
            magnetic(5)
            electric(5)
            if slot is not None:
                leave_high(slot, ed, hd)
            magnetic(0)
            electric(0)
            if slot is not None:
                leave_low(slot, ed)
            for x in range(1, 4):
                magnetic(x)
                electric(x)
            electric(4)
            if cut_to is not None:
                cut_latest(cut_to, ed)
            if slot is not None:
                leave_y(slot, ed, hd)

        def material_window():
            each(-1, lambda m: mat_copy(m).wait_recv())
            for v in range(3):
                mext[v, 1:7, 8:32, :] = mat[v]
                mext[v, 7, 8:32, :] = mx_r[0, v]
                mext[v, 0, 8:32, :] = mx_r[1, v]
                for x in range(6):
                    mext[v, x + 1, 32:33, :] = my_r[YE, v, x:x + 1, :]
                    mext[v, x + 1, 7:8, :] = my_r[YG, v, x:x + 1, :]
                mext[v, 0, 32:33, :] = my_r[C1, v, 0:1, :]
                mext[v, 7, 7:8, :] = my_r[C2, v, 0:1, :]
            for u2 in range(2):
                for v2 in range(2):
                    found = [jnp.zeros((8, 128), jnp.int32)] * 4
                    for u in range(-1, 4):
                        for v in range(3):
                            if u % 2 != u2 or v % 2 != v2:
                                continue
                            ok = (rows + 8 * u >= y0 - 1) & (rows + 8 * u < y0 + 9)
                            ok = ok & (lanes + 128 * v >= z0 - 1) & (lanes + 128 * v < z0 + 129)
                            for xr in range(4):
                                found[xr] = jnp.where(ok, mext[v, x0 + xr, 8 * u + 8:8 * u + 16, :], found[xr])
                    for xr in range(4):
                        wm_s[xr, u2, v2] = found[xr]
            win_copy().start()

        sets = [(e2.at[q], h2.at[q], p2.at[q]) for q in range(3)]
        e_in.wait()
        h_in.wait()
        all_here()
        leave_high(0, sets[0][0], sets[0][1])
        leave_low(0, sets[0][0])
        leave_y(0, sets[0][0], sets[0][1])
        each(1, lambda m: pos_copy(m).start(), AROUND)
        for cp in m_in:
            cp.wait()
        for v in range(3):
            for x in range(6):
                my_s[YE, v, x:x + 1, :] = mat[v, x, 0:1, :]
                my_s[YG, v, x:x + 1, :] = mat[v, x, 23:24, :]
            my_s[C1, v] = jnp.broadcast_to(mat[v, 5, 0:1, :], (8, 128))
            my_s[C2, v] = jnp.broadcast_to(mat[v, 0, 23:24, :], (8, 128))
        each(1, lambda m: mat_copy(m).start())
        tabs = tables(permit, conduct, relax, debye, 1.0, 0.5)

        def factors(x, carry):
            for u in range(3):
                for v in range(3):
                    here = mat[v, x, 8 * u:8 * u + 8, :]
                    for q in range(5):
                        k[(q, x) + tile_at(u, v)] = pick(tabs[q], here)
            return carry

        lax.fori_loop(0, 6, factors, 0)
        for i in range(2):
            for c in range(3):
                ini_s[c, i] = cut(lambda x, r, l: e2[0, c, x, r, l], i)
        ini_copy().start()
        p_in.wait()

        def advance(slot_in, source, target, **then):
            put_halos(slot_in, source[0], target[1])
            update(*source, *target, **then)

        def arrive(slot):
            each(-1, lambda m: halo_copy(m, slot).wait_recv())

        arrive(0)
        advance(0, sets[0], sets[1], slot=1, cut_to=0)
        learn_places()
        material_window()
        arrive(1)
        advance(1, sets[1], sets[2], slot=2, cut_to=1)
        arrive(2)
        advance(2, sets[2], (sets[0][0], sets[0][1], None), cut_to=2)
        del_copy(0).wait_recv()
        place(0, sets[1][0])
        mend_halos(1, 0)
        advance(1, sets[1], sets[0], slot=3)
        arrive(3)
        del_copy(1).wait_recv()
        place(1, sets[0][0])
        mend_halos(3, 1)
        advance(3, sets[0], sets[2])
        e, h, p = sets[2]
        h_out = pltpu.make_async_copy(h.at[:, 1:7, 8:32, :], out.at[0, 3:6], lsem.at[1])
        p_out = pltpu.make_async_copy(p, out.at[0, 6:9], lsem.at[2])
        h_out.start()
        p_out.start()
        del_copy(STEPS - 1).wait_recv()
        e_out = [pltpu.make_async_copy(e.at[:, x, 0:24, :], out.at[0, 0:3, x], lsem.at[12 + x]) for x in range(6)]
        place(STEPS - 1, e, e_out)

        each(1, lambda m: pos_copy(m).wait_send(), AROUND)
        each(1, lambda m: mat_copy(m).wait_send())
        win_copy().wait_send()
        for n in range(SETS):
            each(1, lambda m: halo_copy(m, n).wait_send())
        for n in range(STEPS):
            lat_copy(n).wait_send()
        ini_copy().wait_send()
        h_out.wait()
        p_out.wait()
        for cp in e_out:
            cp.wait()

    @pl.when(jnp.logical_not(coarse))
    def _():
        for ref in (ny_s, fy_s):
            ref[...] = jnp.zeros_like(ref)
        none = jnp.zeros((8, 128), jnp.int32)
        inside = (rows < ly) & (lanes < lz)
        two = lx == 2

        def inside_x(x):
            return jnp.where((x < 3) | two, 1, 0).astype(jnp.int32)

        tabs = tables(permit, conduct, relax, debye, 1.0 / 3.0, 0.25)
        spread = [3 * lanes + r for r in range(3)]
        phase = lanes % 3
        source = [(128 * ((phase + 3 - r) % 3) + lanes) // 3 for r in range(3)]

        def gather_in(ref, lead, ry):
            parts = [ref[(v,) + lead + (pl.ds(ry, 8, stride=3), slice(None))] for v in range(3)]
            tiles = []
            for r in range(3):
                at, src = spread[r] & 127, spread[r] >> 7
                got = [pick(part, at) for part in parts]
                tiles.append(jnp.where(src == 0, got[0], jnp.where(src == 1, got[1], got[2])))
            return tiles

        for cp in m_in:
            cp.wait()

        def fine_factors(x, carry):
            ok = inside & (inside_x(x) + none > 0)
            for ry in range(3):
                for r, here in enumerate(gather_in(mat, (x,), ry)):
                    ka, kc, kb, kf, kg = (pick(tabs[q], here) for q in range(5))
                    t = 3 * ry + r
                    fk[0, x, t] = ka
                    fk[1, x, t] = jnp.where(ok, kc, 0.0)
                    fk[2, x, t] = jnp.where(ok, kb * kg, 0.0)
                    fk[3, x, t] = kf
                    fk[4, x, t] = kg
                    fkr[x, t] = 1.0 / kg
            return carry

        lax.fori_loop(0, 6, fine_factors, 0)
        all_here()
        each(1, lambda m: pos_copy(m).start(), AROUND)
        for cp in f_in:
            cp.wait()
        for c in range(3):
            ff[c, 6] = jnp.zeros((9, 8, 128), F32)
            ff[3 + c, 0] = jnp.zeros((9, 8, 128), F32)

        def load_fine(x, carry):
            ok = inside & (inside_x(x) + none > 0)
            for c in range(9):
                for ry in range(3):
                    for r, here in enumerate(gather_in(stage, (c, x), ry)):
                        t = 3 * ry + r
                        if 3 <= c < 6:
                            ff[c, x + 1, t] = jnp.where(ok, 2.0 * here, 0.0)
                        elif c < 3:
                            ff[c, x, t] = jnp.where(ok, here, 0.0)
                        else:
                            ff[c, x, t] = jnp.where(ok, here * fkr[x, t], 0.0)
            return carry

        lax.fori_loop(0, 6, load_fine, 0)

        back_y, back_z = (8 - y0 % 8) % 8, (128 - z0 % 128) % 128

        def to_box(tile):
            return pltpu.roll(pltpu.roll(tile, back_y, 0), back_z, 1)

        def from_box(tile):
            return pltpu.roll(pltpu.roll(tile, y0 % 8, 0), z0 % 128, 1)

        edge_y = {0: rows == 0, 2: rows == ly - 1}
        edge_z = {0: lanes == 0, 2: lanes == lz - 1}

        def at_layer(x, carry):
            ok = inside & (inside_x(x) + none > 0)
            edge = jnp.where((x == 0) | (x == 3 * lx - 1), 1, 0).astype(jnp.int32)
            edge_x = ok & (edge + none > 0)
            ok_y = {q: m & ok for q, m in edge_y.items()}
            ok_z = {q: m & ok for q, m in edge_z.items()}
            xc = x // 3
            tiles = [(ry, rz) for ry in range(3) for rz in range(3)]
            E = {(c, t): ff[c, x, t] for c in range(3) for t in range(9)}
            F = {(c, t): ff[c, x + 1, t] for c in (1, 2) for t in range(9)}
            H = {}
            for ry, rz in tiles:
                t = 3 * ry + rz
                ex, ey, ez = (E[c, t] for c in range(3))
                if ry < 2:
                    exy, ezy = E[0, t + 3], E[2, t + 3]
                else:
                    exy, ezy = yfwd(E[0, rz]), yfwd(E[2, rz])
                if rz < 2:
                    exz, eyz = E[0, t + 1], E[1, t + 1]
                else:
                    exz, eyz = zfwd(E[0, 3 * ry]), zfwd(E[1, 3 * ry])
                H[0, t] = ff[3, x + 1, t] - ((ezy - ez) - (eyz - ey))
                H[1, t] = ff[4, x + 1, t] - ((exz - ex) - (F[2, t] - ez))
                H[2, t] = ff[5, x + 1, t] - ((F[1, t] - ey) - (exy - ex))
                for c in range(3):
                    ff[3 + c, x + 1, t] = H[c, t]
            for ry, rz in tiles:
                t = 3 * ry + rz
                hx, hy, hz = (H[c, t] for c in range(3))
                if ry > 0:
                    hxy, hzy = H[0, t - 3], H[2, t - 3]
                else:
                    hxy, hzy = ybwd(H[0, 6 + rz]), ybwd(H[2, 6 + rz])
                if rz > 0:
                    hxz, hyz = H[0, t - 1], H[1, t - 1]
                else:
                    hxz, hyz = zbwd(H[0, 3 * ry + 2]), zbwd(H[1, 3 * ry + 2])
                hyx, hzx = ff[4, x, t], ff[5, x, t]
                curls = ((hz - hzy) - (hy - hyz), (hx - hxz) - (hz - hzx), (hy - hyx) - (hx - hxy))
                ka, kc, kb, kf = (fk[q, x, t] for q in range(4))
                for c in range(3):
                    pol = ff[6 + c, x, t]
                    new = ka * E[c, t] + kc * curls[c] + kb * pol
                    marks = []
                    if c != 0:
                        marks.append(edge_x)
                    if c != 1 and ry in ok_y:
                        marks.append(ok_y[ry])
                    if c != 2 and rz in ok_z:
                        marks.append(ok_z[rz])
                    if marks:
                        new = jnp.where(functools.reduce(jnp.logical_or, marks), drv[c, xc], new)
                    ff[c, x, t] = new
                    ff[6 + c, x, t] = kf * pol + new
            return carry

        wrows = lax.broadcasted_iota(jnp.int32, (16, 256), 0)
        wlanes = lax.broadcasted_iota(jnp.int32, (16, 256), 1)
        at_y = y0 - 4 + ((wrows - (y0 - 4)) & 15)
        at_z = z0 - 64 + ((wlanes - (z0 - 64)) & 255)

        def w_in(at, low, size):
            return (at >= low) & (at < low + size)

        def twice(tile):
            return jnp.concatenate([jnp.concatenate([tile, tile], axis=1)] * 2, axis=0)

        def as_int(flag):
            return jnp.where(flag, 1, 0).astype(jnp.int32)

        def up_y(a):
            return pltpu.roll(a, 15, 0)

        def up_z(a):
            return pltpu.roll(a, 255, 1)

        def down_y(a):
            return pltpu.roll(a, 1, 0)

        def down_z(a):
            return pltpu.roll(a, 1, 1)

        region = w_in(at_y, y0, 8) & w_in(at_z, z0, 128)
        w_none = jnp.zeros((16, 256), jnp.int32)
        global_y = at_y + 24 * gb
        held_yz = (at_z >= 0) & (global_y >= 0)
        in_yz = held_yz & (at_z < 384) & (global_y < 24 * ny)

        def changes(d, reach):
            w = {}
            for c in range(3):
                for xr in range(-reach, 2 + reach):
                    w[c, xr] = jnp.where(region, twice(del_s[d, c, xr]), 0.0) if 0 <= xr < 2 else jnp.zeros((16, 256), F32)
            for m, (dx, dy) in enumerate(AROUND):
                far_x, far_y, far_z = place_of[m, 0, 0], place_of[m, 1, 0], place_of[m, 2, 0]
                ok = w_in(at_z, far_z, 128)
                if dy == 0:
                    ok = ok & w_in(at_y, far_y, 8)
                else:
                    ok = ok & w_in(at_y, 24 if dy < 0 else -2, 2)
                for xr in {0: range(-reach, 2 + reach), -1: range(2, 2 + reach), 1: range(-reach, 0)}[dx]:
                    i = x0 + xr + 6 * dx - far_x
                    s0 = jnp.where(i == 0, 1.0, 0.0).astype(F32)
                    s1 = jnp.where(i == 1, 1.0, 0.0).astype(F32)
                    for c in range(3):
                        if dy == 0:
                            tile = s0 * fx_r[m // 2, d, c, 0] + s1 * fx_r[m // 2, d, c, 1]
                        else:
                            pair = [s0 * fy_r[m, d, 6 * r + 2 * c:6 * r + 2 * c + 1, :]
                                    + s1 * fy_r[m, d, 6 * r + 2 * c + 1:6 * r + 2 * c + 2, :] for r in range(2)]
                            low = 0 if dy < 0 else 6
                            tile = jnp.where(rows == low, jnp.broadcast_to(pair[0], (8, 128)),
                                             jnp.broadcast_to(pair[1], (8, 128)))
                        w[c, xr] = w[c, xr] + jnp.where(ok, twice(tile), 0.0)
            return w

        def turned_ahead(w, xr):
            ex, ey, ez = (w[c, xr] for c in range(3))
            moved = ((up_y(ez) - ez) - (up_z(ey) - ey), (up_z(ex) - ex) - (w[2, xr + 1] - ez),
                     (w[1, xr + 1] - ey) - (up_y(ex) - ex))
            ok = held_yz & (as_int(x0 + xr + 6 * ga >= 0) + w_none > 0)
            return [jnp.where(ok, -0.5 * part, 0.0) for part in moved]

        def turned_behind(hh, xr):
            hx, hy, hz = (hh[c, xr] for c in range(3))
            return ((hz - down_y(hz)) - (hy - down_z(hy)), (hx - down_z(hx)) - (hz - hh[2, xr - 1]),
                    (hy - hh[1, xr - 1]) - (hx - down_y(hx)))

        def on_region(wide):
            kept = jnp.where(region, wide, 0.0)
            return (kept[0:8, 0:128] + kept[0:8, 128:256]) + (kept[8:16, 0:128] + kept[8:16, 128:256])

        def window_factors():
            win_copy().wait_recv()
            slab = tables(permit, conduct, relax, debye, 1.0, 0.5)
            for xr in range(4):
                for u2 in range(2):
                    for v2 in range(2):
                        here = wm_r[xr, u2, v2]
                        spot = (xr, slice(8 * u2, 8 * u2 + 8), slice(128 * v2, 128 * v2 + 128))
                        for q in range(2):
                            kw[(q,) + spot] = pick(slab[q], here)
                        kw[(2,) + spot] = pick(slab[2], here) * pick(slab[4], here)

        def respond(n):
            each(-1, lambda m: box_copy(m, n - 1).wait_recv(), AROUND)
            hh = {}
            if n == 1:
                w = changes(0, 2)
                for xr in range(-2, 3):
                    for c, part in enumerate(turned_ahead(w, xr)):
                        hh[c, xr] = part
                        if -1 <= xr <= 1:
                            hw[c, xr + 1] = part
                layers = range(-1, 3)
            else:
                w = changes(1, 1)
                for c in range(3):
                    for xr in range(-1, 3):
                        w[c, xr] = w[c, xr] + ew[c, xr + 1]
                for xr in range(-1, 2):
                    for c, part in enumerate(turned_ahead(w, xr)):
                        hh[c, xr] = hw[c, xr + 1] + part
                layers = range(2)
            for xr in layers:
                ok = in_yz & (as_int((x0 + xr + 6 * ga >= 0) & (x0 + xr + 6 * ga < 6 * nx)) + w_none > 0)
                for c, curl in enumerate(turned_behind(hh, xr)):
                    value = kw[0, xr + 1] * w[c, xr] + kw[1, xr + 1] * curl
                    if n == 1:
                        value = jnp.where(ok, value, 0.0)
                        ew[c, xr + 1] = value
                    else:
                        value = value + kw[2, xr + 1] * ew[c, xr + 1]
                    if 0 <= xr < 2:
                        ear[1, c, xr] = to_box(lat_r[n, c, xr] + on_region(value))

        learn_places()
        ini_copy().wait_recv()
        for c in range(3):
            for i in range(2):
                ear[0, c, i] = to_box(ini_r[c, i])

        for n in range(STEPS):
            lat_copy(n).wait_recv()
            if n == 0:
                for c in range(3):
                    for i in range(2):
                        ear[1, c, i] = to_box(lat_r[0, c, i])
            else:
                if n == 1:
                    window_factors()
                respond(n)

            def substep(s, carry):
                weight = (s + 1).astype(F32) * (1.0 / 3.0)
                drv[...] = ear[0] + weight * (ear[1] - ear[0])
                return lax.fori_loop(0, 6, at_layer, carry, unroll=True)

            lax.fori_loop(0, 3, substep, 0)
            for i in range(2):
                ok = inside & (inside_x(3 * i) + none > 0)
                for c in range(3):
                    total = functools.reduce(
                        jnp.add, [ff[c, 3 * i + j, t] for j in range(3) for t in range(9)])
                    latest = ear[1, c, i]
                    delta = jnp.where(ok, total * (1.0 / 27.0) - latest, 0.0)
                    ear[0, c, i] = latest + delta
                    del_s[n, c, i] = from_box(delta)
            if n + 1 < STEPS:
                for r in range(2):
                    low = jnp.where(y0 <= r, 1.0, 0.0).astype(F32)
                    high = jnp.where(y0 >= 15 + r, 1.0, 0.0).astype(F32)
                    for c in range(3):
                        for i in range(2):
                            row = 6 * r + 2 * c + i
                            fy_s[0, n, row:row + 1, :] = low * del_s[n, c, i, r:r + 1, :]
                            fy_s[1, n, row:row + 1, :] = high * del_s[n, c, i, 6 + r:7 + r, :]
                for m in (4, 5, 6, 7, 0, 2, 1, 3):
                    dx, dy = AROUND[m]

                    @pl.when(exists(dx, dy))
                    def _():
                        box_copy(m, n).start()
                low, high = (jnp.where(x0 == q, 1.0, 0.0).astype(F32) for q in (0, 4))
                left, right = (jnp.where(y0 == q, 1.0, 0.0).astype(F32) for q in (0, 16))
                for c in range(3):
                    nx_s[0, n, c] = low * del_s[n, c, 0]
                    nx_s[1, n, c] = high * del_s[n, c, 1]
                    for i in range(2):
                        ny_s[0, n, 2 * c + i:2 * c + i + 1, :] = left * del_s[n, c, i, 0:1, :]
                        ny_s[1, n, 2 * c + i:2 * c + i + 1, :] = right * del_s[n, c, i, 7:8, :]
                nd_s[0, n] = jnp.broadcast_to((high * left) * del_s[n, 0, 1, 0:1, :], (8, 128))
                nd_s[1, n] = jnp.broadcast_to((low * right) * del_s[n, 1, 0, 7:8, :], (8, 128))
                del_copy(n).start()
                each(1, lambda m: near_copy(m, n).start())
            else:
                del_copy(n).start()

        def save_fine(x, carry):
            for c in range(9):
                for ry in range(3):
                    lift = 1 if 3 <= c < 6 else 0
                    parts = [ff[c, x + lift, 3 * ry + r] for r in range(3)]
                    if c >= 6:
                        parts = [part * fk[4, x, 3 * ry + r] for r, part in enumerate(parts)]
                    got = [pick(part, source[r]) for r, part in enumerate(parts)]
                    for v in range(3):
                        a, b, d = (got[(q + 2 * v) % 3] for q in range(3))
                        value = jnp.where(phase == 0, a, jnp.where(phase == 1, b, d))
                        if lift:
                            value = 0.5 * value
                        stage[v, c, x, pl.ds(ry, 8, stride=3), :] = value
            return carry

        lax.fori_loop(0, 6, save_fine, 0)
        f_out = [pltpu.make_async_copy(stage.at[v], out.at[0, :, :, :, pl.ds(128 * v, 128)], lsem.at[v]) for v in range(3)]
        for cp in f_out:
            cp.start()
        each(1, lambda m: pos_copy(m).wait_send(), AROUND)
        for n in range(STEPS):
            del_copy(n).wait_send()
            if n + 1 < STEPS:
                each(1, lambda m: near_copy(m, n).wait_send())
                each(1, lambda m: box_copy(m, n).wait_send(), AROUND)
        for cp in f_out:
            cp.wait()


def solution(mesh):
    nx, ny = mesh.shape["gx"], mesh.shape["gy"]

    def body(fields, material, permit, conduct, relax, debye, subgrids):
        vm = pltpu.VMEM
        dma = pltpu.SemaphoreType.DMA
        slots = [
            vm((SETS, 2, 24, 384), F32), vm((SETS, 2, 8, 384), F32),
            vm((SETS, 2, 24, 384), F32), vm((SETS, 2, 8, 384), F32),
            vm((SETS, 8, 384), F32), vm((SETS, 8, 384), F32),
        ]
        region = (3, 2, 8, 128)
        near = [vm((2, STEPS - 1, 3, 8, 128), F32), vm((2, STEPS - 1, 8, 128), F32), vm((2, STEPS - 1, 8, 128), F32)]
        return pl.pallas_call(
            functools.partial(kernel, nx, ny),
            out_shape=jax.ShapeDtypeStruct(fields.shape, F32),
            in_specs=[pl.BlockSpec(memory_space=pl.ANY)] * 7,
            out_specs=pl.BlockSpec(memory_space=pl.ANY),
            scratch_shapes=[
                *[pltpu.SMEM((8,), F32)] * 4, pltpu.SMEM((1, 1, 6), jnp.int32),
                vm((3, 3, 7, 32, 384), F32), vm((3, 3, 7, 32, 384), F32), vm((3, 3, 6, 24, 384), F32), vm((5, 6, 24, 384), F32),
                vm((3, 9, 6, 24, 128), F32), vm((3, 6, 24, 128), jnp.int32),
                vm((9, 7, 9, 8, 128), F32), vm((5, 6, 9, 8, 128), F32),
                vm((5, 16, 384), F32), vm((2, 8, 384), F32), vm((2, 8, 384), F32), vm((3, 32, 384), F32), vm((3, 8, 384), F32),
                vm((2,) + region, F32), vm(region, F32), vm((6, 9, 8, 128), F32),
                vm((3, 8, 40, 128), jnp.int32), vm((3, 4, 16, 256), F32), vm((3, 3, 16, 256), F32), vm((3, 4, 16, 256), F32),
                *slots, *slots,
                vm((STEPS,) + region, F32), vm((STEPS,) + region, F32), vm(region, F32), vm(region, F32),
                vm((STEPS,) + region, F32), vm((STEPS,) + region, F32),
                *near, *near, vm((8, 128), jnp.int32), vm((8, 8, 128), jnp.int32), pltpu.SMEM((8, 8, 128), jnp.int32),
                vm((2, STEPS - 1, 16, 128), F32), vm((2, STEPS - 1) + region, F32), vm((8, STEPS - 1, 16, 128), F32),
                vm((6, 3, 8, 128), jnp.int32), vm((2, 3, 24, 128), jnp.int32), vm((6, 3, 8, 128), jnp.int32),
                vm((4, 2, 2, 8, 128), jnp.int32), vm((4, 2, 2, 8, 128), jnp.int32),
                dma((18,)), dma((6, SETS)), dma((6, SETS)),
                dma((STEPS + 1,)), dma((STEPS + 1,)), dma((STEPS,)), dma((STEPS,)),
                dma((6, STEPS)), dma((6, STEPS)), dma((8,)), dma((8,)),
                dma((8, STEPS)), dma((8, STEPS)), dma((6,)), dma((6,)), dma((1,)), dma((1,)),
            ],
            compiler_params=pltpu.CompilerParams(
                collective_id=0, has_side_effects=True, vmem_limit_bytes=63 * 1024 * 1024),
        )(fields, material, permit, conduct, relax, debye, subgrids)

    return jax.shard_map(
        body,
        mesh=mesh,
        in_specs=(P("grid", None, "gx", "gy", None), P("grid", "gx", "gy", None), P(), P(), P(), P(), P("gx", "gy", None)),
        out_specs=P("grid", None, "gx", "gy", None),
        check_vma=False,
    )
```

```python
import functools

import jax
import jax.numpy as jnp
from jax import lax
from jax.experimental import pallas as pl
from jax.experimental.pallas import tpu as pltpu
from jax.sharding import PartitionSpec as P

MESH = pl.DeviceIdType.MESH
STEPS = 3
F32 = jnp.float32

TO_NEXT = ((-1, 0), (0, -1), (1, 0), (0, 1), (1, -1), (-1, 1))
XE, YE, XG, YG, C1, C2 = range(6)
AROUND = TO_NEXT + ((1, 1), (-1, -1))
SETS = STEPS + 1


def lane_iota():
    return lax.broadcasted_iota(jnp.int32, (8, 128), 1)


def row_iota():
    return lax.broadcasted_iota(jnp.int32, (8, 128), 0)


def pick(tile, index):
    return jnp.take_along_axis(tile, index, axis=1, mode="promise_in_bounds")


def zfwd(v):
    n = v.shape[-1]
    lanes = lax.broadcasted_iota(jnp.int32, v.shape, v.ndim - 1)
    return jnp.where(lanes == n - 1, 0.0, pltpu.roll(v, n - 1, v.ndim - 1))


def zbwd(v):
    lanes = lax.broadcasted_iota(jnp.int32, v.shape, v.ndim - 1)
    return jnp.where(lanes == 0, 0.0, pltpu.roll(v, 1, v.ndim - 1))


def yfwd(t):
    return jnp.where(row_iota() == 7, 0.0, pltpu.roll(t, 7, 0))


def ybwd(t):
    return jnp.where(row_iota() == 0, 0.0, pltpu.roll(t, 1, 0))


def tables(permit, conduct, relax, debye, factor, courant):
    lane = lane_iota()

    def spread(ref):
        out = jnp.ones((8, 128), F32)
        for m in range(8):
            out = jnp.where(lane == m, ref[m], out)
        return out

    eps = spread(permit)
    damping = spread(conduct) * factor / (2.0 * eps)
    f0 = (1.0 - damping) / (1.0 + damping)
    f1 = 1.0 / (eps * (1.0 + damping))
    f2 = spread(relax) * factor
    f3 = jnp.exp(-f2)
    f4 = spread(debye)
    return f0 - f1 * f2 * f4, courant * f1, f1 * f2, f3, (1.0 - f3) * f4


def kernel(
    nx, ny,
    fields, material, permit_in, conduct_in, relax_in, debye_in, subgrids_in, out,
    permit, conduct, relax, debye, subgrids, e2, h2, p2, k, stage, mat, ff, fk, pk, pln, own, dl, pd, ear, drv, fkr, mext, ew, hw, kw,
    xe_s, ye_s, xg_s, yg_s, c1_s, c2_s,
    xe_r, ye_r, xg_r, yg_r, c1_r, c2_r,
    lat_s, lat_r, ini_s, ini_r, del_s, del_r,
    nx_s, ny_s, nd_s, nx_r, ny_r, nd_r, pos_s, pos_r, place_of,
    fy_s, fx_r, fy_r, my_s, mx_r, my_r, wm_s, wm_r,
    lsem, hs, hr, bs, br, ds, dr, ns, nr, ps, pr, fs, fr, ms, mr, ws, wr,
):
    grid = lax.axis_index("grid")
    ga = lax.axis_index("gx")
    gb = lax.axis_index("gy")
    coarse = grid == 0
    sends = (xe_s, ye_s, xg_s, yg_s, c1_s, c2_s)
    recvs = (xe_r, ye_r, xg_r, yg_r, c1_r, c2_r)
    delta_s = (nx_s.at[0], ny_s.at[0], nx_s.at[1], ny_s.at[1], nd_s.at[0], nd_s.at[1])
    delta_r = (nx_r.at[0], ny_r.at[0], nx_r.at[1], ny_r.at[1], nd_r.at[0], nd_r.at[1])

    def exists(dx, dy):
        return (ga + dx >= 0) & (ga + dx < nx) & (gb + dy >= 0) & (gb + dy < ny)

    def device(g, dx, dy):
        return (g, jnp.clip(ga + dx, 0, nx - 1), jnp.clip(gb + dy, 0, ny - 1))

    partner = (1 - grid, ga, gb)
    rows, lanes = row_iota(), lane_iota()

    e_in = pltpu.make_async_copy(fields.at[0, 0:3], e2.at[0, :, 0:6, 0:24, :], lsem.at[0])
    h_in = pltpu.make_async_copy(fields.at[0, 3:6], h2.at[0, :, 1:7, 8:32, :], lsem.at[1])
    p_in = pltpu.make_async_copy(fields.at[0, 6:9], p2.at[0], lsem.at[2])
    f_in = [pltpu.make_async_copy(fields.at[0, :, :, :, pl.ds(128 * v, 128)], stage.at[v], lsem.at[v]) for v in range(3)]
    m_in = [pltpu.make_async_copy(material.at[0, :, :, pl.ds(128 * v, 128)], mat.at[v], lsem.at[3 + v]) for v in range(3)]

    @pl.when(coarse)
    def _():
        for cp in (e_in, h_in, p_in):
            cp.start()

    @pl.when(jnp.logical_not(coarse))
    def _():
        for cp in f_in:
            cp.start()

    for cp in m_in:
        cp.start()
    scalars = [
        pltpu.make_async_copy(a, b, lsem.at[7 + q])
        for q, (a, b) in enumerate(((permit_in, permit), (conduct_in, conduct), (relax_in, relax), (debye_in, debye),
                                    (subgrids_in, subgrids)))]
    for cp in scalars:
        cp.start()
    for ref in (nx_r, ny_r, nd_r, pos_r, fx_r, fy_r):
        ref[...] = jnp.zeros_like(ref)

    @pl.when(coarse)
    def _():
        for ref in (mx_r, my_r) + recvs:
            ref[...] = jnp.zeros_like(ref)

    barrier = pltpu.get_barrier_semaphore()
    pl.semaphore_signal(barrier, inc=1, device_id=partner, device_id_type=MESH)
    count = jnp.int32(1)
    for dx, dy in AROUND:
        count = count + exists(dx, dy).astype(jnp.int32)

        @pl.when(exists(dx, dy))
        def _():
            pl.semaphore_signal(barrier, inc=1, device_id=(grid, ga + dx, gb + dy), device_id_type=MESH)

    @pl.when(coarse)
    def _():
        for ref in (ye_s, yg_s, pk, pln, own, my_s, mext):
            ref[...] = jnp.zeros_like(ref)

    for cp in scalars:
        cp.wait()
    x0, y0, z0 = subgrids[0, 0, 0], subgrids[0, 0, 1], subgrids[0, 0, 2]
    lx, ly, lz = subgrids[0, 0, 3], subgrids[0, 0, 4], subgrids[0, 0, 5]
    pos_s[...] = jnp.where(rows == 0, x0, jnp.where(rows == 1, y0, z0))

    def all_here():
        pl.semaphore_wait(barrier, count)

    def remote(src, dst, send, recv, target):
        return pltpu.make_async_remote_copy(
            src_ref=src, dst_ref=dst, send_sem=send, recv_sem=recv, device_id=target, device_id_type=MESH)

    def halo_copy(m, n):
        if m in (C1, C2):
            return remote(sends[m].at[n, 0:1], recvs[m].at[n, 0:1], hs.at[m, n], hr.at[m, n], device(grid, *TO_NEXT[m]))
        return remote(sends[m].at[n], recvs[m].at[n], hs.at[m, n], hr.at[m, n], device(grid, *TO_NEXT[m]))

    def lat_copy(n):
        return remote(lat_s.at[n], lat_r.at[n], bs.at[n], br.at[n], partner)

    def ini_copy():
        return remote(ini_s, ini_r, bs.at[STEPS], br.at[STEPS], partner)

    def del_copy(n):
        return remote(del_s.at[n], del_r.at[n], ds.at[n], dr.at[n], partner)

    def near_copy(m, n):
        return remote(delta_s[m].at[n], delta_r[m].at[n], ns.at[m, n], nr.at[m, n], device(0, *TO_NEXT[m]))

    def box_copy(m, n):
        dx, dy = AROUND[m]
        if dy == 0:
            src, dst = del_s.at[n], fx_r.at[m // 2, n]
        else:
            src, dst = fy_s.at[0 if dy < 0 else 1, n], fy_r.at[m, n]
        return remote(src, dst, fs.at[m, n], fr.at[m, n], device(1, dx, dy))

    def pos_copy(m):
        return remote(pos_s, pos_r.at[m], ps.at[m], pr.at[m], device(grid, *AROUND[m]))

    def mat_copy(m):
        dx, dy = TO_NEXT[m]
        if dy == 0:
            src, dst = mat.at[:, 0 if dx < 0 else 5], mx_r.at[m // 2]
        else:
            src, dst = my_s.at[m], my_r.at[m]
        return remote(src, dst, ms.at[m], mr.at[m], device(0, dx, dy))

    def win_copy():
        return remote(wm_s, wm_r, ws.at[0], wr.at[0], partner)

    def each(turn, fun, over=TO_NEXT):
        for m, (dx, dy) in enumerate(over):
            @pl.when(exists(turn * dx, turn * dy))
            def _():
                fun(m)

    def learn_places():
        each(-1, lambda m: pos_copy(m).wait_recv(), AROUND)
        cp = pltpu.make_async_copy(pos_r, place_of, lsem.at[6])
        cp.start()
        cp.wait()

    def row_in(low, u):
        return (rows + 8 * u >= low) & (rows + 8 * u < low + 8)

    def lane_in(low, v):
        return (lanes + 128 * v >= low) & (lanes + 128 * v < low + 128)

    def tile_at(u, v):
        return (slice(8 * u, 8 * u + 8), slice(128 * v, 128 * v + 128))

    @pl.when(coarse)
    def _():
        flag_x = jnp.where(ga > 0, 1.0, 0.0).astype(F32)
        flag_y = jnp.where(gb > 0, 1.0, 0.0).astype(F32)
        row_ok = [row_in(y0, u) for u in range(3)]
        lane_ok = [lane_in(z0, v) for v in range(3)]
        wide = lax.broadcasted_iota(jnp.int32, (24, 384), 0)

        def cut(load, i):
            tile = jnp.zeros((8, 128), F32)
            for u in range(3):
                for v in range(3):
                    tile = jnp.where(row_ok[u] & lane_ok[v], load(x0 + i, *tile_at(u, v)), tile)
            return tile

        def cut_latest(n, e):
            for i in range(2):
                for c in range(3):
                    lat_s[n, c, i] = cut(lambda x, r, l: e[c, x, r, l], i)
            lat_copy(n).start()

        def place(n, e, done=None):
            for x in range(6):
                s0 = jnp.where(x == x0, 1.0, 0.0).astype(F32)
                s1 = jnp.where(x == x0 + 1, 1.0, 0.0).astype(F32)
                for c in range(3):
                    tile = s0 * del_r[n, c, 0] + s1 * del_r[n, c, 1]
                    for u in range(3):
                        for v in range(3):
                            spot = (c, x) + tile_at(u, v)
                            e[spot] = e[spot] + jnp.where(row_ok[u] & lane_ok[v], tile, 0.0)
                if done is not None:
                    done[x].start()

        def send_halo(m, n):
            @pl.when(exists(*TO_NEXT[m]))
            def _():
                halo_copy(m, n).start()

        def leave_high(n, e, h):
            c1_s[n, 0:1, :] = e[0, 5, 0:1, :]
            send_halo(C1, n)
            ex, ey, ez = e[0, 5, 0:24, :], e[1, 5, 0:24, :], e[2, 5, 0:24, :]
            exy = jnp.where(wide == 23, 0.0, e[0, 5, 1:25, :])
            xg_s[n, 0] = h[1, 6, 8:32, :] - 0.5 * (zfwd(ex) - ex + ez)
            xg_s[n, 1] = h[2, 6, 8:32, :] + 0.5 * (ey + exy - ex)
            send_halo(XG, n)

        def leave_low(n, e):
            c2_s[n, 0:1, :] = e[1, 0, 23:24, :]
            send_halo(C2, n)
            xe_s[n] = e[1:3, 0, 0:24, :]
            send_halo(XE, n)

        def leave_y(n, e, h):
            for x in range(6):
                ye_s[n, 0, x:x + 1, :] = e[0, x, 0:1, :]
                ye_s[n, 1, x:x + 1, :] = e[2, x, 0:1, :]
            send_halo(YE, n)
            for x in range(6):
                for c in range(3):
                    pk[c, x:x + 1, :] = e[c, x, 23:24, :]
                pk[3, x:x + 1, :] = h[0, x + 1, 31:32, :]
                pk[4, x:x + 1, :] = h[2, x + 1, 31:32, :]
            px, py, pz = pk[0, 0:8, :], pk[1, 0:8, :], pk[2, 0:8, :]
            yg_s[n, 0] = pk[3, 0:8, :] + 0.5 * (pz + zfwd(py) - py)
            yg_s[n, 1] = pk[4, 0:8, :] - 0.5 * (pk[1, 1:9, :] - py + px)
            send_halo(YG, n)

        def put_halos(n, e, h):
            e[1:3, 6, 0:24, :] = xe_r[n]
            h[1, 0, 8:32, :] = flag_x * (xg_r[n, 0] + 0.5 * e[2, 0, 0:24, :])
            h[2, 0, 8:32, :] = flag_x * (xg_r[n, 1] - 0.5 * e[1, 0, 0:24, :])
            for x in range(6):
                own[0, x:x + 1, :] = e[0, x, 0:1, :]
                own[1, x:x + 1, :] = e[2, x, 0:1, :]
            pln[0] = flag_y * (yg_r[n, 0] - 0.5 * own[1])
            pln[1] = flag_y * (yg_r[n, 1] + 0.5 * own[0])
            for x in range(6):
                e[0, x, 24:25, :] = ye_r[n, 0, x:x + 1, :]
                e[2, x, 24:25, :] = ye_r[n, 1, x:x + 1, :]
                h[0, x + 1, 7:8, :] = pln[0, x:x + 1, :]
                h[2, x + 1, 7:8, :] = pln[1, x:x + 1, :]

        def put_corners(n, h):
            h[2, 0, 31:32, :] = h[2, 0, 31:32, :] + (0.5 * flag_x) * c1_r[n, 0:1, :]
            h[2, 6, 7:8, :] = h[2, 6, 7:8, :] - (0.5 * flag_y) * c2_r[n, 0:1, :]

        def mend_halos(n, d):
            each(-1, lambda m: near_copy(m, d).wait_recv())
            for u in range(3):
                for v in range(3):
                    spot = tile_at(u, v)
                    ok = row_in(place_of[XE, 1, 0], u) & lane_in(place_of[XE, 2, 0], v)
                    for q in range(2):
                        xe_r[(n, q) + spot] = xe_r[(n, q) + spot] + jnp.where(ok, nx_r[0, d, 1 + q], 0.0)
                    ok = row_in(place_of[XG, 1, 0], u) & lane_in(place_of[XG, 2, 0], v)
                    for c in range(3):
                        dl[(c,) + spot] = jnp.where(ok, nx_r[1, d, c], 0.0)
            tx, ty, tz = dl[0, 0:24, :], dl[1, 0:24, :], dl[2, 0:24, :]
            dl[0, 24:32, :] = jnp.zeros((8, 384), F32)
            xg_r[n, 0] = xg_r[n, 0] - 0.5 * (zfwd(tx) - tx + tz)
            xg_r[n, 1] = xg_r[n, 1] + 0.5 * (ty + dl[0, 1:25, :] - tx)
            for m, keep in ((YE, ny_r.at[0]), (YG, ny_r.at[1])):
                at = place_of[m, 0, 0]
                for c in range(3):
                    two = [jnp.broadcast_to(keep[d, 2 * c + i:2 * c + i + 1, :], (8, 128)) for i in range(2)]
                    both = jnp.where(rows == at, two[0], jnp.where(rows == at + 1, two[1], 0.0))
                    for v in range(3):
                        pd[c, :, 128 * v:128 * v + 128] = jnp.where(lane_in(place_of[m, 2, 0], v), both, 0.0)
                if m == YE:
                    ye_r[n, 0] = ye_r[n, 0] + pd[0]
                    ye_r[n, 1] = ye_r[n, 1] + pd[2]
                else:
                    yg_r[n, 0] = yg_r[n, 0] + 0.5 * (pd[2] + zfwd(pd[1]) - pd[1])
                    yg_r[n, 1] = yg_r[n, 1] - 0.5 * (pltpu.roll(pd[1], 7, 0) - pd[1] + pd[0])
            for m, ref, keep in ((C1, c1_r, nd_r.at[0]), (C2, c2_r, nd_r.at[1])):
                for v in range(3):
                    spot = (n, slice(0, 8), slice(128 * v, 128 * v + 128))
                    ref[spot] = ref[spot] + jnp.where(lane_in(place_of[m, 2, 0], v), keep[d], 0.0)

        def update(e, h, p, ed, hd, pd_, corners, slot=None, cut_to=None):
            def magnetic(x):
                for u in range(3):
                    r = slice(8 * u, 8 * u + 8)
                    ra = slice(8 * u + 1, 8 * u + 9)
                    rh = slice(8 * u + 8, 8 * u + 16)
                    ex, ey, ez = e[0, x, r, :], e[1, x, r, :], e[2, x, r, :]
                    hd[0, x + 1, rh, :] = h[0, x + 1, rh, :] - 0.5 * ((e[2, x, ra, :] - ez) - (zfwd(ey) - ey))
                    hd[1, x + 1, rh, :] = h[1, x + 1, rh, :] - 0.5 * ((zfwd(ex) - ex) - (e[2, x + 1, r, :] - ez))
                    hd[2, x + 1, rh, :] = h[2, x + 1, rh, :] - 0.5 * ((e[1, x + 1, r, :] - ey) - (e[0, x, ra, :] - ex))

            def electric(x):
                for u in range(3):
                    r = slice(8 * u, 8 * u + 8)
                    rh = slice(8 * u + 8, 8 * u + 16)
                    rb = slice(8 * u + 7, 8 * u + 15)
                    hx, hy, hz = hd[0, x + 1, rh, :], hd[1, x + 1, rh, :], hd[2, x + 1, rh, :]
                    cx = (hz - hd[2, x + 1, rb, :]) - (hy - zbwd(hy))
                    cy = (hx - zbwd(hx)) - (hz - hd[2, x, rh, :])
                    cz = (hy - hd[1, x, rh, :]) - (hx - hd[0, x + 1, rb, :])
                    ka, kc, kb, kf, kg = (k[q, x, r, :] for q in range(5))
                    for c, curl in enumerate((cx, cy, cz)):
                        pol = p[c, x, r, :]
                        new = ka * e[c, x, r, :] + kc * curl + kb * pol
                        ed[c, x, r, :] = new
                        if pd_ is not None:
                            pd_[c, x, r, :] = kf * pol + kg * new

            for x in range(6):
                magnetic(x)
                if 1 < x:
                    electric(x - 1)
            corners()
            electric(5)
            if slot is not None:
                leave_high(slot, ed, hd)
            electric(0)
            if slot is not None:
                leave_low(slot, ed)
            if cut_to is not None:
                cut_latest(cut_to, ed)
            if slot is not None:
                leave_y(slot, ed, hd)

        def material_window():
            each(-1, lambda m: mat_copy(m).wait_recv())
            for v in range(3):
                mext[v, 1:7, 8:32, :] = mat[v]
                mext[v, 7, 8:32, :] = mx_r[0, v]
                mext[v, 0, 8:32, :] = mx_r[1, v]
                for x in range(6):
                    mext[v, x + 1, 32:33, :] = my_r[YE, v, x:x + 1, :]
                    mext[v, x + 1, 7:8, :] = my_r[YG, v, x:x + 1, :]
                mext[v, 0, 32:33, :] = my_r[C1, v, 0:1, :]
                mext[v, 7, 7:8, :] = my_r[C2, v, 0:1, :]
            for u2 in range(2):
                for v2 in range(2):
                    found = [jnp.zeros((8, 128), jnp.int32)] * 4
                    for u in range(-1, 4):
                        for v in range(3):
                            if u % 2 != u2 or v % 2 != v2:
                                continue
                            ok = (rows + 8 * u >= y0 - 1) & (rows + 8 * u < y0 + 9)
                            ok = ok & (lanes + 128 * v >= z0 - 1) & (lanes + 128 * v < z0 + 129)
                            for xr in range(4):
                                found[xr] = jnp.where(ok, mext[v, x0 + xr, 8 * u + 8:8 * u + 16, :], found[xr])
                    for xr in range(4):
                        wm_s[xr, u2, v2] = found[xr]
            win_copy().start()

        sets = [(e2.at[q], h2.at[q], p2.at[q]) for q in range(3)]
        e_in.wait()
        h_in.wait()
        all_here()
        leave_high(0, sets[0][0], sets[0][1])
        leave_low(0, sets[0][0])
        leave_y(0, sets[0][0], sets[0][1])
        each(1, lambda m: pos_copy(m).start(), AROUND)
        for cp in m_in:
            cp.wait()
        for v in range(3):
            for x in range(6):
                my_s[YE, v, x:x + 1, :] = mat[v, x, 0:1, :]
                my_s[YG, v, x:x + 1, :] = mat[v, x, 23:24, :]
            my_s[C1, v] = jnp.broadcast_to(mat[v, 5, 0:1, :], (8, 128))
            my_s[C2, v] = jnp.broadcast_to(mat[v, 0, 23:24, :], (8, 128))
        each(1, lambda m: mat_copy(m).start())
        tabs = tables(permit, conduct, relax, debye, 1.0, 0.5)

        def factors(x, carry):
            for u in range(3):
                for v in range(3):
                    here = mat[v, x, 8 * u:8 * u + 8, :]
                    for q in range(5):
                        k[(q, x) + tile_at(u, v)] = pick(tabs[q], here)
            return carry

        lax.fori_loop(0, 6, factors, 0)
        for i in range(2):
            for c in range(3):
                ini_s[c, i] = cut(lambda x, r, l: e2[0, c, x, r, l], i)
        ini_copy().start()
        p_in.wait()

        def advance(slot_in, source, target, fresh, **then):
            def corners():
                if fresh:
                    arrive(slot_in, (C1, C2))
                put_corners(slot_in, target[1])

            if fresh:
                arrive(slot_in, (XE, YE, XG, YG))
            put_halos(slot_in, source[0], target[1])
            update(*source, *target, corners, **then)

        def arrive(slot, which):
            for m in which:
                dx, dy = TO_NEXT[m]

                @pl.when(exists(-dx, -dy))
                def _():
                    halo_copy(m, slot).wait_recv()

        advance(0, sets[0], sets[1], True, slot=1, cut_to=0)
        learn_places()
        material_window()
        advance(1, sets[1], sets[2], True, slot=2, cut_to=1)
        advance(2, sets[2], (sets[0][0], sets[0][1], None), True, cut_to=2)
        del_copy(0).wait_recv()
        place(0, sets[1][0])
        mend_halos(1, 0)
        advance(1, sets[1], sets[0], False, slot=3)
        arrive(3, range(6))
        del_copy(1).wait_recv()
        place(1, sets[0][0])
        mend_halos(3, 1)
        advance(3, sets[0], sets[2], False)
        e, h, p = sets[2]
        h_out = pltpu.make_async_copy(h.at[:, 1:7, 8:32, :], out.at[0, 3:6], lsem.at[1])
        p_out = pltpu.make_async_copy(p, out.at[0, 6:9], lsem.at[2])
        h_out.start()
        p_out.start()
        del_copy(STEPS - 1).wait_recv()
        e_out = [pltpu.make_async_copy(e.at[:, x, 0:24, :], out.at[0, 0:3, x], lsem.at[12 + x]) for x in range(6)]
        place(STEPS - 1, e, e_out)

        each(1, lambda m: pos_copy(m).wait_send(), AROUND)
        each(1, lambda m: mat_copy(m).wait_send())
        win_copy().wait_send()
        for n in range(SETS):
            each(1, lambda m: halo_copy(m, n).wait_send())
        for n in range(STEPS):
            lat_copy(n).wait_send()
        ini_copy().wait_send()
        h_out.wait()
        p_out.wait()
        for cp in e_out:
            cp.wait()

    @pl.when(jnp.logical_not(coarse))
    def _():
        for ref in (ny_s, fy_s):
            ref[...] = jnp.zeros_like(ref)
        none = jnp.zeros((8, 128), jnp.int32)
        inside = (rows < ly) & (lanes < lz)
        two = lx == 2

        def inside_x(x):
            return jnp.where((x < 3) | two, 1, 0).astype(jnp.int32)

        tabs = tables(permit, conduct, relax, debye, 1.0 / 3.0, 0.25)
        spread = [3 * lanes + r for r in range(3)]
        phase = lanes % 3
        source = [(128 * ((phase + 3 - r) % 3) + lanes) // 3 for r in range(3)]

        def gather_in(ref, lead, ry):
            parts = [ref[(v,) + lead + (pl.ds(ry, 8, stride=3), slice(None))] for v in range(3)]
            tiles = []
            for r in range(3):
                at, src = spread[r] & 127, spread[r] >> 7
                got = [pick(part, at) for part in parts]
                tiles.append(jnp.where(src == 0, got[0], jnp.where(src == 1, got[1], got[2])))
            return tiles

        for cp in m_in:
            cp.wait()

        def fine_factors(x, carry):
            ok = inside & (inside_x(x) + none > 0)
            for ry in range(3):
                for r, here in enumerate(gather_in(mat, (x,), ry)):
                    ka, kc, kb, kf, kg = (pick(tabs[q], here) for q in range(5))
                    t = 3 * ry + r
                    fk[0, x, t] = ka
                    fk[1, x, t] = jnp.where(ok, kc, 0.0)
                    fk[2, x, t] = jnp.where(ok, kb * kg, 0.0)
                    fk[3, x, t] = kf
                    fk[4, x, t] = kg
                    fkr[x, t] = 1.0 / kg
            return carry

        lax.fori_loop(0, 6, fine_factors, 0)
        all_here()
        each(1, lambda m: pos_copy(m).start(), AROUND)
        for cp in f_in:
            cp.wait()
        for c in range(3):
            ff[c, 6] = jnp.zeros((9, 8, 128), F32)
            ff[3 + c, 0] = jnp.zeros((9, 8, 128), F32)

        def load_fine(x, carry):
            ok = inside & (inside_x(x) + none > 0)
            for c in range(9):
                for ry in range(3):
                    for r, here in enumerate(gather_in(stage, (c, x), ry)):
                        t = 3 * ry + r
                        if 3 <= c < 6:
                            ff[c, x + 1, t] = jnp.where(ok, 2.0 * here, 0.0)
                        elif c < 3:
                            ff[c, x, t] = jnp.where(ok, here, 0.0)
                        else:
                            ff[c, x, t] = jnp.where(ok, here * fkr[x, t], 0.0)
            return carry

        lax.fori_loop(0, 6, load_fine, 0)

        back_y, back_z = (8 - y0 % 8) % 8, (128 - z0 % 128) % 128

        def to_box(tile):
            return pltpu.roll(pltpu.roll(tile, back_y, 0), back_z, 1)

        def from_box(tile):
            return pltpu.roll(pltpu.roll(tile, y0 % 8, 0), z0 % 128, 1)

        edge_y = {0: rows == 0, 2: rows == ly - 1}
        edge_z = {0: lanes == 0, 2: lanes == lz - 1}

        def at_layer(x, carry, edges=True):
            ok = inside & (inside_x(x) + none > 0)
            edge = jnp.where((x == 0) | (x == 3 * lx - 1), 1, 0).astype(jnp.int32)
            edge_x = ok & (edge + none > 0)
            ok_y = {q: m & ok for q, m in edge_y.items()}
            ok_z = {q: m & ok for q, m in edge_z.items()}
            xc = x // 3
            tiles = [(ry, rz) for ry in range(3) for rz in range(3)]
            E = {(c, t): ff[c, x, t] for c in range(3) for t in range(9)}
            F = {(c, t): ff[c, x + 1, t] for c in (1, 2) for t in range(9)}
            H = {}
            for ry, rz in tiles:
                t = 3 * ry + rz
                ex, ey, ez = (E[c, t] for c in range(3))
                if ry < 2:
                    exy, ezy = E[0, t + 3], E[2, t + 3]
                else:
                    exy, ezy = yfwd(E[0, rz]), yfwd(E[2, rz])
                if rz < 2:
                    exz, eyz = E[0, t + 1], E[1, t + 1]
                else:
                    exz, eyz = zfwd(E[0, 3 * ry]), zfwd(E[1, 3 * ry])
                H[0, t] = ff[3, x + 1, t] - ((ezy - ez) - (eyz - ey))
                H[1, t] = ff[4, x + 1, t] - ((exz - ex) - (F[2, t] - ez))
                H[2, t] = ff[5, x + 1, t] - ((F[1, t] - ey) - (exy - ex))
                for c in range(3):
                    ff[3 + c, x + 1, t] = H[c, t]
            for ry, rz in tiles:
                t = 3 * ry + rz
                hx, hy, hz = (H[c, t] for c in range(3))
                if ry > 0:
                    hxy, hzy = H[0, t - 3], H[2, t - 3]
                else:
                    hxy, hzy = ybwd(H[0, 6 + rz]), ybwd(H[2, 6 + rz])
                if rz > 0:
                    hxz, hyz = H[0, t - 1], H[1, t - 1]
                else:
                    hxz, hyz = zbwd(H[0, 3 * ry + 2]), zbwd(H[1, 3 * ry + 2])
                hyx, hzx = ff[4, x, t], ff[5, x, t]
                curls = ((hz - hzy) - (hy - hyz), (hx - hxz) - (hz - hzx), (hy - hyx) - (hx - hxy))
                ka, kc, kb, kf = (fk[q, x, t] for q in range(4))
                for c in range(3):
                    pol = ff[6 + c, x, t]
                    new = ka * E[c, t] + kc * curls[c] + kb * pol
                    if not edges:
                        ff[c, x, t] = new
                        continue
                    marks = marked(c, ry, rz, edge_x, ok_y, ok_z)
                    if marks:
                        new = jnp.where(functools.reduce(jnp.logical_or, marks), drv[c, xc], new)
                    ff[c, x, t] = new
                    ff[6 + c, x, t] = kf * pol + new
            return carry

        def marked(c, ry, rz, edge_x, ok_y, ok_z):
            marks = []
            if c != 0:
                marks.append(edge_x)
            if c != 1 and ry in ok_y:
                marks.append(ok_y[ry])
            if c != 2 and rz in ok_z:
                marks.append(ok_z[rz])
            return marks

        def start_layer(x, carry):
            return at_layer(x, carry, False)

        def finish_layer(x, carry):
            ok = inside & (inside_x(x) + none > 0)
            edge = jnp.where((x == 0) | (x == 3 * lx - 1), 1, 0).astype(jnp.int32)
            edge_x = ok & (edge + none > 0)
            ok_y = {q: m & ok for q, m in edge_y.items()}
            ok_z = {q: m & ok for q, m in edge_z.items()}
            for ry in range(3):
                for rz in range(3):
                    t = 3 * ry + rz
                    kf = fk[3, x, t]
                    for c in range(3):
                        new = ff[c, x, t]
                        marks = marked(c, ry, rz, edge_x, ok_y, ok_z)
                        if marks:
                            new = jnp.where(functools.reduce(jnp.logical_or, marks), drv[c, x // 3], new)
                            ff[c, x, t] = new
                        ff[6 + c, x, t] = kf * ff[6 + c, x, t] + new
            return carry

        wrows = lax.broadcasted_iota(jnp.int32, (16, 256), 0)
        wlanes = lax.broadcasted_iota(jnp.int32, (16, 256), 1)
        at_y = y0 - 4 + ((wrows - (y0 - 4)) & 15)
        at_z = z0 - 64 + ((wlanes - (z0 - 64)) & 255)

        def w_in(at, low, size):
            return (at >= low) & (at < low + size)

        def twice(tile):
            return jnp.concatenate([jnp.concatenate([tile, tile], axis=1)] * 2, axis=0)

        def as_int(flag):
            return jnp.where(flag, 1, 0).astype(jnp.int32)

        def up_y(a):
            return pltpu.roll(a, 15, 0)

        def up_z(a):
            return pltpu.roll(a, 255, 1)

        def down_y(a):
            return pltpu.roll(a, 1, 0)

        def down_z(a):
            return pltpu.roll(a, 1, 1)

        region = w_in(at_y, y0, 8) & w_in(at_z, z0, 128)
        w_none = jnp.zeros((16, 256), jnp.int32)
        global_y = at_y + 24 * gb
        held_yz = (at_z >= 0) & (global_y >= 0)
        in_yz = held_yz & (at_z < 384) & (global_y < 24 * ny)

        def changes(d, reach):
            w = {}
            for c in range(3):
                for xr in range(-reach, 2 + reach):
                    w[c, xr] = jnp.where(region, twice(del_s[d, c, xr]), 0.0) if 0 <= xr < 2 else jnp.zeros((16, 256), F32)
            for m in (1, 3, 0, 2, 4, 5, 6, 7):
                dx, dy = AROUND[m]

                @pl.when(exists(-dx, -dy))
                def _():
                    box_copy(m, d).wait_recv()

                far_x, far_y, far_z = place_of[m, 0, 0], place_of[m, 1, 0], place_of[m, 2, 0]
                ok = w_in(at_z, far_z, 128)
                if dy == 0:
                    ok = ok & w_in(at_y, far_y, 8)
                else:
                    ok = ok & w_in(at_y, 24 if dy < 0 else -2, 2)
                for xr in {0: range(-reach, 2 + reach), -1: range(2, 2 + reach), 1: range(-reach, 0)}[dx]:
                    i = x0 + xr + 6 * dx - far_x
                    s0 = jnp.where(i == 0, 1.0, 0.0).astype(F32)
                    s1 = jnp.where(i == 1, 1.0, 0.0).astype(F32)
                    for c in range(3):
                        if dy == 0:
                            tile = s0 * fx_r[m // 2, d, c, 0] + s1 * fx_r[m // 2, d, c, 1]
                        else:
                            pair = [s0 * fy_r[m, d, 6 * r + 2 * c:6 * r + 2 * c + 1, :]
                                    + s1 * fy_r[m, d, 6 * r + 2 * c + 1:6 * r + 2 * c + 2, :] for r in range(2)]
                            low = 0 if dy < 0 else 6
                            tile = jnp.where(rows == low, jnp.broadcast_to(pair[0], (8, 128)),
                                             jnp.broadcast_to(pair[1], (8, 128)))
                        w[c, xr] = w[c, xr] + jnp.where(ok, twice(tile), 0.0)
            return w

        def turned_ahead(w, xr):
            ex, ey, ez = (w[c, xr] for c in range(3))
            moved = ((up_y(ez) - ez) - (up_z(ey) - ey), (up_z(ex) - ex) - (w[2, xr + 1] - ez),
                     (w[1, xr + 1] - ey) - (up_y(ex) - ex))
            ok = held_yz & (as_int(x0 + xr + 6 * ga >= 0) + w_none > 0)
            return [jnp.where(ok, -0.5 * part, 0.0) for part in moved]

        def turned_behind(hh, xr):
            hx, hy, hz = (hh[c, xr] for c in range(3))
            return ((hz - down_y(hz)) - (hy - down_z(hy)), (hx - down_z(hx)) - (hz - hh[2, xr - 1]),
                    (hy - hh[1, xr - 1]) - (hx - down_y(hx)))

        def on_region(wide):
            kept = jnp.where(region, wide, 0.0)
            return (kept[0:8, 0:128] + kept[0:8, 128:256]) + (kept[8:16, 0:128] + kept[8:16, 128:256])

        def window_factors():
            win_copy().wait_recv()
            slab = tables(permit, conduct, relax, debye, 1.0, 0.5)
            for xr in range(4):
                for u2 in range(2):
                    for v2 in range(2):
                        here = wm_r[xr, u2, v2]
                        spot = (xr, slice(8 * u2, 8 * u2 + 8), slice(128 * v2, 128 * v2 + 128))
                        for q in range(2):
                            kw[(q,) + spot] = pick(slab[q], here)
                        kw[(2,) + spot] = pick(slab[2], here) * pick(slab[4], here)

        def respond(n):
            hh = {}
            if n == 1:
                w = changes(0, 2)
                for xr in range(-2, 3):
                    for c, part in enumerate(turned_ahead(w, xr)):
                        hh[c, xr] = part
                        if -1 <= xr <= 1:
                            hw[c, xr + 1] = part
                layers = range(-1, 3)
            else:
                w = changes(1, 1)
                for c in range(3):
                    for xr in range(-1, 3):
                        w[c, xr] = w[c, xr] + ew[c, xr + 1]
                for xr in range(-1, 2):
                    for c, part in enumerate(turned_ahead(w, xr)):
                        hh[c, xr] = hw[c, xr + 1] + part
                layers = range(2)
            for xr in layers:
                ok = in_yz & (as_int((x0 + xr + 6 * ga >= 0) & (x0 + xr + 6 * ga < 6 * nx)) + w_none > 0)
                for c, curl in enumerate(turned_behind(hh, xr)):
                    value = kw[0, xr + 1] * w[c, xr] + kw[1, xr + 1] * curl
                    if n == 1:
                        value = jnp.where(ok, value, 0.0)
                        ew[c, xr + 1] = value
                    else:
                        value = value + kw[2, xr + 1] * ew[c, xr + 1]
                    if 0 <= xr < 2:
                        ear[1, c, xr] = to_box(lat_r[n, c, xr] + on_region(value))

        learn_places()
        ini_copy().wait_recv()
        for c in range(3):
            for i in range(2):
                ear[0, c, i] = to_box(ini_r[c, i])

        for n in range(STEPS):
            lax.fori_loop(0, 6, start_layer, 0)
            if n == 1:
                window_factors()
            lat_copy(n).wait_recv()
            if n == 0:
                for c in range(3):
                    for i in range(2):
                        ear[1, c, i] = to_box(lat_r[0, c, i])
            else:
                respond(n)

            drv[...] = ear[0] + (1.0 / 3.0) * (ear[1] - ear[0])
            lax.fori_loop(0, 6, finish_layer, 0)

            def substep(s, carry):
                weight = (s + 1).astype(F32) * (1.0 / 3.0)
                drv[...] = ear[0] + weight * (ear[1] - ear[0])
                return lax.fori_loop(0, 6, at_layer, carry, unroll=True)

            lax.fori_loop(1, 3, substep, 0)
            for i in range(2):
                ok = inside & (inside_x(3 * i) + none > 0)
                for c in range(3):
                    total = functools.reduce(
                        jnp.add, [ff[c, 3 * i + j, t] for j in range(3) for t in range(9)])
                    latest = ear[1, c, i]
                    delta = jnp.where(ok, total * (1.0 / 27.0) - latest, 0.0)
                    ear[0, c, i] = latest + delta
                    del_s[n, c, i] = from_box(delta)
            if n + 1 < STEPS:
                for r in range(2):
                    low = jnp.where(y0 <= r, 1.0, 0.0).astype(F32)
                    high = jnp.where(y0 >= 15 + r, 1.0, 0.0).astype(F32)
                    for c in range(3):
                        for i in range(2):
                            row = 6 * r + 2 * c + i
                            fy_s[0, n, row:row + 1, :] = low * del_s[n, c, i, r:r + 1, :]
                            fy_s[1, n, row:row + 1, :] = high * del_s[n, c, i, 6 + r:7 + r, :]
                for m in (4, 5, 6, 7, 0, 2, 1, 3):
                    dx, dy = AROUND[m]

                    @pl.when(exists(dx, dy))
                    def _():
                        box_copy(m, n).start()
                low, high = (jnp.where(x0 == q, 1.0, 0.0).astype(F32) for q in (0, 4))
                left, right = (jnp.where(y0 == q, 1.0, 0.0).astype(F32) for q in (0, 16))
                for c in range(3):
                    nx_s[0, n, c] = low * del_s[n, c, 0]
                    nx_s[1, n, c] = high * del_s[n, c, 1]
                    for i in range(2):
                        ny_s[0, n, 2 * c + i:2 * c + i + 1, :] = left * del_s[n, c, i, 0:1, :]
                        ny_s[1, n, 2 * c + i:2 * c + i + 1, :] = right * del_s[n, c, i, 7:8, :]
                nd_s[0, n] = jnp.broadcast_to((high * left) * del_s[n, 0, 1, 0:1, :], (8, 128))
                nd_s[1, n] = jnp.broadcast_to((low * right) * del_s[n, 1, 0, 7:8, :], (8, 128))
                del_copy(n).start()
                for m in (4, 5, 0, 2, 1, 3):
                    dx, dy = TO_NEXT[m]

                    @pl.when(exists(dx, dy))
                    def _():
                        near_copy(m, n).start()
            else:
                del_copy(n).start()

        def save_fine(x, carry):
            for c in range(9):
                for ry in range(3):
                    lift = 1 if 3 <= c < 6 else 0
                    parts = [ff[c, x + lift, 3 * ry + r] for r in range(3)]
                    if c >= 6:
                        parts = [part * fk[4, x, 3 * ry + r] for r, part in enumerate(parts)]
                    got = [pick(part, source[r]) for r, part in enumerate(parts)]
                    for v in range(3):
                        a, b, d = (got[(q + 2 * v) % 3] for q in range(3))
                        value = jnp.where(phase == 0, a, jnp.where(phase == 1, b, d))
                        if lift:
                            value = 0.5 * value
                        stage[v, c, x, pl.ds(ry, 8, stride=3), :] = value
            return carry

        lax.fori_loop(0, 6, save_fine, 0)
        f_out = [pltpu.make_async_copy(stage.at[v], out.at[0, :, :, :, pl.ds(128 * v, 128)], lsem.at[v]) for v in range(3)]
        for cp in f_out:
            cp.start()
        each(1, lambda m: pos_copy(m).wait_send(), AROUND)
        for n in range(STEPS):
            del_copy(n).wait_send()
            if n + 1 < STEPS:
                each(1, lambda m: near_copy(m, n).wait_send())
                each(1, lambda m: box_copy(m, n).wait_send(), AROUND)
        for cp in f_out:
            cp.wait()


def solution(mesh):
    nx, ny = mesh.shape["gx"], mesh.shape["gy"]

    def body(fields, material, permit, conduct, relax, debye, subgrids):
        vm = pltpu.VMEM
        dma = pltpu.SemaphoreType.DMA
        slots = [
            vm((SETS, 2, 24, 384), F32), vm((SETS, 2, 8, 384), F32),
            vm((SETS, 2, 24, 384), F32), vm((SETS, 2, 8, 384), F32),
            vm((SETS, 8, 384), F32), vm((SETS, 8, 384), F32),
        ]
        region = (3, 2, 8, 128)
        near = [vm((2, STEPS - 1, 3, 8, 128), F32), vm((2, STEPS - 1, 8, 128), F32), vm((2, STEPS - 1, 8, 128), F32)]
        return pl.pallas_call(
            functools.partial(kernel, nx, ny),
            out_shape=jax.ShapeDtypeStruct(fields.shape, F32),
            in_specs=[pl.BlockSpec(memory_space=pl.ANY)] * 7,
            out_specs=pl.BlockSpec(memory_space=pl.ANY),
            scratch_shapes=[
                *[pltpu.SMEM((8,), F32)] * 4, pltpu.SMEM((1, 1, 6), jnp.int32),
                vm((3, 3, 7, 32, 384), F32), vm((3, 3, 7, 32, 384), F32), vm((3, 3, 6, 24, 384), F32), vm((5, 6, 24, 384), F32),
                vm((3, 9, 6, 24, 128), F32), vm((3, 6, 24, 128), jnp.int32),
                vm((9, 7, 9, 8, 128), F32), vm((5, 6, 9, 8, 128), F32),
                vm((5, 16, 384), F32), vm((2, 8, 384), F32), vm((2, 8, 384), F32), vm((3, 32, 384), F32), vm((3, 8, 384), F32),
                vm((2,) + region, F32), vm(region, F32), vm((6, 9, 8, 128), F32),
                vm((3, 8, 40, 128), jnp.int32), vm((3, 4, 16, 256), F32), vm((3, 3, 16, 256), F32), vm((3, 4, 16, 256), F32),
                *slots, *slots,
                vm((STEPS,) + region, F32), vm((STEPS,) + region, F32), vm(region, F32), vm(region, F32),
                vm((STEPS,) + region, F32), vm((STEPS,) + region, F32),
                *near, *near, vm((8, 128), jnp.int32), vm((8, 8, 128), jnp.int32), pltpu.SMEM((8, 8, 128), jnp.int32),
                vm((2, STEPS - 1, 16, 128), F32), vm((2, STEPS - 1) + region, F32), vm((8, STEPS - 1, 16, 128), F32),
                vm((6, 3, 8, 128), jnp.int32), vm((2, 3, 24, 128), jnp.int32), vm((6, 3, 8, 128), jnp.int32),
                vm((4, 2, 2, 8, 128), jnp.int32), vm((4, 2, 2, 8, 128), jnp.int32),
                dma((18,)), dma((6, SETS)), dma((6, SETS)),
                dma((STEPS + 1,)), dma((STEPS + 1,)), dma((STEPS,)), dma((STEPS,)),
                dma((6, STEPS)), dma((6, STEPS)), dma((8,)), dma((8,)),
                dma((8, STEPS)), dma((8, STEPS)), dma((6,)), dma((6,)), dma((1,)), dma((1,)),
            ],
            compiler_params=pltpu.CompilerParams(
                collective_id=0, has_side_effects=True, vmem_limit_bytes=63 * 1024 * 1024),
        )(fields, material, permit, conduct, relax, debye, subgrids)

    return jax.shard_map(
        body,
        mesh=mesh,
        in_specs=(P("grid", None, "gx", "gy", None), P("grid", "gx", "gy", None), P(), P(), P(), P(), P("gx", "gy", None)),
        out_specs=P("grid", None, "gx", "gy", None),
        check_vma=False,
    )
```

```python
import functools

import jax
import jax.numpy as jnp
from jax import lax
from jax.experimental import pallas as pl
from jax.experimental.pallas import tpu as pltpu
from jax.sharding import PartitionSpec as P

MESH = pl.DeviceIdType.MESH
STEPS = 3
F32 = jnp.float32

TO_NEXT = ((-1, 0), (0, -1), (1, 0), (0, 1), (1, -1), (-1, 1))
XE, YE, XG, YG, C1, C2 = range(6)
AROUND = TO_NEXT + ((1, 1), (-1, -1))
SETS = STEPS + 1


def lane_iota():
    return lax.broadcasted_iota(jnp.int32, (8, 128), 1)


def row_iota():
    return lax.broadcasted_iota(jnp.int32, (8, 128), 0)


def pick(tile, index):
    return jnp.take_along_axis(tile, index, axis=1, mode="promise_in_bounds")


def zfwd(v):
    n = v.shape[-1]
    lanes = lax.broadcasted_iota(jnp.int32, v.shape, v.ndim - 1)
    return jnp.where(lanes == n - 1, 0.0, pltpu.roll(v, n - 1, v.ndim - 1))


def zbwd(v):
    lanes = lax.broadcasted_iota(jnp.int32, v.shape, v.ndim - 1)
    return jnp.where(lanes == 0, 0.0, pltpu.roll(v, 1, v.ndim - 1))


def yfwd(t):
    return jnp.where(row_iota() == 7, 0.0, pltpu.roll(t, 7, 0))


def ybwd(t):
    return jnp.where(row_iota() == 0, 0.0, pltpu.roll(t, 1, 0))


def tables(permit, conduct, relax, debye, factor, courant):
    lane = lane_iota()

    def spread(ref):
        out = jnp.ones((8, 128), F32)
        for m in range(8):
            out = jnp.where(lane == m, ref[m], out)
        return out

    eps = spread(permit)
    damping = spread(conduct) * factor / (2.0 * eps)
    f0 = (1.0 - damping) / (1.0 + damping)
    f1 = 1.0 / (eps * (1.0 + damping))
    f2 = spread(relax) * factor
    f3 = jnp.exp(-f2)
    f4 = spread(debye)
    return f0 - f1 * f2 * f4, courant * f1, f1 * f2, f3, (1.0 - f3) * f4


def kernel(
    nx, ny,
    fields, material, permit_in, conduct_in, relax_in, debye_in, subgrids_in, out,
    permit, conduct, relax, debye, subgrids, e2, h2, p2, k, stage, mat, ff, fk, pk, pln, own, dl, pd, ear, drv, fkr, mext, ew, hw, kw,
    xe_s, ye_s, xg_s, yg_s, c1_s, c2_s,
    xe_r, ye_r, xg_r, yg_r, c1_r, c2_r,
    lat_s, lat_r, ini_s, ini_r, del_s, del_r,
    nx_s, ny_s, nd_s, nx_r, ny_r, nd_r, pos_s, pos_r, place_of,
    fy_s, fx_r, fy_r, my_s, mx_r, my_r, wm_s, wm_r,
    lsem, hs, hr, bs, br, ds, dr, ns, nr, ps, pr, fs, fr, ms, mr, ws, wr,
):
    grid = lax.axis_index("grid")
    ga = lax.axis_index("gx")
    gb = lax.axis_index("gy")
    coarse = grid == 0
    sends = (xe_s, ye_s, xg_s, yg_s, c1_s, c2_s)
    recvs = (xe_r, ye_r, xg_r, yg_r, c1_r, c2_r)
    delta_s = (nx_s.at[0], ny_s.at[0], nx_s.at[1], ny_s.at[1], nd_s.at[0], nd_s.at[1])
    delta_r = (nx_r.at[0], ny_r.at[0], nx_r.at[1], ny_r.at[1], nd_r.at[0], nd_r.at[1])

    def exists(dx, dy):
        return (ga + dx >= 0) & (ga + dx < nx) & (gb + dy >= 0) & (gb + dy < ny)

    def device(g, dx, dy):
        return (g, jnp.clip(ga + dx, 0, nx - 1), jnp.clip(gb + dy, 0, ny - 1))

    partner = (1 - grid, ga, gb)
    rows, lanes = row_iota(), lane_iota()

    e_in = pltpu.make_async_copy(fields.at[0, 0:3], e2.at[0, :, 0:6, 0:24, :], lsem.at[0])
    h_in = pltpu.make_async_copy(fields.at[0, 3:6], h2.at[0, :, 1:7, 8:32, :], lsem.at[1])
    p_in = pltpu.make_async_copy(fields.at[0, 6:9], p2.at[0], lsem.at[2])
    f_in = [pltpu.make_async_copy(fields.at[0, :, :, :, pl.ds(128 * v, 128)], stage.at[v], lsem.at[v]) for v in range(3)]
    m_in = [pltpu.make_async_copy(material.at[0, :, :, pl.ds(128 * v, 128)], mat.at[v], lsem.at[3 + v]) for v in range(3)]

    @pl.when(coarse)
    def _():
        for cp in (e_in, h_in, p_in):
            cp.start()

    @pl.when(jnp.logical_not(coarse))
    def _():
        for cp in f_in:
            cp.start()

    for cp in m_in:
        cp.start()
    scalars = [
        pltpu.make_async_copy(a, b, lsem.at[7 + q])
        for q, (a, b) in enumerate(((permit_in, permit), (conduct_in, conduct), (relax_in, relax), (debye_in, debye),
                                    (subgrids_in, subgrids)))]
    for cp in scalars:
        cp.start()
    for ref in (nx_r, ny_r, nd_r, pos_r, fx_r, fy_r):
        ref[...] = jnp.zeros_like(ref)

    @pl.when(coarse)
    def _():
        for ref in (mx_r, my_r, c1_r, c2_r):
            ref[...] = jnp.zeros_like(ref)
        for m in (XE, YE, XG, YG):
            dx, dy = TO_NEXT[m]

            @pl.when(jnp.logical_not(exists(-dx, -dy)))
            def _():
                recvs[m][...] = jnp.zeros_like(recvs[m])

    barrier = pltpu.get_barrier_semaphore()
    pl.semaphore_signal(barrier, inc=1, device_id=partner, device_id_type=MESH)
    count = jnp.int32(1)
    for dx, dy in AROUND:
        count = count + exists(dx, dy).astype(jnp.int32)

        @pl.when(exists(dx, dy))
        def _():
            pl.semaphore_signal(barrier, inc=1, device_id=(grid, ga + dx, gb + dy), device_id_type=MESH)

    @pl.when(coarse)
    def _():
        for ref in (ye_s, yg_s, pk, pln, own, my_s, mext):
            ref[...] = jnp.zeros_like(ref)

    for cp in scalars:
        cp.wait()
    x0, y0, z0 = subgrids[0, 0, 0], subgrids[0, 0, 1], subgrids[0, 0, 2]
    lx, ly, lz = subgrids[0, 0, 3], subgrids[0, 0, 4], subgrids[0, 0, 5]
    pos_s[...] = jnp.where(rows == 0, x0, jnp.where(rows == 1, y0, z0))

    def all_here():
        pl.semaphore_wait(barrier, count)

    def remote(src, dst, send, recv, target):
        return pltpu.make_async_remote_copy(
            src_ref=src, dst_ref=dst, send_sem=send, recv_sem=recv, device_id=target, device_id_type=MESH)

    def halo_copy(m, n):
        if m in (C1, C2):
            return remote(sends[m].at[n, 0:1], recvs[m].at[n, 0:1], hs.at[m, n], hr.at[m, n], device(grid, *TO_NEXT[m]))
        return remote(sends[m].at[n], recvs[m].at[n], hs.at[m, n], hr.at[m, n], device(grid, *TO_NEXT[m]))

    def lat_copy(n):
        return remote(lat_s.at[n], lat_r.at[n], bs.at[n], br.at[n], partner)

    def ini_copy():
        return remote(ini_s, ini_r, bs.at[STEPS], br.at[STEPS], partner)

    def del_copy(n):
        return remote(del_s.at[n], del_r.at[n], ds.at[n], dr.at[n], partner)

    def near_copy(m, n):
        return remote(delta_s[m].at[n], delta_r[m].at[n], ns.at[m, n], nr.at[m, n], device(0, *TO_NEXT[m]))

    def box_copy(m, n):
        dx, dy = AROUND[m]
        if dy == 0:
            src, dst = del_s.at[n], fx_r.at[m // 2, n]
        else:
            src, dst = fy_s.at[0 if dy < 0 else 1, n], fy_r.at[m, n]
        return remote(src, dst, fs.at[m, n], fr.at[m, n], device(1, dx, dy))

    def pos_copy(m):
        return remote(pos_s, pos_r.at[m], ps.at[m], pr.at[m], device(grid, *AROUND[m]))

    def mat_copy(m):
        dx, dy = TO_NEXT[m]
        if dy == 0:
            src, dst = mat.at[:, 0 if dx < 0 else 5], mx_r.at[m // 2]
        else:
            src, dst = my_s.at[m], my_r.at[m]
        return remote(src, dst, ms.at[m], mr.at[m], device(0, dx, dy))

    def win_copy():
        return remote(wm_s, wm_r, ws.at[0], wr.at[0], partner)

    def each(turn, fun, over=TO_NEXT):
        for m, (dx, dy) in enumerate(over):
            @pl.when(exists(turn * dx, turn * dy))
            def _():
                fun(m)

    def learn_places():
        each(-1, lambda m: pos_copy(m).wait_recv(), AROUND)
        cp = pltpu.make_async_copy(pos_r, place_of, lsem.at[6])
        cp.start()
        cp.wait()

    def row_in(low, u):
        return (rows + 8 * u >= low) & (rows + 8 * u < low + 8)

    def lane_in(low, v):
        return (lanes + 128 * v >= low) & (lanes + 128 * v < low + 128)

    def tile_at(u, v):
        return (slice(8 * u, 8 * u + 8), slice(128 * v, 128 * v + 128))

    @pl.when(coarse)
    def _():
        flag_x = jnp.where(ga > 0, 1.0, 0.0).astype(F32)
        flag_y = jnp.where(gb > 0, 1.0, 0.0).astype(F32)
        row_ok = [row_in(y0, u) for u in range(3)]
        lane_ok = [lane_in(z0, v) for v in range(3)]
        wide = lax.broadcasted_iota(jnp.int32, (24, 384), 0)

        def cut(load, i):
            tile = jnp.zeros((8, 128), F32)
            for u in range(3):
                for v in range(3):
                    tile = jnp.where(row_ok[u] & lane_ok[v], load(x0 + i, *tile_at(u, v)), tile)
            return tile

        def cut_latest(n, e):
            for i in range(2):
                for c in range(3):
                    lat_s[n, c, i] = cut(lambda x, r, l: e[c, x, r, l], i)
            lat_copy(n).start()

        def place(n, e, done=None):
            for x in range(6):
                s0 = jnp.where(x == x0, 1.0, 0.0).astype(F32)
                s1 = jnp.where(x == x0 + 1, 1.0, 0.0).astype(F32)
                for c in range(3):
                    tile = s0 * del_r[n, c, 0] + s1 * del_r[n, c, 1]
                    for u in range(3):
                        for v in range(3):
                            spot = (c, x) + tile_at(u, v)
                            e[spot] = e[spot] + jnp.where(row_ok[u] & lane_ok[v], tile, 0.0)
                if done is not None:
                    done[x].start()

        def send_halo(m, n):
            @pl.when(exists(*TO_NEXT[m]))
            def _():
                halo_copy(m, n).start()

        def leave_high(n, e, h):
            c1_s[n, 0:1, :] = e[0, 5, 0:1, :]
            send_halo(C1, n)
            ex, ey, ez = e[0, 5, 0:24, :], e[1, 5, 0:24, :], e[2, 5, 0:24, :]
            exy = jnp.where(wide == 23, 0.0, e[0, 5, 1:25, :])
            xg_s[n, 0] = h[1, 6, 8:32, :] - 0.5 * (zfwd(ex) - ex + ez)
            xg_s[n, 1] = h[2, 6, 8:32, :] + 0.5 * (ey + exy - ex)
            send_halo(XG, n)

        def leave_low(n, e):
            c2_s[n, 0:1, :] = e[1, 0, 23:24, :]
            send_halo(C2, n)
            xe_s[n] = e[1:3, 0, 0:24, :]
            send_halo(XE, n)

        def leave_y(n, e, h):
            for x in range(6):
                ye_s[n, 0, x:x + 1, :] = e[0, x, 0:1, :]
                ye_s[n, 1, x:x + 1, :] = e[2, x, 0:1, :]
            send_halo(YE, n)
            for x in range(6):
                for c in range(3):
                    pk[c, x:x + 1, :] = e[c, x, 23:24, :]
                pk[3, x:x + 1, :] = h[0, x + 1, 31:32, :]
                pk[4, x:x + 1, :] = h[2, x + 1, 31:32, :]
            px, py, pz = pk[0, 0:8, :], pk[1, 0:8, :], pk[2, 0:8, :]
            yg_s[n, 0] = pk[3, 0:8, :] + 0.5 * (pz + zfwd(py) - py)
            yg_s[n, 1] = pk[4, 0:8, :] - 0.5 * (pk[1, 1:9, :] - py + px)
            send_halo(YG, n)

        def put_halos(n, e, h):
            e[1:3, 6, 0:24, :] = xe_r[n]
            h[1, 0, 8:32, :] = flag_x * (xg_r[n, 0] + 0.5 * e[2, 0, 0:24, :])
            h[2, 0, 8:32, :] = flag_x * (xg_r[n, 1] - 0.5 * e[1, 0, 0:24, :])
            for x in range(6):
                own[0, x:x + 1, :] = e[0, x, 0:1, :]
                own[1, x:x + 1, :] = e[2, x, 0:1, :]
            pln[0] = flag_y * (yg_r[n, 0] - 0.5 * own[1])
            pln[1] = flag_y * (yg_r[n, 1] + 0.5 * own[0])
            for x in range(6):
                e[0, x, 24:25, :] = ye_r[n, 0, x:x + 1, :]
                e[2, x, 24:25, :] = ye_r[n, 1, x:x + 1, :]
                h[0, x + 1, 7:8, :] = pln[0, x:x + 1, :]
                h[2, x + 1, 7:8, :] = pln[1, x:x + 1, :]

        def put_corners(n, h):
            h[2, 0, 31:32, :] = h[2, 0, 31:32, :] + (0.5 * flag_x) * c1_r[n, 0:1, :]
            h[2, 6, 7:8, :] = h[2, 6, 7:8, :] - (0.5 * flag_y) * c2_r[n, 0:1, :]

        def mend_halos(n, d):
            each(-1, lambda m: near_copy(m, d).wait_recv())
            for u in range(3):
                for v in range(3):
                    spot = tile_at(u, v)
                    ok = row_in(place_of[XE, 1, 0], u) & lane_in(place_of[XE, 2, 0], v)
                    for q in range(2):
                        xe_r[(n, q) + spot] = xe_r[(n, q) + spot] + jnp.where(ok, nx_r[0, d, 1 + q], 0.0)
                    ok = row_in(place_of[XG, 1, 0], u) & lane_in(place_of[XG, 2, 0], v)
                    for c in range(3):
                        dl[(c,) + spot] = jnp.where(ok, nx_r[1, d, c], 0.0)
            tx, ty, tz = dl[0, 0:24, :], dl[1, 0:24, :], dl[2, 0:24, :]
            dl[0, 24:32, :] = jnp.zeros((8, 384), F32)
            xg_r[n, 0] = xg_r[n, 0] - 0.5 * (zfwd(tx) - tx + tz)
            xg_r[n, 1] = xg_r[n, 1] + 0.5 * (ty + dl[0, 1:25, :] - tx)
            for m, keep in ((YE, ny_r.at[0]), (YG, ny_r.at[1])):
                at = place_of[m, 0, 0]
                for c in range(3):
                    two = [jnp.broadcast_to(keep[d, 2 * c + i:2 * c + i + 1, :], (8, 128)) for i in range(2)]
                    both = jnp.where(rows == at, two[0], jnp.where(rows == at + 1, two[1], 0.0))
                    for v in range(3):
                        pd[c, :, 128 * v:128 * v + 128] = jnp.where(lane_in(place_of[m, 2, 0], v), both, 0.0)
                if m == YE:
                    ye_r[n, 0] = ye_r[n, 0] + pd[0]
                    ye_r[n, 1] = ye_r[n, 1] + pd[2]
                else:
                    yg_r[n, 0] = yg_r[n, 0] + 0.5 * (pd[2] + zfwd(pd[1]) - pd[1])
                    yg_r[n, 1] = yg_r[n, 1] - 0.5 * (pltpu.roll(pd[1], 7, 0) - pd[1] + pd[0])
            for m, ref, keep in ((C1, c1_r, nd_r.at[0]), (C2, c2_r, nd_r.at[1])):
                for v in range(3):
                    spot = (n, slice(0, 8), slice(128 * v, 128 * v + 128))
                    ref[spot] = ref[spot] + jnp.where(lane_in(place_of[m, 2, 0], v), keep[d], 0.0)

        def update(e, h, p, ed, hd, pd_, corners, slot=None, cut_to=None):
            def magnetic(x):
                for u in range(3):
                    r = slice(8 * u, 8 * u + 8)
                    ra = slice(8 * u + 1, 8 * u + 9)
                    rh = slice(8 * u + 8, 8 * u + 16)
                    ex, ey, ez = e[0, x, r, :], e[1, x, r, :], e[2, x, r, :]
                    hd[0, x + 1, rh, :] = h[0, x + 1, rh, :] - 0.5 * ((e[2, x, ra, :] - ez) - (zfwd(ey) - ey))
                    hd[1, x + 1, rh, :] = h[1, x + 1, rh, :] - 0.5 * ((zfwd(ex) - ex) - (e[2, x + 1, r, :] - ez))
                    hd[2, x + 1, rh, :] = h[2, x + 1, rh, :] - 0.5 * ((e[1, x + 1, r, :] - ey) - (e[0, x, ra, :] - ex))

            def electric(x):
                for u in range(3):
                    r = slice(8 * u, 8 * u + 8)
                    rh = slice(8 * u + 8, 8 * u + 16)
                    rb = slice(8 * u + 7, 8 * u + 15)
                    hx, hy, hz = hd[0, x + 1, rh, :], hd[1, x + 1, rh, :], hd[2, x + 1, rh, :]
                    cx = (hz - hd[2, x + 1, rb, :]) - (hy - zbwd(hy))
                    cy = (hx - zbwd(hx)) - (hz - hd[2, x, rh, :])
                    cz = (hy - hd[1, x, rh, :]) - (hx - hd[0, x + 1, rb, :])
                    ka, kc, kb, kf, kg = (k[q, x, r, :] for q in range(5))
                    for c, curl in enumerate((cx, cy, cz)):
                        pol = p[c, x, r, :]
                        new = ka * e[c, x, r, :] + kc * curl + kb * pol
                        ed[c, x, r, :] = new
                        if pd_ is not None:
                            pd_[c, x, r, :] = kf * pol + kg * new

            for x in range(6):
                magnetic(x)
                if 1 < x:
                    electric(x - 1)
            corners()
            electric(5)
            if slot is not None:
                leave_high(slot, ed, hd)
            electric(0)
            if slot is not None:
                leave_low(slot, ed)
            if cut_to is not None:
                cut_latest(cut_to, ed)
            if slot is not None:
                leave_y(slot, ed, hd)

        def material_window():
            each(-1, lambda m: mat_copy(m).wait_recv())
            for v in range(3):
                mext[v, 1:7, 8:32, :] = mat[v]
                mext[v, 7, 8:32, :] = mx_r[0, v]
                mext[v, 0, 8:32, :] = mx_r[1, v]
                for x in range(6):
                    mext[v, x + 1, 32:33, :] = my_r[YE, v, x:x + 1, :]
                    mext[v, x + 1, 7:8, :] = my_r[YG, v, x:x + 1, :]
                mext[v, 0, 32:33, :] = my_r[C1, v, 0:1, :]
                mext[v, 7, 7:8, :] = my_r[C2, v, 0:1, :]
            for u2 in range(2):
                for v2 in range(2):
                    found = [jnp.zeros((8, 128), jnp.int32)] * 4
                    for u in range(-1, 4):
                        for v in range(3):
                            if u % 2 != u2 or v % 2 != v2:
                                continue
                            ok = (rows + 8 * u >= y0 - 1) & (rows + 8 * u < y0 + 9)
                            ok = ok & (lanes + 128 * v >= z0 - 1) & (lanes + 128 * v < z0 + 129)
                            for xr in range(4):
                                found[xr] = jnp.where(ok, mext[v, x0 + xr, 8 * u + 8:8 * u + 16, :], found[xr])
                    for xr in range(4):
                        wm_s[xr, u2, v2] = found[xr]
            win_copy().start()

        sets = [(e2.at[q], h2.at[q], p2.at[q]) for q in range(3)]
        e_in.wait()
        h_in.wait()
        all_here()
        leave_high(0, sets[0][0], sets[0][1])
        leave_low(0, sets[0][0])
        leave_y(0, sets[0][0], sets[0][1])
        each(1, lambda m: pos_copy(m).start(), AROUND)
        for cp in m_in:
            cp.wait()
        for v in range(3):
            for x in range(6):
                my_s[YE, v, x:x + 1, :] = mat[v, x, 0:1, :]
                my_s[YG, v, x:x + 1, :] = mat[v, x, 23:24, :]
            my_s[C1, v] = jnp.broadcast_to(mat[v, 5, 0:1, :], (8, 128))
            my_s[C2, v] = jnp.broadcast_to(mat[v, 0, 23:24, :], (8, 128))
        each(1, lambda m: mat_copy(m).start())
        tabs = tables(permit, conduct, relax, debye, 1.0, 0.5)

        def factors(x, carry):
            for u in range(3):
                for v in range(3):
                    here = mat[v, x, 8 * u:8 * u + 8, :]
                    for q in range(5):
                        k[(q, x) + tile_at(u, v)] = pick(tabs[q], here)
            return carry

        lax.fori_loop(0, 6, factors, 0)
        for i in range(2):
            for c in range(3):
                ini_s[c, i] = cut(lambda x, r, l: e2[0, c, x, r, l], i)
        ini_copy().start()
        p_in.wait()

        def advance(slot_in, source, target, fresh, **then):
            def corners():
                if fresh:
                    arrive(slot_in, (C1, C2))
                put_corners(slot_in, target[1])

            if fresh:
                arrive(slot_in, (XE, YE, XG, YG))
            put_halos(slot_in, source[0], target[1])
            update(*source, *target, corners, **then)

        def arrive(slot, which):
            for m in which:
                dx, dy = TO_NEXT[m]

                @pl.when(exists(-dx, -dy))
                def _():
                    halo_copy(m, slot).wait_recv()

        advance(0, sets[0], sets[1], True, slot=1, cut_to=0)
        learn_places()
        material_window()
        advance(1, sets[1], sets[2], True, slot=2, cut_to=1)
        advance(2, sets[2], (sets[0][0], sets[0][1], None), True, cut_to=2)
        del_copy(0).wait_recv()
        place(0, sets[1][0])
        mend_halos(1, 0)
        advance(1, sets[1], sets[0], False, slot=3)
        arrive(3, range(6))
        del_copy(1).wait_recv()
        place(1, sets[0][0])
        mend_halos(3, 1)
        advance(3, sets[0], sets[2], False)
        e, h, p = sets[2]
        h_out = pltpu.make_async_copy(h.at[:, 1:7, 8:32, :], out.at[0, 3:6], lsem.at[1])
        p_out = pltpu.make_async_copy(p, out.at[0, 6:9], lsem.at[2])
        h_out.start()
        p_out.start()
        del_copy(STEPS - 1).wait_recv()
        e_out = [pltpu.make_async_copy(e.at[:, x, 0:24, :], out.at[0, 0:3, x], lsem.at[12 + x]) for x in range(6)]
        place(STEPS - 1, e, e_out)

        each(1, lambda m: pos_copy(m).wait_send(), AROUND)
        each(1, lambda m: mat_copy(m).wait_send())
        win_copy().wait_send()
        for n in range(SETS):
            each(1, lambda m: halo_copy(m, n).wait_send())
        for n in range(STEPS):
            lat_copy(n).wait_send()
        ini_copy().wait_send()
        h_out.wait()
        p_out.wait()
        for cp in e_out:
            cp.wait()

    @pl.when(jnp.logical_not(coarse))
    def _():
        for ref in (ny_s, fy_s):
            ref[...] = jnp.zeros_like(ref)
        none = jnp.zeros((8, 128), jnp.int32)
        inside = (rows < ly) & (lanes < lz)
        two = lx == 2

        def inside_x(x):
            return jnp.where((x < 3) | two, 1, 0).astype(jnp.int32)

        tabs = tables(permit, conduct, relax, debye, 1.0 / 3.0, 0.25)
        spread = [3 * lanes + r for r in range(3)]
        phase = lanes % 3
        source = [(128 * ((phase + 3 - r) % 3) + lanes) // 3 for r in range(3)]

        def gather_in(ref, lead, ry):
            parts = [ref[(v,) + lead + (pl.ds(ry, 8, stride=3), slice(None))] for v in range(3)]
            tiles = []
            for r in range(3):
                at, src = spread[r] & 127, spread[r] >> 7
                got = [pick(part, at) for part in parts]
                tiles.append(jnp.where(src == 0, got[0], jnp.where(src == 1, got[1], got[2])))
            return tiles

        for cp in m_in:
            cp.wait()

        def fine_factors(x, carry):
            ok = inside & (inside_x(x) + none > 0)
            for ry in range(3):
                for r, here in enumerate(gather_in(mat, (x,), ry)):
                    ka, kc, kb, kf, kg = (pick(tabs[q], here) for q in range(5))
                    t = 3 * ry + r
                    fk[0, x, t] = ka
                    fk[1, x, t] = jnp.where(ok, kc, 0.0)
                    fk[2, x, t] = jnp.where(ok, kb * kg, 0.0)
                    fk[3, x, t] = kf
                    fk[4, x, t] = kg
                    fkr[x, t] = 1.0 / kg
            return carry

        lax.fori_loop(0, 6, fine_factors, 0)
        all_here()
        each(1, lambda m: pos_copy(m).start(), AROUND)
        for cp in f_in:
            cp.wait()
        for c in range(3):
            ff[c, 6] = jnp.zeros((9, 8, 128), F32)
            ff[3 + c, 0] = jnp.zeros((9, 8, 128), F32)

        def load_fine(x, carry):
            ok = inside & (inside_x(x) + none > 0)
            for c in range(9):
                for ry in range(3):
                    for r, here in enumerate(gather_in(stage, (c, x), ry)):
                        t = 3 * ry + r
                        if 3 <= c < 6:
                            ff[c, x + 1, t] = jnp.where(ok, 2.0 * here, 0.0)
                        elif c < 3:
                            ff[c, x, t] = jnp.where(ok, here, 0.0)
                        else:
                            ff[c, x, t] = jnp.where(ok, here * fkr[x, t], 0.0)
            return carry

        lax.fori_loop(0, 6, load_fine, 0)

        back_y, back_z = (8 - y0 % 8) % 8, (128 - z0 % 128) % 128

        def to_box(tile):
            return pltpu.roll(pltpu.roll(tile, back_y, 0), back_z, 1)

        def from_box(tile):
            return pltpu.roll(pltpu.roll(tile, y0 % 8, 0), z0 % 128, 1)

        edge_y = {0: rows == 0, 2: rows == ly - 1}
        edge_z = {0: lanes == 0, 2: lanes == lz - 1}

        def at_layer(x, carry, edges=True):
            ok = inside & (inside_x(x) + none > 0)
            edge = jnp.where((x == 0) | (x == 3 * lx - 1), 1, 0).astype(jnp.int32)
            edge_x = ok & (edge + none > 0)
            ok_y = {q: m & ok for q, m in edge_y.items()}
            ok_z = {q: m & ok for q, m in edge_z.items()}
            xc = x // 3
            tiles = [(ry, rz) for ry in range(3) for rz in range(3)]
            E = {(c, t): ff[c, x, t] for c in range(3) for t in range(9)}
            F = {(c, t): ff[c, x + 1, t] for c in (1, 2) for t in range(9)}
            H = {}
            for ry, rz in tiles:
                t = 3 * ry + rz
                ex, ey, ez = (E[c, t] for c in range(3))
                if ry < 2:
                    exy, ezy = E[0, t + 3], E[2, t + 3]
                else:
                    exy, ezy = yfwd(E[0, rz]), yfwd(E[2, rz])
                if rz < 2:
                    exz, eyz = E[0, t + 1], E[1, t + 1]
                else:
                    exz, eyz = zfwd(E[0, 3 * ry]), zfwd(E[1, 3 * ry])
                H[0, t] = ff[3, x + 1, t] - ((ezy - ez) - (eyz - ey))
                H[1, t] = ff[4, x + 1, t] - ((exz - ex) - (F[2, t] - ez))
                H[2, t] = ff[5, x + 1, t] - ((F[1, t] - ey) - (exy - ex))
                for c in range(3):
                    ff[3 + c, x + 1, t] = H[c, t]
            for ry, rz in tiles:
                t = 3 * ry + rz
                hx, hy, hz = (H[c, t] for c in range(3))
                if ry > 0:
                    hxy, hzy = H[0, t - 3], H[2, t - 3]
                else:
                    hxy, hzy = ybwd(H[0, 6 + rz]), ybwd(H[2, 6 + rz])
                if rz > 0:
                    hxz, hyz = H[0, t - 1], H[1, t - 1]
                else:
                    hxz, hyz = zbwd(H[0, 3 * ry + 2]), zbwd(H[1, 3 * ry + 2])
                hyx, hzx = ff[4, x, t], ff[5, x, t]
                curls = ((hz - hzy) - (hy - hyz), (hx - hxz) - (hz - hzx), (hy - hyx) - (hx - hxy))
                ka, kc, kb, kf = (fk[q, x, t] for q in range(4))
                for c in range(3):
                    pol = ff[6 + c, x, t]
                    new = ka * E[c, t] + kc * curls[c] + kb * pol
                    if not edges:
                        ff[c, x, t] = new
                        continue
                    marks = marked(c, ry, rz, edge_x, ok_y, ok_z)
                    if marks:
                        new = jnp.where(functools.reduce(jnp.logical_or, marks), drv[c, xc], new)
                    ff[c, x, t] = new
                    ff[6 + c, x, t] = kf * pol + new
            return carry

        def marked(c, ry, rz, edge_x, ok_y, ok_z):
            marks = []
            if c != 0:
                marks.append(edge_x)
            if c != 1 and ry in ok_y:
                marks.append(ok_y[ry])
            if c != 2 and rz in ok_z:
                marks.append(ok_z[rz])
            return marks

        def start_layer(x, carry):
            return at_layer(x, carry, False)

        def finish_layer(x, carry):
            ok = inside & (inside_x(x) + none > 0)
            edge = jnp.where((x == 0) | (x == 3 * lx - 1), 1, 0).astype(jnp.int32)
            edge_x = ok & (edge + none > 0)
            ok_y = {q: m & ok for q, m in edge_y.items()}
            ok_z = {q: m & ok for q, m in edge_z.items()}
            for ry in range(3):
                for rz in range(3):
                    t = 3 * ry + rz
                    kf = fk[3, x, t]
                    for c in range(3):
                        new = ff[c, x, t]
                        marks = marked(c, ry, rz, edge_x, ok_y, ok_z)
                        if marks:
                            new = jnp.where(functools.reduce(jnp.logical_or, marks), drv[c, x // 3], new)
                            ff[c, x, t] = new
                        ff[6 + c, x, t] = kf * ff[6 + c, x, t] + new
            return carry

        wrows = lax.broadcasted_iota(jnp.int32, (16, 256), 0)
        wlanes = lax.broadcasted_iota(jnp.int32, (16, 256), 1)
        at_y = y0 - 4 + ((wrows - (y0 - 4)) & 15)
        at_z = z0 - 64 + ((wlanes - (z0 - 64)) & 255)

        def w_in(at, low, size):
            return (at >= low) & (at < low + size)

        def twice(tile):
            return jnp.concatenate([jnp.concatenate([tile, tile], axis=1)] * 2, axis=0)

        def as_int(flag):
            return jnp.where(flag, 1, 0).astype(jnp.int32)

        def up_y(a):
            return pltpu.roll(a, 15, 0)

        def up_z(a):
            return pltpu.roll(a, 255, 1)

        def down_y(a):
            return pltpu.roll(a, 1, 0)

        def down_z(a):
            return pltpu.roll(a, 1, 1)

        region = w_in(at_y, y0, 8) & w_in(at_z, z0, 128)
        w_none = jnp.zeros((16, 256), jnp.int32)
        global_y = at_y + 24 * gb
        held_yz = (at_z >= 0) & (global_y >= 0)
        in_yz = held_yz & (at_z < 384) & (global_y < 24 * ny)

        def changes(d, reach):
            w = {}
            for c in range(3):
                for xr in range(-reach, 2 + reach):
                    w[c, xr] = jnp.where(region, twice(del_s[d, c, xr]), 0.0) if 0 <= xr < 2 else jnp.zeros((16, 256), F32)
            for m in (1, 3, 0, 2, 4, 5, 6, 7):
                dx, dy = AROUND[m]

                @pl.when(exists(-dx, -dy))
                def _():
                    box_copy(m, d).wait_recv()

                far_x, far_y, far_z = place_of[m, 0, 0], place_of[m, 1, 0], place_of[m, 2, 0]
                ok = w_in(at_z, far_z, 128)
                if dy == 0:
                    ok = ok & w_in(at_y, far_y, 8)
                else:
                    ok = ok & w_in(at_y, 24 if dy < 0 else -2, 2)
                for xr in {0: range(-reach, 2 + reach), -1: range(2, 2 + reach), 1: range(-reach, 0)}[dx]:
                    i = x0 + xr + 6 * dx - far_x
                    s0 = jnp.where(i == 0, 1.0, 0.0).astype(F32)
                    s1 = jnp.where(i == 1, 1.0, 0.0).astype(F32)
                    for c in range(3):
                        if dy == 0:
                            tile = s0 * fx_r[m // 2, d, c, 0] + s1 * fx_r[m // 2, d, c, 1]
                        else:
                            pair = [s0 * fy_r[m, d, 6 * r + 2 * c:6 * r + 2 * c + 1, :]
                                    + s1 * fy_r[m, d, 6 * r + 2 * c + 1:6 * r + 2 * c + 2, :] for r in range(2)]
                            low = 0 if dy < 0 else 6
                            tile = jnp.where(rows == low, jnp.broadcast_to(pair[0], (8, 128)),
                                             jnp.broadcast_to(pair[1], (8, 128)))
                        w[c, xr] = w[c, xr] + jnp.where(ok, twice(tile), 0.0)
            return w

        def turned_ahead(w, xr):
            ex, ey, ez = (w[c, xr] for c in range(3))
            moved = ((up_y(ez) - ez) - (up_z(ey) - ey), (up_z(ex) - ex) - (w[2, xr + 1] - ez),
                     (w[1, xr + 1] - ey) - (up_y(ex) - ex))
            ok = held_yz & (as_int(x0 + xr + 6 * ga >= 0) + w_none > 0)
            return [jnp.where(ok, -0.5 * part, 0.0) for part in moved]

        def turned_behind(hh, xr):
            hx, hy, hz = (hh[c, xr] for c in range(3))
            return ((hz - down_y(hz)) - (hy - down_z(hy)), (hx - down_z(hx)) - (hz - hh[2, xr - 1]),
                    (hy - hh[1, xr - 1]) - (hx - down_y(hx)))

        def on_region(wide):
            kept = jnp.where(region, wide, 0.0)
            return (kept[0:8, 0:128] + kept[0:8, 128:256]) + (kept[8:16, 0:128] + kept[8:16, 128:256])

        def window_factors():
            win_copy().wait_recv()
            slab = tables(permit, conduct, relax, debye, 1.0, 0.5)
            for xr in range(4):
                for u2 in range(2):
                    for v2 in range(2):
                        here = wm_r[xr, u2, v2]
                        spot = (xr, slice(8 * u2, 8 * u2 + 8), slice(128 * v2, 128 * v2 + 128))
                        for q in range(2):
                            kw[(q,) + spot] = pick(slab[q], here)
                        kw[(2,) + spot] = pick(slab[2], here) * pick(slab[4], here)

        def respond(n):
            hh = {}
            if n == 1:
                w = changes(0, 2)
                for xr in range(-2, 3):
                    for c, part in enumerate(turned_ahead(w, xr)):
                        hh[c, xr] = part
                        if -1 <= xr <= 1:
                            hw[c, xr + 1] = part
                layers = range(-1, 3)
            else:
                w = changes(1, 1)
                for c in range(3):
                    for xr in range(-1, 3):
                        w[c, xr] = w[c, xr] + ew[c, xr + 1]
                for xr in range(-1, 2):
                    for c, part in enumerate(turned_ahead(w, xr)):
                        hh[c, xr] = hw[c, xr + 1] + part
                layers = range(2)
            for xr in layers:
                ok = in_yz & (as_int((x0 + xr + 6 * ga >= 0) & (x0 + xr + 6 * ga < 6 * nx)) + w_none > 0)
                for c, curl in enumerate(turned_behind(hh, xr)):
                    value = kw[0, xr + 1] * w[c, xr] + kw[1, xr + 1] * curl
                    if n == 1:
                        value = jnp.where(ok, value, 0.0)
                        ew[c, xr + 1] = value
                    else:
                        value = value + kw[2, xr + 1] * ew[c, xr + 1]
                    if 0 <= xr < 2:
                        ear[1, c, xr] = to_box(lat_r[n, c, xr] + on_region(value))

        learn_places()
        ini_copy().wait_recv()
        for c in range(3):
            for i in range(2):
                ear[0, c, i] = to_box(ini_r[c, i])

        for n in range(STEPS):
            lax.fori_loop(0, 6, start_layer, 0)
            if n == 1:
                window_factors()
            lat_copy(n).wait_recv()
            if n == 0:
                for c in range(3):
                    for i in range(2):
                        ear[1, c, i] = to_box(lat_r[0, c, i])
            else:
                respond(n)

            drv[...] = ear[0] + (1.0 / 3.0) * (ear[1] - ear[0])
            lax.fori_loop(0, 6, finish_layer, 0)

            def substep(s, carry):
                weight = (s + 1).astype(F32) * (1.0 / 3.0)
                drv[...] = ear[0] + weight * (ear[1] - ear[0])
                return lax.fori_loop(0, 6, at_layer, carry, unroll=True)

            lax.fori_loop(1, 3, substep, 0)
            for i in range(2):
                ok = inside & (inside_x(3 * i) + none > 0)
                for c in range(3):
                    total = functools.reduce(
                        jnp.add, [ff[c, 3 * i + j, t] for j in range(3) for t in range(9)])
                    latest = ear[1, c, i]
                    delta = jnp.where(ok, total * (1.0 / 27.0) - latest, 0.0)
                    ear[0, c, i] = latest + delta
                    del_s[n, c, i] = from_box(delta)
            if n + 1 < STEPS:
                for r in range(2):
                    low = jnp.where(y0 <= r, 1.0, 0.0).astype(F32)
                    high = jnp.where(y0 >= 15 + r, 1.0, 0.0).astype(F32)
                    for c in range(3):
                        for i in range(2):
                            row = 6 * r + 2 * c + i
                            fy_s[0, n, row:row + 1, :] = low * del_s[n, c, i, r:r + 1, :]
                            fy_s[1, n, row:row + 1, :] = high * del_s[n, c, i, 6 + r:7 + r, :]
                for m in (4, 5, 6, 7, 0, 2, 1, 3):
                    dx, dy = AROUND[m]

                    @pl.when(exists(dx, dy))
                    def _():
                        box_copy(m, n).start()
                low, high = (jnp.where(x0 == q, 1.0, 0.0).astype(F32) for q in (0, 4))
                left, right = (jnp.where(y0 == q, 1.0, 0.0).astype(F32) for q in (0, 16))
                for c in range(3):
                    nx_s[0, n, c] = low * del_s[n, c, 0]
                    nx_s[1, n, c] = high * del_s[n, c, 1]
                    for i in range(2):
                        ny_s[0, n, 2 * c + i:2 * c + i + 1, :] = left * del_s[n, c, i, 0:1, :]
                        ny_s[1, n, 2 * c + i:2 * c + i + 1, :] = right * del_s[n, c, i, 7:8, :]
                nd_s[0, n] = jnp.broadcast_to((high * left) * del_s[n, 0, 1, 0:1, :], (8, 128))
                nd_s[1, n] = jnp.broadcast_to((low * right) * del_s[n, 1, 0, 7:8, :], (8, 128))
                del_copy(n).start()
                for m in (4, 5, 0, 2, 1, 3):
                    dx, dy = TO_NEXT[m]

                    @pl.when(exists(dx, dy))
                    def _():
                        near_copy(m, n).start()
            else:
                del_copy(n).start()

        def save_fine(x, carry):
            for c in range(9):
                for ry in range(3):
                    lift = 1 if 3 <= c < 6 else 0
                    parts = [ff[c, x + lift, 3 * ry + r] for r in range(3)]
                    if c >= 6:
                        parts = [part * fk[4, x, 3 * ry + r] for r, part in enumerate(parts)]
                    got = [pick(part, source[r]) for r, part in enumerate(parts)]
                    for v in range(3):
                        a, b, d = (got[(q + 2 * v) % 3] for q in range(3))
                        value = jnp.where(phase == 0, a, jnp.where(phase == 1, b, d))
                        if lift:
                            value = 0.5 * value
                        stage[v, c, x, pl.ds(ry, 8, stride=3), :] = value
            return carry

        lax.fori_loop(0, 6, save_fine, 0)
        f_out = [pltpu.make_async_copy(stage.at[v], out.at[0, :, :, :, pl.ds(128 * v, 128)], lsem.at[v]) for v in range(3)]
        for cp in f_out:
            cp.start()
        each(1, lambda m: pos_copy(m).wait_send(), AROUND)
        for n in range(STEPS):
            del_copy(n).wait_send()
            if n + 1 < STEPS:
                each(1, lambda m: near_copy(m, n).wait_send())
                each(1, lambda m: box_copy(m, n).wait_send(), AROUND)
        for cp in f_out:
            cp.wait()


def solution(mesh):
    nx, ny = mesh.shape["gx"], mesh.shape["gy"]

    def body(fields, material, permit, conduct, relax, debye, subgrids):
        vm = pltpu.VMEM
        dma = pltpu.SemaphoreType.DMA
        slots = [
            vm((SETS, 2, 24, 384), F32), vm((SETS, 2, 8, 384), F32),
            vm((SETS, 2, 24, 384), F32), vm((SETS, 2, 8, 384), F32),
            vm((SETS, 8, 384), F32), vm((SETS, 8, 384), F32),
        ]
        region = (3, 2, 8, 128)
        near = [vm((2, STEPS - 1, 3, 8, 128), F32), vm((2, STEPS - 1, 8, 128), F32), vm((2, STEPS - 1, 8, 128), F32)]
        return pl.pallas_call(
            functools.partial(kernel, nx, ny),
            out_shape=jax.ShapeDtypeStruct(fields.shape, F32),
            in_specs=[pl.BlockSpec(memory_space=pl.ANY)] * 7,
            out_specs=pl.BlockSpec(memory_space=pl.ANY),
            scratch_shapes=[
                *[pltpu.SMEM((8,), F32)] * 4, pltpu.SMEM((1, 1, 6), jnp.int32),
                vm((3, 3, 7, 32, 384), F32), vm((3, 3, 7, 32, 384), F32), vm((3, 3, 6, 24, 384), F32), vm((5, 6, 24, 384), F32),
                vm((3, 9, 6, 24, 128), F32), vm((3, 6, 24, 128), jnp.int32),
                vm((9, 7, 9, 8, 128), F32), vm((5, 6, 9, 8, 128), F32),
                vm((5, 16, 384), F32), vm((2, 8, 384), F32), vm((2, 8, 384), F32), vm((3, 32, 384), F32), vm((3, 8, 384), F32),
                vm((2,) + region, F32), vm(region, F32), vm((6, 9, 8, 128), F32),
                vm((3, 8, 40, 128), jnp.int32), vm((3, 4, 16, 256), F32), vm((3, 3, 16, 256), F32), vm((3, 4, 16, 256), F32),
                *slots, *slots,
                vm((STEPS,) + region, F32), vm((STEPS,) + region, F32), vm(region, F32), vm(region, F32),
                vm((STEPS,) + region, F32), vm((STEPS,) + region, F32),
                *near, *near, vm((8, 128), jnp.int32), vm((8, 8, 128), jnp.int32), pltpu.SMEM((8, 8, 128), jnp.int32),
                vm((2, STEPS - 1, 16, 128), F32), vm((2, STEPS - 1) + region, F32), vm((8, STEPS - 1, 16, 128), F32),
                vm((6, 3, 8, 128), jnp.int32), vm((2, 3, 24, 128), jnp.int32), vm((6, 3, 8, 128), jnp.int32),
                vm((4, 2, 2, 8, 128), jnp.int32), vm((4, 2, 2, 8, 128), jnp.int32),
                dma((18,)), dma((6, SETS)), dma((6, SETS)),
                dma((STEPS + 1,)), dma((STEPS + 1,)), dma((STEPS,)), dma((STEPS,)),
                dma((6, STEPS)), dma((6, STEPS)), dma((8,)), dma((8,)),
                dma((8, STEPS)), dma((8, STEPS)), dma((6,)), dma((6,)), dma((1,)), dma((1,)),
            ],
            compiler_params=pltpu.CompilerParams(
                collective_id=0, has_side_effects=True, vmem_limit_bytes=63 * 1024 * 1024),
        )(fields, material, permit, conduct, relax, debye, subgrids)

    return jax.shard_map(
        body,
        mesh=mesh,
        in_specs=(P("grid", None, "gx", "gy", None), P("grid", "gx", "gy", None), P(), P(), P(), P(), P("gx", "gy", None)),
        out_specs=P("grid", None, "gx", "gy", None),
        check_vma=False,
    )
```
